32 devices in a mesh: ctx: 4 (over x, core), fsdp: 8 (over z, y).
Axes of the slice: x: 2, y: 2, z: 4, core: 2. Of those that a mesh axis runs over, the one named last changes fastest.
Arguments:
- hidden_in: bfloat16 [8, 2048, 1024], P('fsdp', 'ctx'), may hold values from -6 to 6
- cotangent: bfloat16 [8, 2048, 1024], P('fsdp', 'ctx'), may hold values from -6 to 6
- lengths: int32 [8], P('fsdp'), may hold values from 512 to 2048, as said below
- block_of: int32 [4, 2], replicated, may hold values from 0 to 7, as said below
- w_qkv: bfloat16 [1024, 3072], P('fsdp'), may hold values from -0.1875 to 0.1875
- w_attn: bfloat16 [1024, 1024], P('fsdp'), may hold values from -0.1875 to 0.1875
- w_up: bfloat16 [1024, 4096], P('fsdp'), may hold values from -0.1875 to 0.1875
- w_down: bfloat16 [4096, 1024], P('fsdp'), may hold values from -0.09375 to 0.09375
- norm_gains: bfloat16 [1024, 4], P('fsdp'), may hold values from 0.5 to 1.5
Outputs:
- output: bfloat16 [8, 2048, 1024], P('fsdp', 'ctx')
- input_grad: float32 [8, 2048, 1024], P('fsdp', 'ctx')
- qkv_grad: float32 [1024, 3072], P('fsdp')
- attn_out_grad: float32 [1024, 1024], P('fsdp')
- up_grad: float32 [1024, 4096], P('fsdp')
- down_grad: float32 [4096, 1024], P('fsdp')
- gains_grad: float32 [1024, 4], P('fsdp')
The draws below stay inside these ranges and needn't reach their ends.
Inputs may be any that keep to these rules, and one draw needn't show every extreme that they name: `lengths`: valid positions of each slot, counted from position 0; some slot is full in every draw. `block_of`: row c gives the blocks of 256 positions whose rows ctx index c holds, in that order; the two of a row sum to 7 and every block appears once.
All inputs are finite; a program needn't handle non-finite values.
Results may differ from the reference program's by a relative error of at most 0.014.
Values may be sent and summed in bfloat16 or wider, within the bound.
No kernel may reach another device: no remote copies, remote signals or barrier semaphores. Data moves between devices by JAX's collectives and lax.ppermute only.
A program may use at most 192 MiB of HBM per device.

```python
import math
import jax
import jax.numpy as jnp
from jax import lax

D = 1024
HEADS = 16
HEAD_DIM = 64
FF = 4096
SLOT = 2048
BLOCK = 256
SLOTS = 8


def draw_lengths(key, part):
    length_key = jax.random.fold_in(key, 11)
    chosen_key = jax.random.fold_in(key, 12)
    drawn = jax.random.randint(length_key, (SLOTS,), SLOT // 4, SLOT + 1, dtype=jnp.int32)
    full_slot = jax.random.randint(chosen_key, (), 0, SLOTS, dtype=jnp.int32)
    return jnp.where(jnp.arange(SLOTS, dtype=jnp.int32) == full_slot, SLOT, drawn).astype(jnp.int32)


def draw_block_of(key, part):
    pair_count = SLOT // (2 * BLOCK)
    ordering = jax.random.permutation(jax.random.fold_in(key, 21), pair_count).astype(jnp.int32)
    flipped = jax.random.randint(jax.random.fold_in(key, 22), (pair_count,), 0, 2, dtype=jnp.int32)
    leading = jnp.where(flipped == 1, 2 * pair_count - 1 - ordering, ordering)
    return jnp.stack([leading, 2 * pair_count - 1 - leading], axis=1).astype(jnp.int32)


def strengthened(entries, key, source, target, parts, factor):
    owner, partner = [(jnp.arange(entries.shape[axis_at]) // (entries.shape[axis_at] // parts)).reshape([-1 if axis == axis_at else 1 for axis in range(entries.ndim)]) for axis_at in (source, target)]
    chosen = jax.random.permutation(key, parts)[partner]
    strong = (owner == chosen) | (owner == (partner + parts // 2) % parts)
    return jnp.where(strong, factor * entries, entries)


def steps_of(own_key, shape, shards, smallest, largest):
    loudness = 1.0
    for dim, blocks in shards:
        steps = jax.random.uniform(jax.random.fold_in(jax.random.fold_in(own_key, 6), dim), (blocks,), jnp.float32, smallest / len(shards), largest / len(shards))
        loudness = loudness * jnp.repeat(jnp.exp(steps), shape[dim] // blocks).reshape((-1,) + (1,) * (len(shape) - 1 - dim))
    return loudness


def bell_draw(key, dims, scale, limit, cuts=(), kind=jnp.bfloat16):
    loudness = steps_of(key, dims, cuts, -0.22, 0.18) if cuts else 1.0
    values = jax.random.normal(key, dims, jnp.float32) * scale * loudness
    return jnp.minimum(jnp.maximum(values, -limit), limit).astype(kind)


def bell_draw_with(stream_key, dims, spread, bound, split, heavy, kind=jnp.bfloat16):
    values = spread * jax.random.normal(stream_key, dims, jnp.float32)
    if split:
        values = values * steps_of(stream_key, dims, split, -0.22, 0.18)
    return jnp.clip(strengthened(values, jax.random.fold_in(stream_key, 3), *heavy), -bound, bound).astype(kind)


def setup_inputs(seed: int = 0) -> dict:
    splits = jax.random.split(jax.random.key(seed), 10)
    hidden_in = bell_draw_with(splits[0], (SLOTS, SLOT, D), 1.0, 6.0, ((0, 8), (1, 4)), (0, 2, 8, 2.0))
    cotangent = bell_draw_with(splits[1], (SLOTS, SLOT, D), 1.0, 6.0, ((0, 8), (1, 4)), (0, 2, 8, 2.0))
    lengths = draw_lengths(jax.random.fold_in(splits[9], 71), 0)
    block_of = draw_block_of(jax.random.fold_in(splits[9], 71), 0)
    w_qkv = bell_draw(splits[4], (D, 3 * D), D ** -0.5, 0.1875, ((0, 8),))
    w_attn = bell_draw(splits[5], (D, D), D ** -0.5, 0.1875, ((0, 8),))
    w_up = bell_draw(splits[6], (D, FF), D ** -0.5, 0.1875, ((0, 8),))
    w_down = bell_draw(splits[7], (FF, D), FF ** -0.5, 0.09375, ((0, 8),))
    norm_gains = jnp.clip(1.0 + 0.1 * jax.random.normal(splits[8], (D, 4), jnp.float32), 0.5, 1.5).astype(jnp.bfloat16)
    return {"hidden_in": hidden_in, "cotangent": cotangent, "lengths": lengths, "block_of": block_of, "w_qkv": w_qkv, "w_attn": w_attn, "w_up": w_up, "w_down": w_down, "norm_gains": norm_gains}


@jax.custom_vjp
def low(v):
    return lax.optimization_barrier(v.astype(jnp.bfloat16)).astype(jnp.float32)

@jax.custom_vjp
def low_back(v):
    return v

def low_keep(v):
    return (low(v), None)

def low_pass(kept, grad):
    return (grad,)

def back_keep(v):
    return (v, None)

def back_low(kept, grad):
    return (low(grad),)
low.defvjp(low_keep, low_pass)
low_back.defvjp(back_keep, back_low)

def layer_norm(values, gain_vec):
    average = lax.optimization_barrier(jnp.mean(values, axis=-1, keepdims=True))
    centered = values - average
    variance = lax.optimization_barrier(jnp.mean(centered * centered, axis=-1, keepdims=True))
    return centered * lax.rsqrt(variance + 1e-05) * gain_vec

def rotate(values, positions):
    half_dim = HEAD_DIM // 2
    counter = jnp.arange(half_dim, dtype=jnp.float32)
    inverse = jnp.exp(counter * (-2.0 * math.log(10000.0) / HEAD_DIM))
    angles = positions.astype(jnp.float32)[:, None] * inverse[None, :]
    cosine = jnp.cos(angles)[:, None, :]
    sine_part = jnp.sin(angles)[:, None, :]
    leading = values[..., :half_dim]
    trailing = values[..., half_dim:]
    return jnp.concatenate([leading * cosine - trailing * sine_part, trailing * cosine + leading * sine_part], axis=-1)

def slot_layer(params, hidden, positions, length):
    w_qkv, w_attn, w_up, w_down, gains = params
    highest = lax.Precision.HIGHEST
    rows_all = hidden.shape[0]
    normed = low(layer_norm(hidden, gains[:, 0]))
    mixed = low_back(jnp.dot(normed, w_qkv, precision=highest))
    queries = low(rotate(mixed[:, :D].reshape(rows_all, HEADS, HEAD_DIM), positions))
    keys_all = low(rotate(mixed[:, D:2 * D].reshape(rows_all, HEADS, HEAD_DIM), positions))
    values_all = low(mixed[:, 2 * D:].reshape(rows_all, HEADS, HEAD_DIM))
    key_live = positions < length
    block_rows = min(512, rows_all)

    def attend(index):
        start = (index * block_rows).astype(jnp.int32)
        query_block = lax.dynamic_slice_in_dim(queries, start, block_rows, 0)
        query_pos = lax.dynamic_slice_in_dim(positions, start, block_rows, 0)
        scores = low_back(jnp.einsum('qhd,khd->hqk', query_block, keys_all, precision=highest) * 0.125)
        allowed = ((positions[None, :] <= query_pos[:, None]) & key_live[None, :])[None]
        masked = jnp.where(allowed, scores, -1e+30)
        log_total = jax.nn.logsumexp(masked, axis=-1, keepdims=True)
        probs = low(jnp.where(allowed, jnp.exp(scores - log_total), 0.0))
        return jnp.einsum('hqk,khd->qhd', probs, values_all, precision=highest)
    attended = lax.map(jax.checkpoint(attend), jnp.arange(rows_all // block_rows, dtype=jnp.int32))
    attended = low_back(low(attended.reshape(rows_all, D)))
    branch = low_back(jnp.dot(attended, w_attn, precision=highest))
    middle = hidden + layer_norm(branch, gains[:, 1])
    normed_mid = low(layer_norm(middle, gains[:, 2]))
    lifted = low_back(jnp.dot(normed_mid, w_up, precision=highest))
    activated = low(jax.nn.gelu(lifted, approximate=True))
    lowered = low_back(jnp.dot(activated, w_down, precision=highest))
    return middle + layer_norm(lowered, gains[:, 3])

def reference(hidden_in, cotangent, lengths, block_of, w_qkv, w_attn, w_up, w_down, norm_gains):
    params = (w_qkv.astype(jnp.float32), w_attn.astype(jnp.float32), w_up.astype(jnp.float32), w_down.astype(jnp.float32), norm_gains.astype(jnp.float32))
    block_list = block_of.reshape(-1).astype(jnp.int32)
    offsets = jnp.arange(BLOCK, dtype=jnp.int32)
    positions = (block_list[:, None] * BLOCK + offsets[None, :]).reshape(-1).astype(jnp.int32)

    def per_slot(totals, items):
        hidden, incoming, length = items
        hidden = hidden.astype(jnp.float32)

        def apply_layer(weights_all, hidden_rows):
            return slot_layer(weights_all, hidden_rows, positions, length)
        result, pullback = jax.vjp(apply_layer, params, hidden)
        live_rows = (positions < length).astype(jnp.float32)[:, None]
        grads_params, grad_hidden = pullback(incoming.astype(jnp.float32) * live_rows)
        totals = jax.tree.map(lambda running, added: running + added, totals, grads_params)
        return (totals, (result.astype(jnp.bfloat16), grad_hidden))
    zeros_all = jax.tree.map(jnp.zeros_like, params)
    totals, (outputs, grads_in) = lax.scan(per_slot, zeros_all, (hidden_in, cotangent, lengths))
    return (outputs, grads_in, totals[0], totals[1], totals[2], totals[3], totals[4])
```

```python
import math

import jax
import jax.numpy as jnp
from jax import lax
from jax.experimental import pallas as pl
from jax.experimental.pallas import tpu as pltpu
from jax.sharding import PartitionSpec as P

HEAD_DIM = 64
BF = jnp.bfloat16
F32 = jnp.float32
NEG = -1e30
EPS = 1e-05


def mm(left, right):
    return jnp.dot(left, right, preferred_element_type=F32)


def mm_tn(left, right):
    return lax.dot_general(left, right, (((0,), (0,)), ((), ())), preferred_element_type=F32)


def mm_nt(left, right):
    return lax.dot_general(left, right, (((1,), (1,)), ((), ())), preferred_element_type=F32)


def swap(value, bit):
    return lax.ppermute(value, "ctx", [(i, i ^ bit) for i in range(4)])


def ring_pairs(n):
    order = list(range(0, n, 2)) + list(range(n - 1, 0, -2))
    ahead = [(order[i], order[(i + 1) % n]) for i in range(n)]
    return ahead, [(b, a) for a, b in ahead]


def ring_owner(place, n):
    place = lax.rem(place + 2 * n, n)
    return jnp.where(place < n // 2, 2 * place, 2 * (n - place) - 1)


def ring_place(me, n):
    return jnp.where(lax.rem(me, 2) == 0, lax.div(me, 2), n - 1 - lax.div(me, 2))


def ring_gather(block, n, flip, store, target):
    ahead, back = ring_pairs(n)
    sign = -1
    if flip:
        ahead, back, sign = back, ahead, 1
    me = lax.axis_index("fsdp")
    place = ring_place(me, n)
    target = store(target, me, block)
    one = two = block
    for step in range(1, n // 2 + 1):
        one = lax.ppermute(one, "fsdp", ahead)
        if step <= (n - 1) // 2:
            two = lax.ppermute(two, "fsdp", back)
        target = store(target, ring_owner(place + sign * step, n), one)
        if step <= (n - 1) // 2:
            target = store(target, ring_owner(place - sign * step, n), two)
    return target


def ring_scatter(pick, n, flip):
    ahead, back = ring_pairs(n)
    sign = 1
    if flip:
        ahead, back, sign = back, ahead, -1
    place = ring_place(lax.axis_index("fsdp"), n)

    def at(offset):
        return pick(ring_owner(place + offset, n))

    far, near = n // 2, (n - 1) // 2
    one, two = at(sign * far), at(-sign * near)
    for step in range(far):
        one = lax.ppermute(one, "fsdp", ahead)
        if step < near:
            two = lax.ppermute(two, "fsdp", back)
        left = far - 1 - step
        if left > 0:
            one = (one.astype(F32) + at(sign * left).astype(F32)).astype(BF)
        left = near - 1 - step
        if left > 0:
            two = (two.astype(F32) + at(-sign * left).astype(F32)).astype(BF)
    return one.astype(F32) + two.astype(F32) + at(0).astype(F32)


def normalize(values):
    average = jnp.mean(values, axis=-1, keepdims=True)
    centered = values - average
    variance = jnp.mean(centered * centered, axis=-1, keepdims=True)
    scale = lax.rsqrt(variance + EPS)
    return centered * scale, scale


def norm_back(unit, scale, gain, incoming):
    weighted = incoming * gain
    return (
        weighted
        - jnp.mean(weighted, axis=-1, keepdims=True)
        - unit * jnp.mean(weighted * unit, axis=-1, keepdims=True)
    ) * scale


def turned(value, cosine, sine_signed, inverse):
    width = value.shape[1]
    lane = lax.broadcasted_iota(jnp.int32, value.shape, 1)
    half = HEAD_DIM // 2
    other = jnp.where(
        lax.rem(lane, HEAD_DIM) < half,
        pltpu.roll(value, width - half, 1),
        pltpu.roll(value, half, 1),
    )
    repeat = width // cosine.shape[1]
    cosine = jnp.concatenate([cosine] * repeat, axis=1)
    sine_signed = jnp.concatenate([sine_signed] * repeat, axis=1)
    if inverse:
        return value * cosine - other * sine_signed
    return value * cosine + other * sine_signed


def project(hidden, weight, gain, cosine, sine_signed):
    rows, dim = hidden.shape
    width = weight.shape[1]
    part = width // 3
    step = 512

    def body(hidden_ref, weight_ref, gain_ref, cos_ref, sin_ref, normed_ref, out_ref):
        unit, _ = normalize(hidden_ref[...].astype(F32))
        normed = (unit * gain_ref[...]).astype(BF)
        normed_ref[...] = normed
        mixed = mm(normed, weight_ref[...])
        cos_part, sin_part = cos_ref[...], sin_ref[...]
        queries = turned(mixed[:, :part], cos_part, sin_part, False).astype(BF)
        out_ref[:, :part] = (queries.astype(F32) * 0.125).astype(BF)
        out_ref[:, part : 2 * part] = turned(
            mixed[:, part : 2 * part], cos_part, sin_part, False
        ).astype(BF)
        out_ref[:, 2 * part :] = mixed[:, 2 * part :].astype(BF)

    return pl.pallas_call(
        body,
        grid=(rows // step,),
        in_specs=[
            pl.BlockSpec((step, dim), lambda i: (i, 0)),
            pl.BlockSpec((dim, width), lambda i: (0, 0)),
            pl.BlockSpec((1, dim), lambda i: (0, 0)),
            pl.BlockSpec((step, 128), lambda i: (i, 0)),
            pl.BlockSpec((step, 128), lambda i: (i, 0)),
        ],
        out_specs=[
            pl.BlockSpec((step, dim), lambda i: (i, 0)),
            pl.BlockSpec((step, width), lambda i: (i, 0)),
        ],
        out_shape=[
            jax.ShapeDtypeStruct((rows, dim), BF),
            jax.ShapeDtypeStruct((rows, width), BF),
        ],
        compiler_params=pltpu.CompilerParams(vmem_limit_bytes=32 << 20),
        cost_estimate=pl.CostEstimate(
            flops=2 * rows * dim * width, bytes_accessed=12 << 20, transcendentals=rows
        ),
        name="project",
    )(hidden, weight, gain, cosine, sine_signed)


def head_masked(value, heads):
    row = lax.broadcasted_iota(jnp.int32, value.shape, 0)
    return [
        jnp.where(lax.div(row, HEAD_DIM) == h, value, 0.0).astype(BF) for h in range(heads)
    ]


def folded(value, op):
    rows, cols = value.shape
    return op(value.reshape(rows // 8, 8, cols), axis=0)


def attention(order, length, qkv, blk):
    rows = qkv.shape[0]
    width = qkv.shape[1] // 3
    heads = width // HEAD_DIM
    nb = rows // blk

    def body(order_ref, length_ref, qkv_ref, out_ref, lse_ref, keys, values_t, q_masked, scores, total):
        live = length_ref[0]

        def fill(p, carry):
            rows_at = pl.ds(pl.multiple_of(order_ref[p] * blk, blk), blk)
            keys[p] = qkv_ref[rows_at, width : 2 * width]
            values_t[p] = jnp.transpose(qkv_ref[rows_at, 2 * width :].astype(F32)).astype(BF)
            return carry

        lax.fori_loop(0, nb, fill, 0)

        def per_block(i, carry):
            rows_at = pl.ds(pl.multiple_of(order_ref[i] * blk, blk), blk)
            query_t = jnp.transpose(qkv_ref[rows_at, :width].astype(F32))
            for h, masked in enumerate(head_masked(query_t, heads)):
                q_masked[h] = masked

            def first(j, tops, masks):
                key_block = keys[j]
                if masks:
                    key_pos = j * blk + lax.broadcasted_iota(jnp.int32, (blk, blk), 0)
                    query_pos = i * blk + lax.broadcasted_iota(jnp.int32, (blk, blk), 1)
                    allowed = (key_pos <= query_pos) & (key_pos < live)
                new = []
                for h in range(heads):
                    s = mm(key_block, q_masked[h])
                    if masks:
                        s = jnp.where(allowed, s, NEG)
                    scores[h, j] = s
                    new.append(jnp.maximum(tops[h], folded(s, jnp.max)))
                return tuple(new)

            whole = jnp.minimum(i, lax.div(live, blk))
            tops = tuple(jnp.full((8, blk), NEG, F32) for _ in range(heads))
            tops = lax.fori_loop(0, whole, lambda j, c: first(j, c, False), tops)
            tops = lax.fori_loop(whole, i + 1, lambda j, c: first(j, c, True), tops)
            tops = [jnp.max(t, axis=0, keepdims=True) for t in tops]
            total[...] = jnp.zeros_like(total)

            def second(j, sums):
                new = []
                for h in range(heads):
                    p = jnp.exp(scores[h, j] - tops[h])
                    new.append(sums[h] + folded(p, jnp.sum))
                    at = slice(h * HEAD_DIM, (h + 1) * HEAD_DIM)
                    total[at, :] += mm(values_t[j, at, :], p.astype(BF))
                return tuple(new)

            sums = tuple(jnp.zeros((8, blk), F32) for _ in range(heads))
            sums = lax.fori_loop(0, i + 1, second, sums)
            scaled = []
            for h in range(heads):
                sum_h = jnp.sum(sums[h], axis=0, keepdims=True)
                lse_ref[i, h : h + 1, :] = tops[h] + jnp.log(sum_h)
                scaled.append(total[h * HEAD_DIM : (h + 1) * HEAD_DIM, :] * (1.0 / sum_h))
            out_ref[rows_at, :] = jnp.transpose(jnp.concatenate(scaled, axis=0)).astype(BF)
            return carry

        lax.fori_loop(0, nb, per_block, 0)

    tiles = nb * (nb + 1) // 2 * heads
    vm = pl.BlockSpec(memory_space=pltpu.VMEM)
    sm = pl.BlockSpec(memory_space=pltpu.SMEM)
    return pl.pallas_call(
        body,
        in_specs=[sm, sm, vm],
        out_specs=[vm, vm],
        out_shape=[
            jax.ShapeDtypeStruct((rows, width), BF),
            jax.ShapeDtypeStruct((nb, 8, blk), F32),
        ],
        scratch_shapes=[
            pltpu.VMEM((nb, blk, width), BF),
            pltpu.VMEM((nb, width, blk), BF),
            pltpu.VMEM((heads, width, blk), BF),
            pltpu.VMEM((heads, nb, blk, blk), F32),
            pltpu.VMEM((width, blk), F32),
        ],
        compiler_params=pltpu.CompilerParams(vmem_limit_bytes=32 << 20),
        cost_estimate=pl.CostEstimate(
            flops=tiles * 8 * blk * blk * width // 4,
            bytes_accessed=5 << 20,
            transcendentals=tiles * blk * blk,
        ),
        name="attention",
    )(order, length, qkv)


def attention_back(order, length, qkv, grad_out, out, lse, cosine, sine_signed, blk):
    rows = qkv.shape[0]
    width = qkv.shape[1] // 3
    heads = width // HEAD_DIM
    nb = rows // blk

    def body(
        order_ref, length_ref, qkv_ref, gout_ref, att_ref, lse_ref, cos_ref, sin_ref, result_ref,
        keys, keys_t, values, q_cols, q_rows, g_cols, g_rows, grad_q, grad_k, grad_v, inner,
    ):
        live = length_ref[0]

        def fill(p, carry):
            rows_at = pl.ds(pl.multiple_of(order_ref[p] * blk, blk), blk)
            key_block = qkv_ref[rows_at, width : 2 * width]
            keys[p] = key_block
            keys_t[p] = jnp.transpose(key_block.astype(F32)).astype(BF)
            values[p] = qkv_ref[rows_at, 2 * width :]
            grad_k[p] = jnp.zeros((blk, width), F32)
            grad_v[p] = jnp.zeros((blk, width), F32)
            return carry

        lax.fori_loop(0, nb, fill, 0)
        lane_head = lax.div(lax.broadcasted_iota(jnp.int32, (blk, width), 1), HEAD_DIM)

        def per_block(i, carry):
            rows_at = pl.ds(pl.multiple_of(order_ref[i] * blk, blk), blk)
            query = qkv_ref[rows_at, :width].astype(F32)
            gout = gout_ref[rows_at, :].astype(F32)
            inner_t = jnp.transpose(gout * att_ref[rows_at, :].astype(F32))
            for h, masked in enumerate(head_masked(jnp.transpose(query), heads)):
                q_cols[h] = masked
            for h, masked in enumerate(head_masked(jnp.transpose(gout), heads)):
                g_cols[h] = masked
            for h in range(heads):
                at = slice(h * blk, (h + 1) * blk)
                q_rows[at, :] = jnp.where(lane_head == h, query, 0.0).astype(BF)
                g_rows[at, :] = jnp.where(lane_head == h, gout, 0.0).astype(BF)
                inner[h : h + 1, :] = jnp.sum(
                    inner_t[h * HEAD_DIM : (h + 1) * HEAD_DIM, :], axis=0, keepdims=True
                )
            grad_q[...] = jnp.zeros_like(grad_q)

            def tile(j, carry, masks):
                key_block, value_block = keys[j], values[j]
                if masks:
                    key_pos = j * blk + lax.broadcasted_iota(jnp.int32, (blk, blk), 0)
                    query_pos = i * blk + lax.broadcasted_iota(jnp.int32, (blk, blk), 1)
                    allowed = (key_pos <= query_pos) & (key_pos < live)
                probs, grads = [], []
                for h in range(heads):
                    s = mm(key_block, q_cols[h])
                    if masks:
                        s = jnp.where(allowed, s, NEG)
                    p = jnp.exp(s - lse_ref[i, h : h + 1, :])
                    d = p * (mm(value_block, g_cols[h]) - inner[h : h + 1, :])
                    probs.append(p.astype(BF))
                    d = d.astype(BF)
                    grads.append(d)
                    at = slice(h * HEAD_DIM, (h + 1) * HEAD_DIM)
                    grad_q[at, :] += mm(keys_t[j, at, :], d)
                grad_v[j] += mm(jnp.concatenate(probs, axis=1), g_rows[...])
                grad_k[j] += mm(jnp.concatenate(grads, axis=1), q_rows[...])
                return carry

            whole = jnp.minimum(i, lax.div(live, blk))
            lax.fori_loop(0, whole, lambda j, c: tile(j, c, False), 0)
            lax.fori_loop(whole, i + 1, lambda j, c: tile(j, c, True), 0)
            result_ref[rows_at, :width] = turned(
                jnp.transpose(grad_q[...]) * 0.125, cos_ref[rows_at, :], sin_ref[rows_at, :], True
            ).astype(BF)
            return carry

        lax.fori_loop(0, nb, per_block, 0)

        def drain(p, carry):
            rows_at = pl.ds(pl.multiple_of(order_ref[p] * blk, blk), blk)
            result_ref[rows_at, width : 2 * width] = turned(
                grad_k[p], cos_ref[rows_at, :], sin_ref[rows_at, :], True
            ).astype(BF)
            result_ref[rows_at, 2 * width :] = grad_v[p].astype(BF)
            return carry

        lax.fori_loop(0, nb, drain, 0)

    tiles = nb * (nb + 1) // 2 * heads
    vm = pl.BlockSpec(memory_space=pltpu.VMEM)
    sm = pl.BlockSpec(memory_space=pltpu.SMEM)
    return pl.pallas_call(
        body,
        in_specs=[sm, sm] + [vm] * 6,
        out_specs=vm,
        out_shape=jax.ShapeDtypeStruct((rows, 3 * width), BF),
        scratch_shapes=[
            pltpu.VMEM((nb, blk, width), BF),
            pltpu.VMEM((nb, width, blk), BF),
            pltpu.VMEM((nb, blk, width), BF),
            pltpu.VMEM((heads, width, blk), BF),
            pltpu.VMEM((heads * blk, width), BF),
            pltpu.VMEM((heads, width, blk), BF),
            pltpu.VMEM((heads * blk, width), BF),
            pltpu.VMEM((width, blk), F32),
            pltpu.VMEM((nb, blk, width), F32),
            pltpu.VMEM((nb, blk, width), F32),
            pltpu.VMEM((8, blk), F32),
        ],
        compiler_params=pltpu.CompilerParams(vmem_limit_bytes=40 << 20),
        cost_estimate=pl.CostEstimate(
            flops=tiles * 20 * blk * blk * width // 4,
            bytes_accessed=12 << 20,
            transcendentals=tiles * blk * blk,
        ),
        name="attention_back",
    )(order, length, qkv, grad_out, out, lse, cosine, sine_signed)


def gelu_both(u):
    scale = math.sqrt(2.0 / math.pi)
    inside = jnp.tanh(scale * (u + 0.044715 * u * u * u))
    value = 0.5 * u * (1.0 + inside)
    slope = 0.5 * (1.0 + inside) + 0.5 * u * (1.0 - inside * inside) * scale * (
        1.0 + 3.0 * 0.044715 * u * u
    )
    return value, slope


def per_device(n, hidden_in, cotangent, lengths, block_of, w_qkv, w_attn, w_up, w_down, norm_gains):
    own_rows, dim = hidden_in.shape[1:]
    rows = 4 * own_rows
    blk = own_rows // 2
    ff = w_up.shape[1]
    shard = dim // n
    ff_shard = ff // n
    ff_half = ff_shard // 2
    part = dim // 4
    extra = 16
    q = lax.axis_index("ctx")
    c = lax.rem(q, 2)
    length = lengths[0]

    groups = [lax.bitwise_xor(q, g) for g in range(4)]
    blocks = jnp.concatenate([lax.dynamic_slice_in_dim(block_of, g, 1, 0)[0] for g in groups])
    order = jnp.sum(
        jnp.where(
            blocks[None, :] == jnp.arange(8, dtype=jnp.int32)[:, None],
            jnp.arange(8, dtype=jnp.int32)[None, :],
            0,
        ),
        axis=1,
        dtype=jnp.int32,
    )
    offsets = jnp.arange(blk, dtype=jnp.int32)
    pos = (blocks[:, None] * blk + offsets[None, :]).reshape(-1)
    lane = jnp.arange(128, dtype=jnp.int32)
    half_dim = HEAD_DIM // 2
    inverse = jnp.exp((lane % half_dim).astype(F32) * (-2.0 * math.log(10000.0) / HEAD_DIM))
    angles = pos.astype(F32)[:, None] * inverse[None, :]
    cosine = jnp.cos(angles)
    sine_signed = jnp.sin(angles) * jnp.where(lane % HEAD_DIM < half_dim, -1.0, 1.0)[None, :]

    parts = [
        lax.dynamic_slice_in_dim(w_qkv, t * dim + q * part, part, 1) for t in range(3)
    ] + [lax.dynamic_slice_in_dim(w_attn, q * part, part, 1)]
    gain_rows = jnp.pad(norm_gains.T, ((0, extra - 4), (0, dim - shard)))
    bundle = jnp.concatenate([jnp.concatenate(parts, axis=1), gain_rows], axis=0)
    up_own = lax.dynamic_index_in_dim(
        w_up.reshape(shard, n, 2, ff_half), c, 2, keepdims=False
    ).reshape(shard, n * ff_half)
    down_own = lax.dynamic_slice_in_dim(w_down, c * ff_half, ff_half, 0)

    def store_bundle(target, owner, block):
        to_qkv, to_attn, to_gains = target
        return (
            lax.dynamic_update_slice(to_qkv, block[:shard, : 3 * part], (owner * shard, 0)),
            lax.dynamic_update_slice(to_attn, block[:shard, 3 * part :], (owner * shard, 0)),
            lax.dynamic_update_slice(to_gains, block[None, shard:, :shard], (owner, 0, 0)),
        )

    def store_rows(target, owner, block):
        return lax.dynamic_update_slice(target, block, (owner * block.shape[0], 0))

    hidden_b = hidden_in[0]
    hidden_x = swap(hidden_b, 2)
    hidden_c = swap(hidden_b, 1)
    hidden_d = swap(hidden_x, 1)
    qkv_w, attn_q, gains_n = ring_gather(
        bundle,
        n,
        False,
        store_bundle,
        (
            jnp.zeros((dim, 3 * part), BF),
            jnp.zeros((dim, part), BF),
            jnp.zeros((n, extra, shard), BF),
        ),
    )
    up_w = ring_gather(up_own, n, False, store_rows, jnp.zeros((dim, n * ff_half), BF))
    down_w = ring_gather(down_own, n, True, store_rows, jnp.zeros((n * ff_half, dim), BF))
    gains = jnp.transpose(gains_n[:, :4, :], (1, 0, 2)).reshape(4, dim).astype(F32)

    hidden_all = jnp.concatenate([hidden_b, hidden_c, hidden_x, hidden_d], axis=0)
    normed, qkv = project(hidden_all, qkv_w, gains[0:1], cosine, sine_signed)
    attn_x = swap(attn_q, 2)
    attn_pair = swap(jnp.stack([attn_q, attn_x]), 1)
    attn_parts = jnp.stack([attn_q, attn_pair[0], attn_x, attn_pair[1]])

    def in_order(stacked, axis):
        return jnp.concatenate(
            [
                lax.dynamic_index_in_dim(stacked, lax.bitwise_xor(q, b), 0, keepdims=False)
                for b in range(4)
            ],
            axis=axis,
        )

    attn_w = in_order(attn_parts, 1)
    att, lse = attention(order, length[None], qkv, blk)
    att_g = att.reshape(4, own_rows, part)
    attended = in_order(jnp.stack([att_g[0]] + [swap(att_g[g], g) for g in range(1, 4)]), 1)
    hidden = hidden_b.astype(F32)
    branch = mm(attended, attn_w)
    unit1, scale1 = normalize(branch)
    middle = hidden + unit1 * gains[1]
    unit2, scale2 = normalize(middle)
    normed_mid = (unit2 * gains[2]).astype(BF)
    normed_mid2 = jnp.concatenate([normed_mid, swap(normed_mid, 1)], axis=0)
    lifted = mm(normed_mid2, up_w)
    activated = gelu_both(lifted)[0].astype(BF)
    lowered = swap(mm(activated[own_rows:], down_w), 1) + mm(activated[:own_rows], down_w)
    unit3, scale3 = normalize(lowered)
    result = middle + unit3 * gains[3]

    live = (pos[:own_rows] < length).astype(F32)[:, None]
    upstream = cotangent[0].astype(F32) * live
    grad_lowered = norm_back(unit3, scale3, gains[3], upstream).astype(BF)
    grad_lowered2 = jnp.concatenate([grad_lowered, swap(grad_lowered, 1)], axis=0)
    grad_activated = mm_nt(grad_lowered2, down_w)
    grad_lifted = (grad_activated * gelu_both(lifted)[1]).astype(BF)
    down_g = mm_tn(activated, grad_lowered2).astype(BF)
    up_g = mm_tn(normed_mid2, grad_lifted).astype(BF)
    grad_normed_mid = swap(mm_nt(grad_lifted[own_rows:], up_w), 1) + mm_nt(
        grad_lifted[:own_rows], up_w
    )
    grad_middle = upstream + norm_back(unit2, scale2, gains[2], grad_normed_mid)
    grad_branch = norm_back(unit1, scale1, gains[1], grad_middle).astype(BF)
    grad_attended = mm_nt(grad_branch, attn_w).astype(BF)
    to_groups = [lax.dynamic_slice_in_dim(grad_attended, g * part, part, 1) for g in groups]
    grad_out = jnp.concatenate(
        [to_groups[0]] + [swap(to_groups[g], g) for g in range(1, 4)], axis=0
    )
    attn_g = mm_tn(attended, grad_branch).astype(BF)
    half_cols = dim // 2
    attn_half = lax.dynamic_slice_in_dim(attn_g, c * half_cols, half_cols, 1).astype(F32) + swap(
        lax.dynamic_slice_in_dim(attn_g, (1 - c) * half_cols, half_cols, 1), 1
    ).astype(F32)
    attn_half = attn_half.astype(BF)
    down_sum = ring_scatter(
        lambda s: lax.dynamic_slice_in_dim(down_g, s * ff_half, ff_half, 0), n, False
    )
    up_sum = ring_scatter(
        lambda s: jnp.concatenate(
            [
                lax.dynamic_slice_in_dim(up_g, s * shard, shard, 0),
                lax.dynamic_slice_in_dim(attn_half, s * shard, shard, 0),
            ],
            axis=1,
        ),
        n,
        True,
    )
    grad_mixed = attention_back(
        order, length[None], qkv, grad_out, att, lse, cosine, sine_signed, blk
    )
    qkv_g = mm_tn(normed, grad_mixed).astype(BF)
    partial = mm_nt(grad_mixed, qkv_w).astype(BF).reshape(4, own_rows, dim)
    came = swap(jnp.stack([partial[1], partial[3]]), 1).astype(F32)
    own_part = partial[0].astype(F32) + came[0]
    for_x = (partial[2].astype(F32) + came[1]).astype(BF)
    grad_normed = own_part + swap(for_x, 2).astype(F32)
    unit0, scale0 = normalize(hidden)
    input_grad = grad_middle + norm_back(unit0, scale0, gains[0], grad_normed)
    gains_g = jnp.stack(
        [
            jnp.sum(grad_normed * unit0, axis=0),
            jnp.sum(grad_middle * unit1, axis=0),
            jnp.sum(grad_normed_mid * unit2, axis=0),
            jnp.sum(upstream * unit3, axis=0),
        ]
    ).astype(BF)
    gains_p = jnp.pad(
        jnp.transpose(gains_g.reshape(4, n, shard), (1, 0, 2)),
        ((0, 0), (0, extra - 4), (0, 3 * part - shard)),
    )
    last = ring_scatter(
        lambda s: jnp.concatenate(
            [
                lax.dynamic_slice_in_dim(qkv_g, s * shard, shard, 0),
                lax.dynamic_index_in_dim(gains_p, s, 0, keepdims=False),
            ],
            axis=0,
        ),
        n,
        False,
    )

    def rounded(value):
        return lax.reduce_precision(value, 8, 7)

    def both_x(value):
        value = rounded(value)
        return value + swap(value.astype(BF), 2).astype(F32)

    down_x, up_x = both_x(down_sum), both_x(up_sum)
    down_both = jnp.stack([down_x, swap(down_x, 1)])
    up_both = jnp.stack([up_x, swap(up_x, 1)])

    def by_core(stacked):
        return [
            lax.dynamic_index_in_dim(stacked, lax.bitwise_xor(c, b), 0, keepdims=False)
            for b in range(2)
        ]

    down_out = jnp.concatenate(by_core(down_both), axis=0)
    up_two = by_core(up_both)
    mlp_width = n * ff_half
    up_out = jnp.stack(
        [v[:, :mlp_width].reshape(shard, n, ff_half) for v in up_two], axis=2
    ).reshape(shard, ff)
    attn_out = jnp.concatenate([v[:, mlp_width:] for v in up_two], axis=1)
    last = rounded(last)
    last_b = last.astype(BF)
    last_x = swap(last_b, 2)
    last_pair = swap(jnp.stack([last_b, last_x]), 1)
    stacked = jnp.stack([last_b, last_pair[0], last_x, last_pair[1]])
    quarters = [
        lax.dynamic_index_in_dim(stacked, lax.bitwise_xor(q, b), 0, keepdims=False).astype(F32)
        for b in range(4)
    ]
    qkv_out = jnp.concatenate(
        [quarters[b][:shard, t * part : (t + 1) * part] for t in range(3) for b in range(4)],
        axis=1,
    )
    gains_out = (
        quarters[0][shard : shard + 4, :shard]
        + quarters[1][shard : shard + 4, :shard]
        + quarters[2][shard : shard + 4, :shard]
        + quarters[3][shard : shard + 4, :shard]
    ).T
    return (
        result.astype(BF)[None],
        input_grad[None],
        qkv_out,
        attn_out,
        up_out,
        down_out,
        gains_out,
    )


def solution(mesh):
    n = mesh.shape["fsdp"]

    def step(*args):
        return per_device(n, *args)

    rows = P("fsdp", "ctx", None)
    weight = P("fsdp", None)
    return jax.shard_map(
        step,
        mesh=mesh,
        in_specs=(rows, rows, P("fsdp"), P()) + (weight,) * 5,
        out_specs=(rows, rows) + (weight,) * 5,
        check_vma=False,
    )
```

```python
import math

import jax
import jax.numpy as jnp
from jax import lax
from jax.experimental import pallas as pl
from jax.experimental.pallas import tpu as pltpu
from jax.sharding import PartitionSpec as P

HEAD_DIM = 64
PAIR = 2 * HEAD_DIM
EXTRA = 16
BF = jnp.bfloat16
F32 = jnp.float32
NEG = -1e30
EPS = 1e-05
VM = pl.BlockSpec(memory_space=pltpu.VMEM)
SM = pl.BlockSpec(memory_space=pltpu.SMEM)


def mm(left, right):
    return jnp.dot(left, right, preferred_element_type=F32)


def mm_tn(left, right):
    return lax.dot_general(left, right, (((0,), (0,)), ((), ())), preferred_element_type=F32)


def mm_nt(left, right):
    return lax.dot_general(left, right, (((1,), (1,)), ((), ())), preferred_element_type=F32)


def swap(value, bit):
    return lax.ppermute(value, "ctx", [(i, i ^ bit) for i in range(4)])


def blank(shape, dtype):
    return pl.pallas_call(
        lambda out_ref: None,
        out_specs=pl.BlockSpec(memory_space=pl.ANY),
        out_shape=jax.ShapeDtypeStruct(shape, dtype),
        name="blank",
    )()


def ring_pairs(n):
    order = list(range(0, n, 2)) + list(range(n - 1, 0, -2))
    ahead = [(order[i], order[(i + 1) % n]) for i in range(n)]
    return ahead, [(b, a) for a, b in ahead]


def ring_owner(place, n):
    place = lax.rem(place + 2 * n, n)
    return jnp.where(place < n // 2, 2 * place, 2 * (n - place) - 1)


def ring_place(me, n):
    return jnp.where(lax.rem(me, 2) == 0, lax.div(me, 2), n - 1 - lax.div(me, 2))


def after(value, *others):
    return lax.optimization_barrier((value,) + others)[0] if others else value


class Gather:
    def __init__(self, block, n, flip, store, target):
        self.ahead, self.back = ring_pairs(n)
        self.sign = -1
        if flip:
            self.ahead, self.back, self.sign = self.back, self.ahead, 1
        me = lax.axis_index("fsdp")
        self.n, self.place, self.count = n, ring_place(me, n), 0
        self.store, self.one, self.two = store, block, block
        self.target = store(target, me, block)

    def step(self, *others):
        if self.count == self.n // 2:
            return
        self.count += 1
        n, hops = self.n, self.sign * self.count
        self.one = lax.ppermute(after(self.one, *others), "fsdp", self.ahead)
        both = self.count <= (n - 1) // 2
        if both:
            self.two = lax.ppermute(after(self.two, *others), "fsdp", self.back)
        self.target = self.store(self.target, ring_owner(self.place + hops, n), self.one)
        if both:
            self.target = self.store(self.target, ring_owner(self.place - hops, n), self.two)

    def rest(self):
        while self.count < self.n // 2:
            self.step()
        return self.target


class Scatter:
    def __init__(self, pick, n, flip):
        self.ahead, self.back = ring_pairs(n)
        self.sign = 1
        if flip:
            self.ahead, self.back, self.sign = self.back, self.ahead, -1
        self.place = ring_place(lax.axis_index("fsdp"), n)
        self.n, self.pick, self.count = n, pick, 0
        self.one = self.at(self.sign * (n // 2))
        self.two = self.at(-self.sign * ((n - 1) // 2))

    def at(self, offset, *blocks):
        return self.pick(ring_owner(self.place + offset, self.n), *blocks)

    def step(self, *others):
        if self.count == self.n // 2:
            return
        self.count += 1
        self.one = lax.ppermute(after(self.one, *others), "fsdp", self.ahead)
        both = self.count <= (self.n - 1) // 2
        if both:
            self.two = lax.ppermute(after(self.two, *others), "fsdp", self.back)
        left = self.n // 2 - self.count
        if left > 0:
            self.one = self.at(self.sign * left, self.one)
        left = (self.n - 1) // 2 - self.count
        if both and left > 0:
            self.two = self.at(-self.sign * left, self.two)

    def rest(self):
        while self.count < self.n // 2:
            self.step()
        return self.at(0, self.one, self.two)


def rows_of(array, size):
    def pick(owner, *blocks):
        value = lax.dynamic_slice_in_dim(array, owner * size, size, 0)
        if not blocks:
            return value
        value = value.astype(F32)
        for block in blocks:
            value = value + block.astype(F32)
        return value.astype(BF)

    return pick


def up_pick(up_g, attn_half, sums, shard):
    wide, narrow = up_g.shape[1], attn_half.shape[1]

    def pick(owner, *blocks):
        def body(owner_ref, up_ref, attn_ref, sums_ref, *refs):
            out_ref = refs[-1]

            def put(rows, cols, value):
                if blocks:
                    value = value.astype(F32)
                    for ref in refs[:-1]:
                        value = value + ref[rows, cols].astype(F32)
                out_ref[rows, cols] = value.astype(BF)

            top, below = slice(0, shard), slice(shard, shard + EXTRA)
            put(top, slice(0, wide), up_ref[...])
            put(top, slice(wide, wide + narrow), attn_ref[...])
            put(below, slice(0, sums.shape[1]), sums_ref[...])
            out_ref[below, sums.shape[1] :] = jnp.zeros(
                (EXTRA, wide + narrow - sums.shape[1]), BF
            )

        whole = pl.BlockSpec((shard + EXTRA, wide + narrow), lambda i, o: (0, 0))
        return pl.pallas_call(
            body,
            grid_spec=pltpu.PrefetchScalarGridSpec(
                num_scalar_prefetch=1,
                grid=(1,),
                in_specs=[
                    pl.BlockSpec((shard, wide), lambda i, o: (o[0], 0)),
                    pl.BlockSpec((shard, narrow), lambda i, o: (o[0], 0)),
                    pl.BlockSpec(sums.shape, lambda i, o: (0, 0)),
                ]
                + [whole] * len(blocks),
                out_specs=whole,
            ),
            out_shape=jax.ShapeDtypeStruct((shard + EXTRA, wide + narrow), BF),
            compiler_params=pltpu.CompilerParams(vmem_limit_bytes=16 << 20),
            cost_estimate=pl.CostEstimate(
                flops=1 << 20, bytes_accessed=(2 + len(blocks)) << 20, transcendentals=0
            ),
            name="up_pick",
        )(owner[None], up_g, attn_half, sums, *blocks)

    return pick


def normalize(values):
    average = jnp.mean(values, axis=-1, keepdims=True)
    centered = values - average
    variance = jnp.mean(centered * centered, axis=-1, keepdims=True)
    scale = lax.rsqrt(variance + EPS)
    return centered * scale, scale


def norm_back(unit, scale, gain, incoming):
    weighted = incoming * gain
    return (
        weighted
        - jnp.mean(weighted, axis=-1, keepdims=True)
        - unit * jnp.mean(weighted * unit, axis=-1, keepdims=True)
    ) * scale


def turned(value, cosine, sine_signed, inverse):
    width = value.shape[1]
    lane = lax.broadcasted_iota(jnp.int32, value.shape, 1)
    half = HEAD_DIM // 2
    other = jnp.where(
        lax.rem(lane, HEAD_DIM) < half,
        pltpu.roll(value, width - half, 1),
        pltpu.roll(value, half, 1),
    )
    repeat = width // cosine.shape[1]
    cosine = jnp.concatenate([cosine] * repeat, axis=1)
    sine_signed = jnp.concatenate([sine_signed] * repeat, axis=1)
    if inverse:
        return value * cosine - other * sine_signed
    return value * cosine + other * sine_signed


def project(hidden, weight, gain, cosine, sine_signed):
    rows, dim = hidden.shape
    width = weight.shape[1]
    pairs = width // (3 * PAIR)
    step = 512

    def body(hidden_ref, weight_ref, gain_ref, cos_ref, sin_ref, normed_ref, *out_refs):
        unit, _ = normalize(hidden_ref[...].astype(F32))
        normed = (unit * gain_ref[0:1, :].astype(F32)).astype(BF)
        normed_ref[...] = normed
        mixed = mm(normed, weight_ref[...])
        cos_part, sin_part = cos_ref[...], sin_ref[...]
        for p, out_ref in enumerate(out_refs):
            at = 3 * PAIR * p
            queries = turned(mixed[:, at : at + PAIR], cos_part, sin_part, False)
            out_ref[:, :PAIR] = (queries * (0.125 * math.log2(math.e))).astype(BF)
            out_ref[:, PAIR : 2 * PAIR] = turned(
                mixed[:, at + PAIR : at + 2 * PAIR], cos_part, sin_part, False
            ).astype(BF)
            out_ref[:, 2 * PAIR :] = mixed[:, at + 2 * PAIR : at + 3 * PAIR].astype(BF)

    return pl.pallas_call(
        body,
        grid=(rows // step,),
        in_specs=[
            pl.BlockSpec((step, dim), lambda i: (i, 0)),
            pl.BlockSpec((dim, width), lambda i: (0, 0)),
            pl.BlockSpec((EXTRA, dim), lambda i: (0, 0)),
            pl.BlockSpec((step, 128), lambda i: (i, 0)),
            pl.BlockSpec((step, 128), lambda i: (i, 0)),
        ],
        out_specs=[
            pl.BlockSpec((step, dim), lambda i: (i, 0)),
        ]
        + [pl.BlockSpec((step, 3 * PAIR), lambda i: (i, 0))] * pairs,
        out_shape=[jax.ShapeDtypeStruct((rows, dim), BF)]
        + [jax.ShapeDtypeStruct((rows, 3 * PAIR), BF)] * pairs,
        compiler_params=pltpu.CompilerParams(vmem_limit_bytes=32 << 20),
        cost_estimate=pl.CostEstimate(
            flops=2 * rows * dim * width, bytes_accessed=12 << 20, transcendentals=rows
        ),
        name="project",
    )(hidden, weight, gain, cosine, sine_signed)


def folded(value, op):
    rows, cols = value.shape
    return op(value.reshape(rows // 8, 8, cols), axis=0)


def head_columns(target, p, value_t, heads):
    for h in range(heads):
        at = slice(h * HEAD_DIM, (h + 1) * HEAD_DIM)
        if h:
            target[p, h, : h * HEAD_DIM, :] = jnp.zeros((h * HEAD_DIM, value_t.shape[1]), BF)
        target[p, h, at, :] = value_t[at, :]
        rest = (heads - 1 - h) * HEAD_DIM
        if rest:
            target[p, h, (h + 1) * HEAD_DIM :, :] = jnp.zeros((rest, value_t.shape[1]), BF)


def tile_mask(i, j, live, blk):
    key = j * blk + lax.broadcasted_iota(jnp.int32, (blk, blk), 0)
    query = i * blk + lax.broadcasted_iota(jnp.int32, (blk, blk), 1)
    return (key <= query) & (key < live)


def open_tiles(edge, nb):
    return sum(jnp.minimum(i, edge) for i in range(nb))


def next_open(i, j, edge, nb):
    end = j + 1 >= jnp.minimum(i, edge)
    return jnp.minimum(jnp.where(end, i + 1, i), nb - 1), jnp.where(end, 0, j + 1)


def attention(order, length, qkv, blk):
    rows = qkv.shape[0]
    width = qkv.shape[1] // 3
    heads = width // HEAD_DIM
    nb = rows // blk

    def body(order_ref, length_ref, qkv_ref, out_ref, lse_ref, keys, values_t, q_cols, even, odd, even_top, odd_top, total, tops, sums):
        live = length_ref[0]
        edge = lax.div(live, blk)

        def fill(p, carry):
            rows_at = pl.ds(pl.multiple_of(order_ref[p] * blk, blk), blk)
            keys[p] = qkv_ref[rows_at, width : 2 * width]
            values_t[p] = jnp.transpose(qkv_ref[rows_at, 2 * width :])
            head_columns(q_cols, p, jnp.transpose(qkv_ref[rows_at, :width]), heads)
            return carry

        lax.fori_loop(0, nb, fill, 0)

        def ahead(i, j, into, top, masks):
            key_block = keys[j]
            for h in range(heads):
                s = mm(key_block, q_cols[i, h])
                if masks:
                    s = jnp.where(tile_mask(i, j, live, blk), s, NEG)
                into[h] = s
                top[h] = folded(s, jnp.max)

        def work(i, j, scores, top, first):
            for h in range(heads):
                new = jnp.broadcast_to(jnp.max(top[h], axis=0, keepdims=True), (8, blk))
                if not first:
                    old = tops[i, h]
                    new = jnp.maximum(old, new)
                    shrink = jnp.exp2(old - new)
                tops[i, h] = new
                p = jnp.exp2(scores[h] - new[0:1])
                added = folded(p, jnp.sum)
                sums[i, h] = added if first else sums[i, h] * shrink + added
                at = slice(h * HEAD_DIM, (h + 1) * HEAD_DIM)
                product = mm(values_t[j, at, :], p.astype(BF))
                total[i, at, :] = product if first else total[i, at, :] * shrink[0:1] + product

        ahead(0, 0, even, even_top, True)

        def masked_pair(t, carry):
            i0 = 2 * t
            i1 = i0 + 1
            i2 = jnp.minimum(i0 + 2, nb - 1)
            ahead(i1, jnp.minimum(i1, edge), odd, odd_top, True)
            work(i0, jnp.minimum(i0, edge), even, even_top, True)
            ahead(i2, jnp.minimum(i2, edge), even, even_top, True)
            work(i1, jnp.minimum(i1, edge), odd, odd_top, True)
            return carry

        lax.fori_loop(0, nb // 2, masked_pair, 0)

        ahead(1, 0, even, even_top, False)

        def pair(t, place):
            i0, j0 = place
            i1, j1 = next_open(i0, j0, edge, nb)
            ahead(i1, j1, odd, odd_top, False)
            work(i0, j0, even, even_top, False)
            i2, j2 = next_open(i1, j1, edge, nb)
            ahead(i2, j2, even, even_top, False)
            work(i1, j1, odd, odd_top, False)
            return (i2, j2)

        count = open_tiles(edge, nb)
        i_last, j_last = lax.fori_loop(0, lax.div(count, 2), pair, (jnp.int32(1), jnp.int32(0)))

        @pl.when(lax.rem(count, 2) == 1)
        def _():
            work(i_last, j_last, even, even_top, False)

        def drain(p, carry):
            rows_at = pl.ds(pl.multiple_of(order_ref[p] * blk, blk), blk)
            scaled = []
            for h in range(heads):
                sum_h = jnp.sum(sums[p, h], axis=0, keepdims=True)
                lse_ref[p, h : h + 1, :] = tops[p, h][0:1] + jnp.log2(sum_h)
                scaled.append((total[p, h * HEAD_DIM : (h + 1) * HEAD_DIM, :] * (1.0 / sum_h)).astype(BF))
            out_ref[rows_at, :] = jnp.transpose(jnp.concatenate(scaled, axis=0))
            return carry

        lax.fori_loop(0, nb, drain, 0)

    vm = pl.BlockSpec(memory_space=pltpu.VMEM)
    sm = pl.BlockSpec(memory_space=pltpu.SMEM)
    return pl.pallas_call(
        body,
        in_specs=[sm, sm, vm],
        out_specs=[vm, vm],
        out_shape=[jax.ShapeDtypeStruct((rows, width), BF), jax.ShapeDtypeStruct((nb, 8, blk), F32)],
        scratch_shapes=[
            pltpu.VMEM((nb, blk, width), BF),
            pltpu.VMEM((nb, width, blk), BF),
            pltpu.VMEM((nb, heads, width, blk), BF),
            pltpu.VMEM((heads, blk, blk), F32),
            pltpu.VMEM((heads, blk, blk), F32),
            pltpu.VMEM((heads, 8, blk), F32),
            pltpu.VMEM((heads, 8, blk), F32),
            pltpu.VMEM((nb, width, blk), F32),
            pltpu.VMEM((nb, heads, 8, blk), F32),
            pltpu.VMEM((nb, heads, 8, blk), F32),
        ],
        compiler_params=pltpu.CompilerParams(vmem_limit_bytes=24 << 20),
        cost_estimate=pl.CostEstimate(
            flops=heads * 4500000000, bytes_accessed=3 << 20, transcendentals=heads << 21
        ),
        name="attention",
    )(order, length, qkv)


def attention_back(order, length, qkv, grad_out, out, lse, cosine, sine_signed, blk):
    rows = qkv.shape[0]
    width = qkv.shape[1] // 3
    heads = width // HEAD_DIM
    nb = rows // blk

    def body(
        order_ref, length_ref, qkv_ref, gout_ref, att_ref, lse_ref, cos_ref, sin_ref, result_ref,
        keys, keys_t, values, q_cols, q_rows, g_cols, g_rows, grad_q, grad_k, grad_v, inner,
        even_p, even_d, odd_p, odd_d,
    ):
        live = length_ref[0]
        edge = lax.div(live, blk)
        lane_head = lax.div(lax.broadcasted_iota(jnp.int32, (1, width), 1), HEAD_DIM)
        picks = [jnp.where(lane_head == h, 1.0, 0.0).astype(BF) for h in range(heads)]

        def fill(p, carry):
            rows_at = pl.ds(pl.multiple_of(order_ref[p] * blk, blk), blk)
            key_block = qkv_ref[rows_at, width : 2 * width]
            keys[p] = key_block
            keys_t[p] = jnp.transpose(key_block)
            values[p] = qkv_ref[rows_at, 2 * width :]
            grad_k[p] = jnp.zeros((blk, width), F32)
            grad_v[p] = jnp.zeros((blk, width), F32)
            query = qkv_ref[rows_at, :width]
            gout = gout_ref[rows_at, :]
            inner_t = jnp.transpose(gout.astype(F32) * att_ref[rows_at, :].astype(F32))
            head_columns(q_cols, p, jnp.transpose(query), heads)
            head_columns(g_cols, p, jnp.transpose(gout), heads)
            for h in range(heads):
                at = slice(h * blk, (h + 1) * blk)
                q_rows[p, at, :] = query * picks[h]
                g_rows[p, at, :] = gout * picks[h]
                inner[p, h : h + 1, :] = jnp.sum(
                    inner_t[h * HEAD_DIM : (h + 1) * HEAD_DIM, :], axis=0, keepdims=True
                )
            return carry

        lax.fori_loop(0, nb, fill, 0)

        def make(i, j, to_p, to_d, masks):
            key_block, value_block = keys[j], values[j]
            for h in range(heads):
                s = mm(key_block, q_cols[i, h])
                if masks:
                    s = jnp.where(tile_mask(i, j, live, blk), s, NEG)
                p = jnp.exp2(s - lse_ref[i, h : h + 1, :])
                d = p * (mm(value_block, g_cols[i, h]) - inner[i, h : h + 1, :])
                to_p[:, h * blk : (h + 1) * blk] = p.astype(BF)
                to_d[:, h * blk : (h + 1) * blk] = d.astype(BF)

        def use(i, j, from_p, from_d, first):
            grad_v[j] += mm(from_p[...], g_rows[i])
            grad_k[j] += mm(from_d[...], q_rows[i])
            for h in range(heads):
                at = slice(h * HEAD_DIM, (h + 1) * HEAD_DIM)
                product = mm(keys_t[j, at, :], from_d[:, h * blk : (h + 1) * blk])
                if first:
                    grad_q[i, at, :] = product
                else:
                    grad_q[i, at, :] += product

        make(0, 0, even_p, even_d, True)

        def masked_pair(t, carry):
            i0 = 2 * t
            i1 = i0 + 1
            i2 = jnp.minimum(i0 + 2, nb - 1)
            make(i1, jnp.minimum(i1, edge), odd_p, odd_d, True)
            use(i0, jnp.minimum(i0, edge), even_p, even_d, True)
            make(i2, jnp.minimum(i2, edge), even_p, even_d, True)
            use(i1, jnp.minimum(i1, edge), odd_p, odd_d, True)
            return carry

        lax.fori_loop(0, nb // 2, masked_pair, 0)

        make(1, 0, even_p, even_d, False)

        def pair(t, place):
            i0, j0 = place
            i1, j1 = next_open(i0, j0, edge, nb)
            make(i1, j1, odd_p, odd_d, False)
            use(i0, j0, even_p, even_d, False)
            i2, j2 = next_open(i1, j1, edge, nb)
            make(i2, j2, even_p, even_d, False)
            use(i1, j1, odd_p, odd_d, False)
            return (i2, j2)

        count = open_tiles(edge, nb)
        i_last, j_last = lax.fori_loop(0, lax.div(count, 2), pair, (jnp.int32(1), jnp.int32(0)))

        @pl.when(lax.rem(count, 2) == 1)
        def _():
            use(i_last, j_last, even_p, even_d, False)

        def drain(p, carry):
            rows_at = pl.ds(pl.multiple_of(order_ref[p] * blk, blk), blk)
            cos_part, sin_part = cos_ref[rows_at, :], sin_ref[rows_at, :]
            result_ref[rows_at, :width] = turned(jnp.transpose(grad_q[p]) * 0.125, cos_part, sin_part, True).astype(BF)
            result_ref[rows_at, width : 2 * width] = turned(grad_k[p] * math.log(2.0), cos_part, sin_part, True).astype(BF)
            result_ref[rows_at, 2 * width :] = grad_v[p].astype(BF)
            return carry

        lax.fori_loop(0, nb, drain, 0)

    vm = pl.BlockSpec(memory_space=pltpu.VMEM)
    sm = pl.BlockSpec(memory_space=pltpu.SMEM)
    return pl.pallas_call(
        body,
        in_specs=[sm, sm] + [vm] * 6,
        out_specs=vm,
        out_shape=jax.ShapeDtypeStruct((rows, 3 * width), BF),
        scratch_shapes=[
            pltpu.VMEM((nb, blk, width), BF),
            pltpu.VMEM((nb, width, blk), BF),
            pltpu.VMEM((nb, blk, width), BF),
            pltpu.VMEM((nb, heads, width, blk), BF),
            pltpu.VMEM((nb, heads * blk, width), BF),
            pltpu.VMEM((nb, heads, width, blk), BF),
            pltpu.VMEM((nb, heads * blk, width), BF),
            pltpu.VMEM((nb, width, blk), F32),
            pltpu.VMEM((nb, blk, width), F32),
            pltpu.VMEM((nb, blk, width), F32),
            pltpu.VMEM((nb, 8, blk), F32),
            pltpu.VMEM((blk, heads * blk), BF),
            pltpu.VMEM((blk, heads * blk), BF),
            pltpu.VMEM((blk, heads * blk), BF),
            pltpu.VMEM((blk, heads * blk), BF),
        ],
        compiler_params=pltpu.CompilerParams(vmem_limit_bytes=36 << 20),
        cost_estimate=pl.CostEstimate(
            flops=heads * 9000000000, bytes_accessed=6 << 20, transcendentals=heads << 21
        ),
        name="attention_back",
    )(order, length, qkv, grad_out, out, lse, cosine, sine_signed)


def gelu_both(u):
    scale = math.sqrt(2.0 / math.pi)
    inside = jnp.tanh(scale * (u + 0.044715 * u * u * u))
    value = 0.5 * u * (1.0 + inside)
    slope = 0.5 * (1.0 + inside) + 0.5 * u * (1.0 - inside * inside) * scale * (
        1.0 + 3.0 * 0.044715 * u * u
    )
    return value, slope


def bundle_up(q, w_qkv, w_attn, gain_rows, part):
    shard, dim = w_attn.shape
    pairs = part // PAIR

    def body(q_ref, qkv_ref, attn_ref, gain_ref, out_ref):
        at = q_ref[0] * part
        for p in range(pairs):
            for t in range(3):
                to = (3 * p + t) * PAIR
                out_ref[:shard, to : to + PAIR] = qkv_ref[
                    :, pl.ds(pl.multiple_of(t * dim + at + p * PAIR, PAIR), PAIR)
                ]
        out_ref[:shard, 3 * part :] = attn_ref[:, pl.ds(pl.multiple_of(at, part), part)]
        out_ref[shard:, :] = jnp.zeros((EXTRA, dim), BF)
        out_ref[shard:, : gain_ref.shape[1]] = gain_ref[...]

    return pl.pallas_call(
        body,
        in_specs=[SM, VM, VM, VM],
        out_specs=VM,
        out_shape=jax.ShapeDtypeStruct((shard + EXTRA, dim), BF),
        compiler_params=pltpu.CompilerParams(vmem_limit_bytes=8 << 20),
        name="bundle_up",
    )(q[None], w_qkv, w_attn, gain_rows)


def attention_end(q, came, attn_w, hidden, gains, blk):
    rows, dim = hidden.shape
    pairs = len(came)
    part = pairs * PAIR

    def body(q_ref, *refs):
        came_refs = refs[:pairs]
        weight_ref, hidden_ref, gain_ref, att_ref, branch_ref, middle_ref, normed_ref = refs[pairs:]
        for b in range(4):
            for p in range(pairs):
                at = b * part + p * PAIR
                att_ref[:, at : at + PAIR] = came_refs[p][lax.bitwise_xor(q_ref[0], b)]
        branch = mm(att_ref[...], weight_ref[...])
        branch_ref[...] = branch
        middle = hidden_ref[...].astype(F32) + normalize(branch)[0] * gain_ref[1:2, :].astype(F32)
        middle_ref[...] = middle
        normed_ref[...] = (normalize(middle)[0] * gain_ref[2:3, :].astype(F32)).astype(BF)

    row = pl.BlockSpec((blk, dim), lambda i: (i, 0))
    return pl.pallas_call(
        body,
        grid=(rows // blk,),
        in_specs=[SM]
        + [pl.BlockSpec((4, blk, PAIR), lambda i: (0, i, 0))] * pairs
        + [
            pl.BlockSpec(attn_w.shape, lambda i: (0, 0)),
            row,
            pl.BlockSpec(gains.shape, lambda i: (0, 0)),
        ],
        out_specs=[row] * 4,
        out_shape=[
            jax.ShapeDtypeStruct((rows, dim), BF),
            jax.ShapeDtypeStruct((rows, dim), F32),
            jax.ShapeDtypeStruct((rows, dim), F32),
            jax.ShapeDtypeStruct((rows, dim), BF),
        ],
        compiler_params=pltpu.CompilerParams(vmem_limit_bytes=24 << 20),
        cost_estimate=pl.CostEstimate(
            flops=2 * rows * dim * dim, bytes_accessed=10 << 20, transcendentals=0
        ),
        name="attention_end",
    )(q[None], *came, attn_w, hidden, gains)


def upstream_of(base_ref, length_ref, cotangent_ref, blk):
    pos = base_ref[pl.program_id(0)] * blk + lax.broadcasted_iota(jnp.int32, (blk, 1), 0)
    return cotangent_ref[...].astype(F32) * jnp.where(pos < length_ref[0], 1.0, 0.0)


def column_sums(value):
    return jnp.sum(value, axis=0, keepdims=True)


def top(bases, length, own, came, middle, cotangent, gains, blk):
    rows, dim = middle.shape

    def body(base_ref, length_ref, own_ref, came_ref, middle_ref, cot_ref, gain_ref, result_ref, grad_ref, sum_ref):
        gain = gain_ref[3:4, :].astype(F32)
        unit, scale = normalize(own_ref[...] + came_ref[...])
        result_ref[...] = (middle_ref[...] + unit * gain).astype(BF)
        upstream = upstream_of(base_ref, length_ref, cot_ref, blk)
        grad_ref[...] = norm_back(unit, scale, gain, upstream).astype(BF)

        @pl.when(pl.program_id(0) == 0)
        def _():
            sum_ref[...] = jnp.zeros_like(sum_ref)

        sum_ref[0:1, :] += column_sums(upstream * unit)

    row = pl.BlockSpec((blk, dim), lambda i: (i, 0))
    return pl.pallas_call(
        body,
        grid=(rows // blk,),
        in_specs=[SM, SM, row, row, row, row, pl.BlockSpec(gains.shape, lambda i: (0, 0))],
        out_specs=[row, row, pl.BlockSpec((8, dim), lambda i: (0, 0))],
        out_shape=[
            jax.ShapeDtypeStruct((rows, dim), BF),
            jax.ShapeDtypeStruct((rows, dim), BF),
            jax.ShapeDtypeStruct((8, dim), F32),
        ],
        compiler_params=pltpu.CompilerParams(vmem_limit_bytes=24 << 20),
        cost_estimate=pl.CostEstimate(flops=20 << 20, bytes_accessed=9 << 20, transcendentals=0),
        name="top",
    )(bases, length, own, came, middle, cotangent, gains)


def middle_back(q, bases, length, own, came, middle, branch, cotangent, gains, attn_w, last_sum, blk):
    rows, dim = middle.shape
    part = dim // 4
    pairs = part // PAIR
    steps = rows // blk

    def body(
        q_ref, base_ref, length_ref, own_ref, came_ref, middle_ref, branch_ref, cot_ref, gain_ref, weight_ref,
        last_ref, middle_out, branch_out, pieces_out, sums_out, attended, sums,
    ):
        i = pl.program_id(0)
        incoming = own_ref[...] + came_ref[...]
        unit, scale = normalize(middle_ref[...])
        grad_middle = upstream_of(base_ref, length_ref, cot_ref, blk) + norm_back(
            unit, scale, gain_ref[2:3, :].astype(F32), incoming
        )
        middle_out[...] = grad_middle
        sum2 = column_sums(incoming * unit)
        unit, scale = normalize(branch_ref[...])
        sum1 = column_sums(grad_middle * unit)
        grad_branch = norm_back(unit, scale, gain_ref[1:2, :].astype(F32), grad_middle).astype(BF)
        branch_out[...] = grad_branch
        attended[...] = mm_nt(grad_branch, weight_ref[...]).astype(BF)
        for g in range(4):
            at = lax.bitwise_xor(q_ref[0], g) * part
            for p in range(pairs):
                pieces_out[p, g] = attended[:, pl.ds(pl.multiple_of(at + p * PAIR, PAIR), PAIR)]

        @pl.when(i == 0)
        def _():
            sums[...] = jnp.zeros_like(sums)

        sums[0:1, :] += sum1
        sums[1:2, :] += sum2

        @pl.when(i == steps - 1)
        def _():
            sums[2:3, :] = last_ref[0:1, :]
            sums_out[...] = sums[...].astype(BF)

    row = pl.BlockSpec((blk, dim), lambda i: (i, 0))

    def whole(array):
        return pl.BlockSpec(array.shape, lambda i: (0, 0))

    return pl.pallas_call(
        body,
        grid=(steps,),
        in_specs=[SM, SM, SM, row, row, row, row, row, whole(gains), whole(attn_w), whole(last_sum)],
        out_specs=[
            row,
            row,
            pl.BlockSpec((pairs, 4, blk, PAIR), lambda i: (0, 0, i, 0)),
            pl.BlockSpec((EXTRA, dim), lambda i: (0, 0)),
        ],
        out_shape=[
            jax.ShapeDtypeStruct((rows, dim), F32),
            jax.ShapeDtypeStruct((rows, dim), BF),
            jax.ShapeDtypeStruct((pairs, 4, rows, PAIR), BF),
            jax.ShapeDtypeStruct((EXTRA, dim), BF),
        ],
        scratch_shapes=[pltpu.VMEM((blk, dim), BF), pltpu.VMEM((EXTRA, dim), F32)],
        compiler_params=pltpu.CompilerParams(vmem_limit_bytes=32 << 20),
        cost_estimate=pl.CostEstimate(
            flops=2 * rows * dim * dim, bytes_accessed=16 << 20, transcendentals=0
        ),
        name="middle_back",
    )(q[None], bases, length, own, came, middle, branch, cotangent, gains, attn_w, last_sum)


def bottom(own, from_core, from_x, hidden, grad_middle, gains, blk):
    rows, dim = hidden.shape

    def body(own_ref, core_ref, x_ref, hidden_ref, middle_ref, gain_ref, out_ref):
        incoming = own_ref[...] + core_ref[...].astype(F32) + x_ref[...].astype(F32)
        unit, scale = normalize(hidden_ref[...].astype(F32))
        out_ref[...] = middle_ref[...] + norm_back(
            unit, scale, gain_ref[0:1, :].astype(F32), incoming
        )

    row = pl.BlockSpec((blk, dim), lambda i: (i, 0))
    return pl.pallas_call(
        body,
        grid=(rows // blk,),
        in_specs=[row] * 5 + [pl.BlockSpec(gains.shape, lambda i: (0, 0))],
        out_specs=row,
        out_shape=jax.ShapeDtypeStruct((rows, dim), F32),
        compiler_params=pltpu.CompilerParams(vmem_limit_bytes=24 << 20),
        cost_estimate=pl.CostEstimate(flops=20 << 20, bytes_accessed=9 << 20, transcendentals=0),
        name="bottom",
    )(own, from_core, from_x, hidden, grad_middle, gains)


def up_end(c, mine, peer, shard, n, ff_half):
    wide = n * ff_half
    narrow = mine.shape[1] - wide
    if ff_half % 128:
        first = jnp.where(c == 0, mine, peer)[:shard]
        second = jnp.where(c == 0, peer, mine)[:shard]
        blocks = [v[:, :wide].reshape(shard, n, ff_half) for v in (first, second)]
        return (
            jnp.stack(blocks, axis=2).reshape(shard, 2 * wide),
            jnp.concatenate([first[:, wide:], second[:, wide:]], axis=1),
        )

    def body(c_ref, mine_ref, peer_ref, up_ref, attn_ref):
        def put(first, second):
            for s in range(n):
                at = slice(s * ff_half, (s + 1) * ff_half)
                up_ref[:, 2 * s * ff_half : (2 * s + 1) * ff_half] = first[:shard, at]
                up_ref[:, (2 * s + 1) * ff_half : (2 * s + 2) * ff_half] = second[:shard, at]
            attn_ref[:, :narrow] = first[:shard, wide:]
            attn_ref[:, narrow:] = second[:shard, wide:]

        @pl.when(c_ref[0] == 0)
        def _():
            put(mine_ref, peer_ref)

        @pl.when(c_ref[0] == 1)
        def _():
            put(peer_ref, mine_ref)

    return pl.pallas_call(
        body,
        in_specs=[SM, VM, VM],
        out_specs=[VM, VM],
        out_shape=[
            jax.ShapeDtypeStruct((shard, 2 * wide), F32),
            jax.ShapeDtypeStruct((shard, 2 * narrow), F32),
        ],
        compiler_params=pltpu.CompilerParams(vmem_limit_bytes=16 << 20),
        cost_estimate=pl.CostEstimate(flops=1 << 20, bytes_accessed=6 << 20, transcendentals=0),
        name="up_end",
    )(c[None], mine, peer)


def qkv_end(q, quarters, w_qkv, own_gains, late, part):
    shard, wide = w_qkv.shape
    pairs = len(quarters)
    dim = wide // 3

    def body(q_ref, *refs):
        quarter_refs = refs[:pairs]
        weight_ref, gain_ref, late_ref, out_ref, gains_ref = refs[pairs:]
        total = jnp.zeros((shard, PAIR), F32)
        for b in range(4):
            for p in range(pairs):
                block = quarter_refs[p][lax.bitwise_xor(q_ref[0], b)].astype(F32)
                for t in range(3):
                    at = t * dim + b * part + p * PAIR
                    value = block[:, t * PAIR : (t + 1) * PAIR]
                    out_ref[:, at : at + PAIR] = value
                    total = total + value * weight_ref[:, at : at + PAIR].astype(F32)
        first = jnp.sum(total, axis=1, keepdims=True) / gain_ref[:, 0:1].astype(F32)
        lane = lax.broadcasted_iota(jnp.int32, (shard, 4), 1)
        gains_ref[...] = jnp.where(lane == 0, first, late_ref[...])

    return pl.pallas_call(
        body,
        in_specs=[SM] + [VM] * (pairs + 3),
        out_specs=[VM, VM],
        out_shape=[
            jax.ShapeDtypeStruct((shard, wide), F32),
            jax.ShapeDtypeStruct((shard, 4), F32),
        ],
        compiler_params=pltpu.CompilerParams(vmem_limit_bytes=16 << 20),
        cost_estimate=pl.CostEstimate(flops=1 << 20, bytes_accessed=4 << 20, transcendentals=0),
        name="qkv_end",
    )(q[None], *quarters, w_qkv, own_gains, late)


def per_device(n, hidden_in, cotangent, lengths, block_of, w_qkv, w_attn, w_up, w_down, norm_gains):
    own_rows, dim = hidden_in.shape[1:]
    rows = 4 * own_rows
    blk = own_rows // 2
    ff = w_up.shape[1]
    shard = dim // n
    ff_half = ff // n // 2
    part = dim // 4
    pairs = part // PAIR
    q = lax.axis_index("ctx")
    c = lax.rem(q, 2)

    gain_rows = jnp.pad(norm_gains.T, ((0, EXTRA - 4), (0, 0)))
    bundle = bundle_up(q, w_qkv, w_attn, gain_rows, part)

    def store_bundle(target, owner, block):
        to_qkv, to_attn, to_gains = target
        return (
            lax.dynamic_update_slice(to_qkv, block[:shard, : 3 * part], (owner * shard, 0)),
            lax.dynamic_update_slice(to_attn, block[:shard, 3 * part :], (owner * shard, 0)),
            lax.dynamic_update_slice(to_gains, block[shard:, :shard], (0, owner * shard)),
        )

    def store_rows(target, owner, block):
        return lax.dynamic_update_slice(target, block, (owner * block.shape[0], 0))

    lead = Gather(
        bundle,
        n,
        False,
        store_bundle,
        (blank((dim, 3 * part), BF), blank((dim, part), BF), blank((EXTRA, dim), BF)),
    )
    lead.step()
    hidden_b = hidden_in[0]
    hidden_x = swap(after(hidden_b, bundle), 2)
    hidden_c = swap(after(hidden_b, bundle), 1)
    hidden_d = swap(hidden_x, 1)
    qkv_w, attn_q, gains = lead.rest()
    up_own = lax.dynamic_index_in_dim(
        w_up.reshape(shard, n, 2, ff_half), c, 2, keepdims=False
    ).reshape(shard, n * ff_half)
    down_own = lax.dynamic_slice_in_dim(w_down, c * ff_half, ff_half, 0)
    up = Gather(after(up_own, lead.one), n, False, store_rows, blank((dim, n * ff_half), BF))
    down = Gather(after(down_own, lead.one), n, True, store_rows, blank((n * ff_half, dim), BF))
    up.step()
    down.step()

    groups = [lax.bitwise_xor(q, g) for g in range(4)]
    blocks = jnp.concatenate([lax.dynamic_slice_in_dim(block_of, g, 1, 0)[0] for g in groups])
    order = jnp.sum(
        jnp.where(
            blocks[None, :] == jnp.arange(8, dtype=jnp.int32)[:, None],
            jnp.arange(8, dtype=jnp.int32)[None, :],
            0,
        ),
        axis=1,
        dtype=jnp.int32,
    )
    bases = blocks[:2]
    offsets = jnp.arange(blk, dtype=jnp.int32)
    pos = (blocks[:, None] * blk + offsets[None, :]).reshape(-1)
    lane = jnp.arange(128, dtype=jnp.int32)
    half_dim = HEAD_DIM // 2
    inverse = jnp.exp((lane % half_dim).astype(F32) * (-2.0 * math.log(10000.0) / HEAD_DIM))
    angles = pos.astype(F32)[:, None] * inverse[None, :]
    cosine = jnp.cos(angles)
    sine_signed = jnp.sin(angles) * jnp.where(lane % HEAD_DIM < half_dim, -1.0, 1.0)[None, :]

    hidden_all = blank((rows, dim), BF)
    for g, block in enumerate((hidden_b, hidden_c, hidden_x, hidden_d)):
        hidden_all = lax.dynamic_update_slice(hidden_all, block, (g * own_rows, 0))
    normed, *qkv = project(hidden_all, qkv_w, gains, cosine, sine_signed)
    up.step(qkv[0])
    attn_x = swap(attn_q, 2)
    attn_pair = swap(jnp.stack([attn_q, attn_x]), 1)
    attn_parts = jnp.stack([attn_q, attn_pair[0], attn_x, attn_pair[1]])
    attn_w = jnp.concatenate(
        [
            lax.dynamic_index_in_dim(attn_parts, lax.bitwise_xor(q, b), 0, keepdims=False)
            for b in range(4)
        ],
        axis=1,
    )
    att, lse, came = [], [], []
    for p in range(pairs):
        att_p, lse_p = attention(order, lengths, qkv[p], blk)
        att.append(att_p)
        lse.append(lse_p)
        att_g = att_p.reshape(4, own_rows, PAIR)
        came.append(jnp.stack([att_g[0]] + [swap(att_g[g], g) for g in range(1, 4)]))
    down.step(*att)
    attended, branch, middle, normed_mid = attention_end(q, came, attn_w, hidden_b, gains, blk)
    normed_mid2 = jnp.concatenate([normed_mid, swap(normed_mid, 1)], axis=0)
    up_w, down_w = up.rest(), down.rest()
    lifted = mm(normed_mid2, up_w)
    activated, slope = [v.astype(BF) for v in gelu_both(lifted)]
    lowered_c = swap(mm(activated[own_rows:], down_w), 1)
    lowered = mm(activated[:own_rows], down_w)
    result, grad_lowered, last_sum = top(
        bases, lengths, lowered, lowered_c, middle, cotangent[0], gains, blk
    )

    grad_lowered2 = jnp.concatenate([grad_lowered, swap(grad_lowered, 1)], axis=0)
    down_g = mm_tn(activated, grad_lowered2).astype(BF)
    down_ring = Scatter(rows_of(down_g, ff_half), n, False)
    down_ring.step()
    grad_lifted = (
        mm_nt(after(grad_lowered2, down_g), down_w) * slope.astype(F32)
    ).astype(BF)
    normed_mid_c = swap(mm_nt(grad_lifted[own_rows:], up_w), 1)
    grad_normed_mid = mm_nt(grad_lifted[:own_rows], up_w)
    grad_middle, grad_branch, pieces, sums = middle_back(
        q, bases, lengths, grad_normed_mid, normed_mid_c, middle, branch, cotangent[0], gains, attn_w, last_sum, blk
    )
    grad_out = [
        jnp.concatenate([pieces[p, 0]] + [swap(pieces[p, g], g) for g in range(1, 4)], axis=0)
        for p in range(pairs)
    ]
    attn_g = mm_tn(attended, grad_branch).astype(BF)
    half_cols = dim // 2
    attn_half = lax.dynamic_slice_in_dim(attn_g, c * half_cols, half_cols, 1).astype(F32) + swap(
        lax.dynamic_slice_in_dim(attn_g, (1 - c) * half_cols, half_cols, 1), 1
    ).astype(F32)
    attn_half = attn_half.astype(BF)
    up_g = mm_tn(normed_mid2, after(grad_lifted, pieces)).astype(BF)
    up_ring = Scatter(up_pick(up_g, attn_half, sums, shard), n, True)
    up_ring.step()
    grad_out[0] = after(grad_out[0], up_g)
    grad_mixed, rings = [], []
    for p in range(pairs):
        mixed_p = attention_back(
            order, lengths, qkv[p], grad_out[p], att[p], lse[p], cosine, sine_signed, blk
        )
        down_ring.step(mixed_p)
        qkv_g = mm_tn(normed, mixed_p).astype(BF)
        rings.append(Scatter(rows_of(qkv_g, shard), n, p % 2 == 1))
        grad_mixed.append(mixed_p)

    def normed_back(g):
        at = slice(g * own_rows, (g + 1) * own_rows)
        wide = 3 * PAIR
        return sum(
            mm_nt(grad_mixed[p][at], qkv_w[:, p * wide : (p + 1) * wide]) for p in range(pairs)
        )

    for_x = (normed_back(2) + swap(normed_back(3).astype(BF), 1).astype(F32)).astype(BF)
    from_x = swap(for_x, 2)
    from_core = swap(normed_back(1).astype(BF), 1)
    input_grad = bottom(normed_back(0), from_core, from_x, hidden_b, grad_middle, gains, blk)

    def both_x(value):
        return value.astype(F32) + swap(value, 2).astype(F32)

    down_x = both_x(down_ring.rest())
    down_c = swap(down_x, 1)
    down_out = jnp.concatenate(
        [jnp.where(c == 0, down_x, down_c), jnp.where(c == 0, down_c, down_x)], axis=0
    )
    up_x = both_x(up_ring.rest())
    up_c = swap(up_x, 1)
    up_out, attn_out = up_end(c, up_x, up_c, shard, n, ff_half)
    me = lax.axis_index("fsdp")
    late = lax.dynamic_slice(up_x, (shard, me * shard), (4, shard)) + lax.dynamic_slice(
        up_c, (shard, me * shard), (4, shard)
    )
    late = jnp.roll(late, 1, axis=0).T
    quarters = []
    for p in range(pairs):
        last = rings[p].rest()
        last_x = swap(last, 2)
        last_pair = swap(jnp.stack([last, last_x]), 1)
        quarters.append(jnp.stack([last, last_pair[0], last_x, last_pair[1]]))
    qkv_out, gains_out = qkv_end(q, quarters, w_qkv, norm_gains, late, part)
    return (
        result[None],
        input_grad[None],
        qkv_out,
        attn_out,
        up_out,
        down_out,
        gains_out,
    )


def solution(mesh):
    n = mesh.shape["fsdp"]

    def step(*args):
        return per_device(n, *args)

    rows = P("fsdp", "ctx", None)
    weight = P("fsdp", None)
    return jax.shard_map(
        step,
        mesh=mesh,
        in_specs=(rows, rows, P("fsdp"), P()) + (weight,) * 5,
        out_specs=(rows, rows) + (weight,) * 5,
        check_vma=False,
    )
```

```python
import math

import jax
import jax.numpy as jnp
import numpy as np
from jax import lax
from jax.experimental import pallas as pl
from jax.experimental.pallas import tpu as pltpu
from jax.sharding import PartitionSpec as P

HEAD_DIM = 64
PAIR = 2 * HEAD_DIM
EXTRA = 16
BF = jnp.bfloat16
F32 = jnp.float32
NEG = -1e30
EPS = 1e-05
VM = pl.BlockSpec(memory_space=pltpu.VMEM)
SM = pl.BlockSpec(memory_space=pltpu.SMEM)
SMALL = pl.CostEstimate(flops=3 << 30, bytes_accessed=6 << 20, transcendentals=0)


def mm(left, right):
    return jnp.dot(left, right, preferred_element_type=F32)


def mm_tn(left, right):
    return lax.dot_general(left, right, (((0,), (0,)), ((), ())), preferred_element_type=F32)


def mm_nt(left, right):
    return lax.dot_general(left, right, (((1,), (1,)), ((), ())), preferred_element_type=F32)


def swap(value, bit):
    return lax.ppermute(value, "ctx", [(i, i ^ bit) for i in range(4)])


def blank(shape, dtype):
    return pl.pallas_call(
        lambda out_ref: None,
        out_specs=pl.BlockSpec(memory_space=pl.ANY),
        out_shape=jax.ShapeDtypeStruct(shape, dtype),
        name="blank",
    )()


def ring_pairs(n):
    order = list(range(0, n, 2)) + list(range(n - 1, 0, -2))
    ahead = [(order[i], order[(i + 1) % n]) for i in range(n)]
    return ahead, [(b, a) for a, b in ahead]


def ring_owner(place, n):
    place = lax.rem(place + 2 * n, n)
    return jnp.where(place < n // 2, 2 * place, 2 * (n - place) - 1)


def ring_place(me, n):
    return jnp.where(lax.rem(me, 2) == 0, lax.div(me, 2), n - 1 - lax.div(me, 2))


def tie(*trees):
    return lax.optimization_barrier(trees)


class Gather:
    def __init__(self, block, n, flip, store, target):
        self.ahead, self.back = ring_pairs(n)
        self.sign = -1
        if flip:
            self.ahead, self.back, self.sign = self.back, self.ahead, 1
        me = lax.axis_index("fsdp")
        self.n, self.place, self.count = n, ring_place(me, n), 0
        self.store, self.blocks = store, [block, block]
        self.target = store(target, me, block)

    def more(self):
        return self.count < self.n // 2

    def send(self):
        self.count += 1
        sent = [lax.ppermute(self.blocks[0], "fsdp", self.ahead)]
        if self.count <= (self.n - 1) // 2:
            sent.append(lax.ppermute(self.blocks[1], "fsdp", self.back))
        return sent

    def land(self, came):
        self.blocks = came
        for block, sign in zip(came, (self.sign, -self.sign)):
            owner = ring_owner(self.place + sign * self.count, self.n)
            self.target = self.store(self.target, owner, block)

    def rest(self):
        while self.more():
            self.land(tie(self.send())[0])
        return self.target


class Scatter:
    def __init__(self, pick, n, flip):
        self.ahead, self.back = ring_pairs(n)
        self.sign = 1
        if flip:
            self.ahead, self.back, self.sign = self.back, self.ahead, -1
        self.place = ring_place(lax.axis_index("fsdp"), n)
        self.n, self.pick, self.count = n, pick, 0
        self.blocks = [self.at(self.sign * (n // 2)), self.at(-self.sign * ((n - 1) // 2))]

    def at(self, offset, *blocks):
        return self.pick(offset, ring_owner(self.place + offset, self.n), *blocks)

    def more(self):
        return self.count < self.n // 2

    def send(self):
        self.count += 1
        sent = [lax.ppermute(self.blocks[0], "fsdp", self.ahead)]
        if self.count <= (self.n - 1) // 2:
            sent.append(lax.ppermute(self.blocks[1], "fsdp", self.back))
        return sent

    def land(self, came):
        one, two = self.n // 2 - self.count, (self.n - 1) // 2 - self.count
        if one > 0:
            self.blocks[0] = self.at(self.sign * one, came[0])
            if two > 0:
                self.blocks[1] = self.at(-self.sign * two, came[1])
            elif len(came) > 1:
                self.blocks[1] = came[1]
        else:
            self.total = self.at(0, came[0], came[1] if len(came) > 1 else self.blocks[1])

    def rest(self):
        while self.more():
            self.land(tie(self.send())[0])
        return self.total


def rows_of(array, size):
    def pick(offset, owner, *blocks):
        value = lax.dynamic_slice_in_dim(array, owner * size, size, 0)
        if not blocks:
            return value
        value = value.astype(F32)
        for block in blocks:
            value = value + block.astype(F32)
        return value.astype(BF)

    return pick


def spots(n):
    far, near = n // 2, (n - 1) // 2
    order = []
    for k in range(far):
        order.append(far - k)
        if k < near:
            order.append(k - near)
    return order + [0]


def picked(array, owners, side):
    rows, cols = array.shape[2:]
    count = owners.shape[0]

    def body(owners_ref, side_ref, from_ref, to_ref):
        to_ref[...] = from_ref[...].reshape(rows, cols)

    return pl.pallas_call(
        body,
        grid_spec=pltpu.PrefetchScalarGridSpec(
            num_scalar_prefetch=2,
            grid=(count,),
            in_specs=[pl.BlockSpec((1, 1, rows, cols), lambda i, o, d: (o[i], d[0], 0, 0))],
            out_specs=pl.BlockSpec((rows, cols), lambda i, o, d: (i, 0)),
        ),
        out_shape=jax.ShapeDtypeStruct((count * rows, cols), array.dtype),
        compiler_params=pltpu.CompilerParams(vmem_limit_bytes=8 << 20),
        cost_estimate=pl.CostEstimate(flops=1 << 20, bytes_accessed=2 << 20, transcendentals=0),
        name="picked",
    )(owners, side[None], array)


def down_pick(down_g, side, from_x, n):
    rows, dim = down_g.shape[2:]
    order = spots(n)

    def pick(offset, owner, *blocks):
        each = n // 4
        place = order.index(offset)
        value = lax.dynamic_slice(down_g, (owner, side, 0, 0), (1, 1, rows, dim)).reshape(rows, dim)
        at = place % each * rows
        value = value.astype(F32) + from_x[place // each][at : at + rows].astype(F32)
        for block in blocks:
            value = value + block.astype(F32)
        return value.astype(BF)

    return pick


def last_pick(wide_g, narrow_g, sums, rows):
    wide, narrow = wide_g.shape[1], narrow_g.shape[1]

    def pick(offset, owner, *blocks):
        def body(owner_ref, wide_ref, narrow_ref, sums_ref, *refs):
            out_ref = refs[-1]

            def put(at_rows, at_cols, value):
                value = value.astype(F32)
                for ref in refs[:-1]:
                    value = value + ref[at_rows, at_cols].astype(F32)
                out_ref[at_rows, at_cols] = value.astype(BF)

            upper, lower = slice(0, rows), slice(rows, rows + EXTRA)
            put(upper, slice(0, wide), wide_ref[...])
            put(upper, slice(wide, wide + narrow), narrow_ref[...])
            put(lower, slice(0, wide + narrow), sums_ref[...])

        whole = pl.BlockSpec((rows + EXTRA, wide + narrow), lambda i, o: (0, 0))
        return pl.pallas_call(
            body,
            grid_spec=pltpu.PrefetchScalarGridSpec(
                num_scalar_prefetch=1,
                grid=(1,),
                in_specs=[
                    pl.BlockSpec((rows, wide), lambda i, o: (o[0], 0)),
                    pl.BlockSpec((rows, narrow), lambda i, o: (o[0], 0)),
                    pl.BlockSpec(sums.shape, lambda i, o: (0, 0)),
                ]
                + [whole] * len(blocks),
                out_specs=whole,
            ),
            out_shape=jax.ShapeDtypeStruct((rows + EXTRA, wide + narrow), BF),
            compiler_params=pltpu.CompilerParams(vmem_limit_bytes=8 << 20),
            cost_estimate=SMALL,
            name="last_pick",
        )(owner[None], wide_g, narrow_g, sums, *blocks)

    return pick


def normalize(values):
    average = jnp.mean(values, axis=-1, keepdims=True)
    centered = values - average
    variance = jnp.mean(centered * centered, axis=-1, keepdims=True)
    scale = lax.rsqrt(variance + EPS)
    return centered * scale, scale


def norm_back(unit, scale, gain, incoming):
    weighted = incoming * gain
    return (
        weighted
        - jnp.mean(weighted, axis=-1, keepdims=True)
        - unit * jnp.mean(weighted * unit, axis=-1, keepdims=True)
    ) * scale


def turned(value, cosine, sine_signed, inverse):
    width = value.shape[1]
    lane = lax.broadcasted_iota(jnp.int32, value.shape, 1)
    half = HEAD_DIM // 2
    other = jnp.where(
        lax.rem(lane, HEAD_DIM) < half,
        pltpu.roll(value, width - half, 1),
        pltpu.roll(value, half, 1),
    )
    repeat = width // cosine.shape[1]
    cosine = jnp.concatenate([cosine] * repeat, axis=1)
    sine_signed = jnp.concatenate([sine_signed] * repeat, axis=1)
    if inverse:
        return value * cosine - other * sine_signed
    return value * cosine + other * sine_signed


def block_at(q_ref, block_ref, k):
    return block_ref[lax.bitwise_xor(q_ref[0], lax.div(k, 2)), lax.rem(k, 2)]


def fill_order(order, q_ref, block_ref, count):
    def put(k, carry):
        order[block_at(q_ref, block_ref, k)] = k
        return carry

    lax.fori_loop(0, count, put, 0)


def rotary_tables(blk, count):
    lane = np.arange(PAIR)
    half = HEAD_DIM // 2
    inverse = np.exp(-2.0 * math.log(10000.0) / HEAD_DIM * (lane % half))
    sign = np.where(lane % HEAD_DIM < half, -1.0, 1.0)
    inside = np.arange(blk)[:, None] * inverse[None, :]
    starts = np.arange(count)[:, None] * blk * inverse[None, :]
    return [
        jnp.asarray(v, F32)
        for v in (np.cos(inside), np.sin(inside) * sign, np.cos(starts), np.sin(starts) * sign)
    ]


def tables_at(table_refs, block):
    cos_in, sin_in, cos_at, sin_at = table_refs
    cos_b, sin_b = cos_at[pl.ds(block, 1), :], sin_at[pl.ds(block, 1), :]
    cos_r, sin_r = cos_in[...], sin_in[...]
    return cos_r * cos_b - sin_r * sin_b, sin_r * cos_b + cos_r * sin_b


def project(q, block_of, hidden, weight, gains, tables, blk):
    rows, dim = hidden.shape
    width = weight.shape[1]
    pairs = width // (3 * PAIR)
    step = 2 * blk

    def body(q_ref, block_ref, hidden_ref, weight_ref, gain_ref, *refs):
        table_refs, normed_ref, out_refs = refs[:4], refs[4], refs[5:]
        unit, _ = normalize(hidden_ref[...].astype(F32))
        normed = (unit * gain_ref[0:1, :].astype(F32)).astype(BF)
        normed_ref[...] = normed
        mixed = mm(normed, weight_ref[...])
        halves = [
            tables_at(table_refs, block_at(q_ref, block_ref, 2 * pl.program_id(0) + k))
            for k in range(2)
        ]
        cos_part, sin_part = [jnp.concatenate(v, axis=0) for v in zip(*halves)]
        for p, out_ref in enumerate(out_refs):
            at = 3 * PAIR * p
            queries = turned(mixed[:, at : at + PAIR], cos_part, sin_part, False)
            out_ref[:, :PAIR] = (queries * (0.125 * math.log2(math.e))).astype(BF)
            out_ref[:, PAIR : 2 * PAIR] = turned(
                mixed[:, at + PAIR : at + 2 * PAIR], cos_part, sin_part, False
            ).astype(BF)
            out_ref[:, 2 * PAIR :] = mixed[:, at + 2 * PAIR : at + 3 * PAIR].astype(BF)

    def whole(array):
        return pl.BlockSpec(array.shape, lambda i: (0, 0))

    return pl.pallas_call(
        body,
        grid=(rows // step,),
        in_specs=[SM, SM, pl.BlockSpec((step, dim), lambda i: (i, 0)), whole(weight), whole(gains)]
        + [whole(t) for t in tables],
        out_specs=[pl.BlockSpec((step, dim), lambda i: (i, 0))]
        + [pl.BlockSpec((step, 3 * PAIR), lambda i: (i, 0))] * pairs,
        out_shape=[jax.ShapeDtypeStruct((rows, dim), BF)]
        + [jax.ShapeDtypeStruct((rows, 3 * PAIR), BF)] * pairs,
        compiler_params=pltpu.CompilerParams(vmem_limit_bytes=32 << 20),
        cost_estimate=pl.CostEstimate(
            flops=2 * rows * dim * width, bytes_accessed=12 << 20, transcendentals=rows
        ),
        name="project",
    )(q[None], block_of, hidden, weight, gains, *tables)


def folded(value, op):
    rows, cols = value.shape
    return op(value.reshape(rows // 8, 8, cols), axis=0)


def head_columns(target, p, value_t, heads):
    for h in range(heads):
        at = slice(h * HEAD_DIM, (h + 1) * HEAD_DIM)
        if h:
            target[p, h, : h * HEAD_DIM, :] = jnp.zeros((h * HEAD_DIM, value_t.shape[1]), BF)
        target[p, h, at, :] = value_t[at, :]
        rest = (heads - 1 - h) * HEAD_DIM
        if rest:
            target[p, h, (h + 1) * HEAD_DIM :, :] = jnp.zeros((rest, value_t.shape[1]), BF)


def tile_mask(i, j, live, blk):
    key = j * blk + lax.broadcasted_iota(jnp.int32, (blk, blk), 0)
    query = i * blk + lax.broadcasted_iota(jnp.int32, (blk, blk), 1)
    return (key <= query) & (key < live)


def open_tiles(edge, nb):
    return sum(jnp.minimum(i, edge) for i in range(nb))


def next_open(i, j, edge, nb):
    end = j + 1 >= jnp.minimum(i, edge)
    return jnp.minimum(jnp.where(end, i + 1, i), nb - 1), jnp.where(end, 0, j + 1)


def attention(q, block_of, length, qkv, blk):
    rows = qkv[0].shape[0]
    pairs = len(qkv)
    width = pairs * PAIR
    heads = width // HEAD_DIM
    nb = rows // blk

    def body(
        q_ref, block_ref, length_ref, *refs,
    ):
        qkv_refs, out_refs, lse_refs = refs[:pairs], refs[pairs : 2 * pairs], refs[2 * pairs : 3 * pairs]
        (keys, values_t, q_cols, even, odd, even_top, odd_top, total, tops, sums, order_ref) = refs[3 * pairs :]
        fill_order(order_ref, q_ref, block_ref, nb)
        live = length_ref[0]
        edge = lax.div(live, blk)

        def fill(p, carry):
            rows_at = pl.ds(pl.multiple_of(order_ref[p] * blk, blk), blk)
            keys[p] = jnp.concatenate([r[rows_at, PAIR : 2 * PAIR] for r in qkv_refs], axis=1)
            values_t[p] = jnp.transpose(
                jnp.concatenate([r[rows_at, 2 * PAIR :] for r in qkv_refs], axis=1)
            )
            queries = jnp.concatenate([r[rows_at, :PAIR] for r in qkv_refs], axis=1)
            head_columns(q_cols, p, jnp.transpose(queries), heads)
            return carry

        lax.fori_loop(0, nb, fill, 0)

        def ahead(i, j, into, top, masks):
            key_block = keys[j]
            for h in range(heads):
                s = mm(key_block, q_cols[i, h])
                if masks:
                    s = jnp.where(tile_mask(i, j, live, blk), s, NEG)
                into[h] = s
                top[h] = folded(s, jnp.max)

        def work(i, j, scores, top, first):
            for h in range(heads):
                new = jnp.broadcast_to(jnp.max(top[h], axis=0, keepdims=True), (8, blk))
                if not first:
                    old = tops[i, h]
                    new = jnp.maximum(old, new)
                    shrink = jnp.exp2(old - new)
                tops[i, h] = new
                p = jnp.exp2(scores[h] - new[0:1])
                added = folded(p, jnp.sum)
                sums[i, h] = added if first else sums[i, h] * shrink + added
                at = slice(h * HEAD_DIM, (h + 1) * HEAD_DIM)
                product = mm(values_t[j, at, :], p.astype(BF))
                total[i, at, :] = product if first else total[i, at, :] * shrink[0:1] + product

        ahead(0, 0, even, even_top, True)

        def masked_pair(t, carry):
            i0 = 2 * t
            i1 = i0 + 1
            i2 = jnp.minimum(i0 + 2, nb - 1)
            ahead(i1, jnp.minimum(i1, edge), odd, odd_top, True)
            work(i0, jnp.minimum(i0, edge), even, even_top, True)
            ahead(i2, jnp.minimum(i2, edge), even, even_top, True)
            work(i1, jnp.minimum(i1, edge), odd, odd_top, True)
            return carry

        lax.fori_loop(0, nb // 2, masked_pair, 0)

        ahead(1, 0, even, even_top, False)

        def pair(t, place):
            i0, j0 = place
            i1, j1 = next_open(i0, j0, edge, nb)
            ahead(i1, j1, odd, odd_top, False)
            work(i0, j0, even, even_top, False)
            i2, j2 = next_open(i1, j1, edge, nb)
            ahead(i2, j2, even, even_top, False)
            work(i1, j1, odd, odd_top, False)
            return (i2, j2)

        count = open_tiles(edge, nb)
        i_last, j_last = lax.fori_loop(0, lax.div(count, 2), pair, (jnp.int32(1), jnp.int32(0)))

        @pl.when(lax.rem(count, 2) == 1)
        def _():
            work(i_last, j_last, even, even_top, False)

        def drain(p, carry):
            rows_at = pl.ds(pl.multiple_of(order_ref[p] * blk, blk), blk)
            scaled = []
            for h in range(heads):
                sum_h = jnp.sum(sums[p, h], axis=0, keepdims=True)
                lse_refs[h // 2][p, h % 2 : h % 2 + 1, :] = tops[p, h][0:1] + jnp.log2(sum_h)
                scaled.append((total[p, h * HEAD_DIM : (h + 1) * HEAD_DIM, :] * (1.0 / sum_h)).astype(BF))
            both = jnp.transpose(jnp.concatenate(scaled, axis=0))
            for k, ref in enumerate(out_refs):
                ref[rows_at, :] = both[:, k * PAIR : (k + 1) * PAIR]
            return carry

        lax.fori_loop(0, nb, drain, 0)

    vm = pl.BlockSpec(memory_space=pltpu.VMEM)
    sm = pl.BlockSpec(memory_space=pltpu.SMEM)
    result = pl.pallas_call(
        body,
        in_specs=[sm, sm, sm] + [vm] * pairs,
        out_specs=[vm] * (2 * pairs),
        out_shape=[jax.ShapeDtypeStruct((rows, PAIR), BF)] * pairs
        + [jax.ShapeDtypeStruct((nb, 8, blk), F32)] * pairs,
        scratch_shapes=[
            pltpu.VMEM((nb, blk, width), BF),
            pltpu.VMEM((nb, width, blk), BF),
            pltpu.VMEM((nb, heads, width, blk), BF),
            pltpu.VMEM((heads, blk, blk), F32),
            pltpu.VMEM((heads, blk, blk), F32),
            pltpu.VMEM((heads, 8, blk), F32),
            pltpu.VMEM((heads, 8, blk), F32),
            pltpu.VMEM((nb, width, blk), F32),
            pltpu.VMEM((nb, heads, 8, blk), F32),
            pltpu.VMEM((nb, heads, 8, blk), F32),
            pltpu.SMEM((nb,), jnp.int32),
        ],
        compiler_params=pltpu.CompilerParams(vmem_limit_bytes=24 << 20),
        cost_estimate=pl.CostEstimate(
            flops=heads * 4500000000, bytes_accessed=3 << 20, transcendentals=heads << 21
        ),
        name="attention",
    )(q[None], block_of, length, *qkv)
    return result[:pairs], result[pairs:]


def attention_back(q, block_of, length, qkv, grad_out, out, lse, tables, blk):
    rows = qkv.shape[0]
    width = qkv.shape[1] // 3
    heads = width // HEAD_DIM
    nb = rows // blk

    def body(
        q_ref, block_ref, length_ref, qkv_ref, gout_ref, att_ref, lse_ref, cos_in, sin_in, cos_at, sin_at, result_ref,
        keys, keys_t, values, q_cols, q_rows, g_cols, g_rows, grad_q, grad_k, grad_v, inner,
        even_p, even_d, odd_p, odd_d, order_ref,
    ):
        fill_order(order_ref, q_ref, block_ref, nb)
        live = length_ref[0]
        edge = lax.div(live, blk)
        lane_head = lax.div(lax.broadcasted_iota(jnp.int32, (1, width), 1), HEAD_DIM)
        picks = [jnp.where(lane_head == h, 1.0, 0.0).astype(BF) for h in range(heads)]

        def fill(p, carry):
            rows_at = pl.ds(pl.multiple_of(order_ref[p] * blk, blk), blk)
            key_block = qkv_ref[rows_at, width : 2 * width]
            keys[p] = key_block
            keys_t[p] = jnp.transpose(key_block)
            values[p] = qkv_ref[rows_at, 2 * width :]
            grad_k[p] = jnp.zeros((blk, width), F32)
            grad_v[p] = jnp.zeros((blk, width), F32)
            query = qkv_ref[rows_at, :width]
            gout = gout_ref[rows_at, :]
            inner_t = jnp.transpose(gout.astype(F32) * att_ref[rows_at, :].astype(F32))
            head_columns(q_cols, p, jnp.transpose(query), heads)
            head_columns(g_cols, p, jnp.transpose(gout), heads)
            for h in range(heads):
                at = slice(h * blk, (h + 1) * blk)
                q_rows[p, at, :] = query * picks[h]
                g_rows[p, at, :] = gout * picks[h]
                inner[p, h : h + 1, :] = jnp.sum(
                    inner_t[h * HEAD_DIM : (h + 1) * HEAD_DIM, :], axis=0, keepdims=True
                )
            return carry

        lax.fori_loop(0, nb, fill, 0)

        def make(i, j, to_p, to_d, masks):
            key_block, value_block = keys[j], values[j]
            for h in range(heads):
                s = mm(key_block, q_cols[i, h])
                if masks:
                    s = jnp.where(tile_mask(i, j, live, blk), s, NEG)
                p = jnp.exp2(s - lse_ref[i, h : h + 1, :])
                d = p * (mm(value_block, g_cols[i, h]) - inner[i, h : h + 1, :])
                to_p[:, h * blk : (h + 1) * blk] = p.astype(BF)
                to_d[:, h * blk : (h + 1) * blk] = d.astype(BF)

        def use(i, j, from_p, from_d, first):
            grad_v[j] += mm(from_p[...], g_rows[i])
            grad_k[j] += mm(from_d[...], q_rows[i])
            for h in range(heads):
                at = slice(h * HEAD_DIM, (h + 1) * HEAD_DIM)
                product = mm(keys_t[j, at, :], from_d[:, h * blk : (h + 1) * blk])
                if first:
                    grad_q[i, at, :] = product
                else:
                    grad_q[i, at, :] += product

        make(0, 0, even_p, even_d, True)

        def masked_pair(t, carry):
            i0 = 2 * t
            i1 = i0 + 1
            i2 = jnp.minimum(i0 + 2, nb - 1)
            make(i1, jnp.minimum(i1, edge), odd_p, odd_d, True)
            use(i0, jnp.minimum(i0, edge), even_p, even_d, True)
            make(i2, jnp.minimum(i2, edge), even_p, even_d, True)
            use(i1, jnp.minimum(i1, edge), odd_p, odd_d, True)
            return carry

        lax.fori_loop(0, nb // 2, masked_pair, 0)

        make(1, 0, even_p, even_d, False)

        def pair(t, place):
            i0, j0 = place
            i1, j1 = next_open(i0, j0, edge, nb)
            make(i1, j1, odd_p, odd_d, False)
            use(i0, j0, even_p, even_d, False)
            i2, j2 = next_open(i1, j1, edge, nb)
            make(i2, j2, even_p, even_d, False)
            use(i1, j1, odd_p, odd_d, False)
            return (i2, j2)

        count = open_tiles(edge, nb)
        i_last, j_last = lax.fori_loop(0, lax.div(count, 2), pair, (jnp.int32(1), jnp.int32(0)))

        @pl.when(lax.rem(count, 2) == 1)
        def _():
            use(i_last, j_last, even_p, even_d, False)

        def drain(p, carry):
            rows_at = pl.ds(pl.multiple_of(order_ref[p] * blk, blk), blk)
            cos_part, sin_part = tables_at((cos_in, sin_in, cos_at, sin_at), p)
            result_ref[rows_at, :width] = turned(jnp.transpose(grad_q[p]) * 0.125, cos_part, sin_part, True).astype(BF)
            result_ref[rows_at, width : 2 * width] = turned(grad_k[p] * math.log(2.0), cos_part, sin_part, True).astype(BF)
            result_ref[rows_at, 2 * width :] = grad_v[p].astype(BF)
            return carry

        lax.fori_loop(0, nb, drain, 0)

    vm = pl.BlockSpec(memory_space=pltpu.VMEM)
    sm = pl.BlockSpec(memory_space=pltpu.SMEM)
    return pl.pallas_call(
        body,
        in_specs=[sm] * 3 + [vm] * 8,
        out_specs=vm,
        out_shape=jax.ShapeDtypeStruct((rows, 3 * width), BF),
        scratch_shapes=[
            pltpu.VMEM((nb, blk, width), BF),
            pltpu.VMEM((nb, width, blk), BF),
            pltpu.VMEM((nb, blk, width), BF),
            pltpu.VMEM((nb, heads, width, blk), BF),
            pltpu.VMEM((nb, heads * blk, width), BF),
            pltpu.VMEM((nb, heads, width, blk), BF),
            pltpu.VMEM((nb, heads * blk, width), BF),
            pltpu.VMEM((nb, width, blk), F32),
            pltpu.VMEM((nb, blk, width), F32),
            pltpu.VMEM((nb, blk, width), F32),
            pltpu.VMEM((nb, 8, blk), F32),
            pltpu.VMEM((blk, heads * blk), BF),
            pltpu.VMEM((blk, heads * blk), BF),
            pltpu.VMEM((blk, heads * blk), BF),
            pltpu.VMEM((blk, heads * blk), BF),
            pltpu.SMEM((nb,), jnp.int32),
        ],
        compiler_params=pltpu.CompilerParams(vmem_limit_bytes=36 << 20),
        cost_estimate=pl.CostEstimate(
            flops=heads * 9000000000, bytes_accessed=6 << 20, transcendentals=heads << 21
        ),
        name="attention_back",
    )(q[None], block_of, length, qkv, grad_out, out, lse, *tables)


def gelu_both(u):
    scale = math.sqrt(2.0 / math.pi)
    inside = jnp.tanh(scale * (u + 0.044715 * u * u * u))
    value = 0.5 * u * (1.0 + inside)
    slope = 0.5 * (1.0 + inside) + 0.5 * u * (1.0 - inside * inside) * scale * (
        1.0 + 3.0 * 0.044715 * u * u
    )
    return value, slope


def bundle_up(q, w_qkv, w_attn, gain_rows, part):
    shard, dim = w_attn.shape
    pairs = part // PAIR

    def body(q_ref, qkv_ref, attn_ref, gain_ref, out_ref):
        at = q_ref[0] * part
        for p in range(pairs):
            for t in range(3):
                to = (3 * p + t) * PAIR
                out_ref[:shard, to : to + PAIR] = qkv_ref[
                    :, pl.ds(pl.multiple_of(t * dim + at + p * PAIR, PAIR), PAIR)
                ]
        out_ref[:shard, 3 * part :] = attn_ref[:, pl.ds(pl.multiple_of(at, part), part)]
        out_ref[shard:, :] = jnp.zeros((EXTRA, dim), BF)
        out_ref[shard:, : gain_ref.shape[1]] = gain_ref[...]

    return pl.pallas_call(
        body,
        in_specs=[SM, VM, VM, VM],
        out_specs=VM,
        out_shape=jax.ShapeDtypeStruct((shard + EXTRA, dim), BF),
        compiler_params=pltpu.CompilerParams(vmem_limit_bytes=8 << 20),
        name="bundle_up",
    )(q[None], w_qkv, w_attn, gain_rows)


def up_half(c, w_up, n):
    shard, ff = w_up.shape
    half = ff // n // 2
    if half % 128:
        return lax.dynamic_index_in_dim(
            w_up.reshape(shard, n, 2, half), c, 2, keepdims=False
        ).reshape(shard, n * half)

    def body(c_ref, from_ref, to_ref):
        for core in range(2):

            @pl.when(c_ref[0] == core)
            def _(core=core):
                for s in range(n):
                    at = (2 * s + core) * half
                    to_ref[:, s * half : (s + 1) * half] = from_ref[:, at : at + half]

    return pl.pallas_call(
        body,
        in_specs=[SM, VM],
        out_specs=VM,
        out_shape=jax.ShapeDtypeStruct((shard, n * half), w_up.dtype),
        compiler_params=pltpu.CompilerParams(vmem_limit_bytes=8 << 20),
        cost_estimate=SMALL,
        name="up_half",
    )(c[None], w_up)


def attention_end(q, att, from_core, from_x, attn_w, hidden, gains, blk):
    rows, dim = hidden.shape
    pairs = len(att)
    part = pairs * PAIR
    steps = rows // blk

    def body(q_ref, *refs):
        own_refs = refs[:pairs]
        (
            one_ref, two_ref, three_ref, weight_ref, hidden_ref, gain_ref, att_ref, branch_ref, middle_ref, normed_ref,
        ) = refs[pairs:]
        for p in range(pairs):
            senders = (own_refs[p][...], one_ref[p], two_ref[p], three_ref[p])
            for g, block in enumerate(senders):
                at = lax.bitwise_xor(q_ref[0], g) * part + p * PAIR
                att_ref[:, pl.ds(pl.multiple_of(at, PAIR), PAIR)] = block
        branch = mm(att_ref[...], weight_ref[...])
        branch_ref[...] = branch
        middle = hidden_ref[...].astype(F32) + normalize(branch)[0] * gain_ref[1:2, :].astype(F32)
        middle_ref[...] = middle
        normed_ref[...] = (normalize(middle)[0] * gain_ref[2:3, :].astype(F32)).astype(BF)

    row = pl.BlockSpec((blk, dim), lambda i: (i, 0))
    first = pl.BlockSpec((pairs, blk, PAIR), lambda i: (0, i, 0))
    second = pl.BlockSpec((pairs, blk, PAIR), lambda i: (0, steps + i, 0))
    return pl.pallas_call(
        body,
        grid=(steps,),
        in_specs=[SM]
        + [pl.BlockSpec((blk, PAIR), lambda i: (i, 0))] * pairs
        + [
            first,
            first,
            second,
            pl.BlockSpec(attn_w.shape, lambda i: (0, 0)),
            row,
            pl.BlockSpec(gains.shape, lambda i: (0, 0)),
        ],
        out_specs=[row] * 4,
        out_shape=[
            jax.ShapeDtypeStruct((rows, dim), BF),
            jax.ShapeDtypeStruct((rows, dim), F32),
            jax.ShapeDtypeStruct((rows, dim), F32),
            jax.ShapeDtypeStruct((rows, dim), BF),
        ],
        compiler_params=pltpu.CompilerParams(vmem_limit_bytes=24 << 20),
        cost_estimate=SMALL,
        name="attention_end",
    )(q[None], *att, from_core, from_x, from_core, attn_w, hidden, gains)


def lifted_back(grad_lowered, down_w, slope):
    rows, dim = grad_lowered.shape
    wide = down_w.shape[0]
    step = 512

    def body(grad_ref, weight_ref, slope_ref, out_ref):
        out_ref[...] = (
            mm_nt(grad_ref[...], weight_ref[...]) * slope_ref[...].astype(F32)
        ).astype(BF)

    return pl.pallas_call(
        body,
        grid=(wide // step,),
        in_specs=[
            pl.BlockSpec((rows, dim), lambda i: (0, 0)),
            pl.BlockSpec((step, dim), lambda i: (i, 0)),
            pl.BlockSpec((rows, step), lambda i: (0, i)),
        ],
        out_specs=pl.BlockSpec((rows, step), lambda i: (0, i)),
        out_shape=jax.ShapeDtypeStruct((rows, wide), BF),
        compiler_params=pltpu.CompilerParams(vmem_limit_bytes=32 << 20),
        cost_estimate=SMALL,
        name="lifted_back",
    )(grad_lowered, down_w, slope)


def upstream_of(base_ref, length_ref, cotangent_ref, blk):
    pos = base_ref[pl.program_id(0)] * blk + lax.broadcasted_iota(jnp.int32, (blk, 1), 0)
    return cotangent_ref[...].astype(F32) * jnp.where(pos < length_ref[0], 1.0, 0.0)


def column_sums(value):
    return jnp.sum(value, axis=0, keepdims=True)


def top(bases, length, own, came, middle, cotangent, gains, blk):
    rows, dim = middle.shape

    def body(base_ref, length_ref, own_ref, came_ref, middle_ref, cot_ref, gain_ref, result_ref, grad_ref, sum_ref):
        gain = gain_ref[3:4, :].astype(F32)
        unit, scale = normalize(own_ref[...] + came_ref[...])
        result_ref[...] = (middle_ref[...] + unit * gain).astype(BF)
        upstream = upstream_of(base_ref, length_ref, cot_ref, blk)
        grad_ref[...] = norm_back(unit, scale, gain, upstream).astype(BF)

        @pl.when(pl.program_id(0) == 0)
        def _():
            sum_ref[...] = jnp.zeros_like(sum_ref)

        sum_ref[0:1, :] += column_sums(upstream * unit)

    row = pl.BlockSpec((blk, dim), lambda i: (i, 0))
    return pl.pallas_call(
        body,
        grid=(rows // blk,),
        in_specs=[SM, SM, row, row, row, row, pl.BlockSpec(gains.shape, lambda i: (0, 0))],
        out_specs=[row, row, pl.BlockSpec((8, dim), lambda i: (0, 0))],
        out_shape=[
            jax.ShapeDtypeStruct((rows, dim), BF),
            jax.ShapeDtypeStruct((rows, dim), BF),
            jax.ShapeDtypeStruct((8, dim), F32),
        ],
        compiler_params=pltpu.CompilerParams(vmem_limit_bytes=24 << 20),
        cost_estimate=pl.CostEstimate(flops=20 << 20, bytes_accessed=9 << 20, transcendentals=0),
        name="top",
    )(bases, length, own, came, middle, cotangent, gains)


def middle_back(q, bases, length, own, came, middle, branch, cotangent, gains, attn_w, last_sum, blk):
    rows, dim = middle.shape
    part = dim // 4
    pairs = part // PAIR
    steps = rows // blk

    def body(
        q_ref, base_ref, length_ref, own_ref, came_ref, middle_ref, branch_ref, cot_ref, gain_ref, weight_ref,
        last_ref, middle_out, branch_out, pieces_out, sums_out, attended, sums,
    ):
        i = pl.program_id(0)
        incoming = own_ref[...] + came_ref[...]
        unit, scale = normalize(middle_ref[...])
        grad_middle = upstream_of(base_ref, length_ref, cot_ref, blk) + norm_back(
            unit, scale, gain_ref[2:3, :].astype(F32), incoming
        )
        middle_out[...] = grad_middle
        sum2 = column_sums(incoming * unit)
        unit, scale = normalize(branch_ref[...])
        sum1 = column_sums(grad_middle * unit)
        grad_branch = norm_back(unit, scale, gain_ref[1:2, :].astype(F32), grad_middle).astype(BF)
        branch_out[...] = grad_branch
        attended[...] = mm_nt(grad_branch, weight_ref[...]).astype(BF)
        for g in range(4):
            at = lax.bitwise_xor(q_ref[0], g) * part
            for p in range(pairs):
                pieces_out[p, g] = attended[:, pl.ds(pl.multiple_of(at + p * PAIR, PAIR), PAIR)]

        @pl.when(i == 0)
        def _():
            sums[...] = jnp.zeros_like(sums)

        sums[0:1, :] += sum1
        sums[1:2, :] += sum2

        @pl.when(i == steps - 1)
        def _():
            sums[2:3, :] = last_ref[0:1, :]
            sums_out[...] = sums[...].astype(BF)

    row = pl.BlockSpec((blk, dim), lambda i: (i, 0))

    def whole(array):
        return pl.BlockSpec(array.shape, lambda i: (0, 0))

    return pl.pallas_call(
        body,
        grid=(steps,),
        in_specs=[SM, SM, SM, row, row, row, row, row, whole(gains), whole(attn_w), whole(last_sum)],
        out_specs=[
            row,
            row,
            pl.BlockSpec((pairs, 4, blk, PAIR), lambda i: (0, 0, i, 0)),
            pl.BlockSpec((EXTRA, dim), lambda i: (0, 0)),
        ],
        out_shape=[
            jax.ShapeDtypeStruct((rows, dim), F32),
            jax.ShapeDtypeStruct((rows, dim), BF),
            jax.ShapeDtypeStruct((pairs, 4, rows, PAIR), BF),
            jax.ShapeDtypeStruct((EXTRA, dim), BF),
        ],
        scratch_shapes=[pltpu.VMEM((blk, dim), BF), pltpu.VMEM((EXTRA, dim), F32)],
        compiler_params=pltpu.CompilerParams(vmem_limit_bytes=32 << 20),
        cost_estimate=pl.CostEstimate(
            flops=2 * rows * dim * dim, bytes_accessed=16 << 20, transcendentals=0
        ),
        name="middle_back",
    )(q[None], bases, length, own, came, middle, branch, cotangent, gains, attn_w, last_sum)


def bottom(own, from_core, from_x, hidden, grad_middle, gains, blk):
    rows, dim = hidden.shape

    def body(own_ref, core_ref, x_ref, hidden_ref, middle_ref, gain_ref, out_ref):
        incoming = own_ref[...] + core_ref[...].astype(F32) + x_ref[...].astype(F32)
        unit, scale = normalize(hidden_ref[...].astype(F32))
        out_ref[...] = middle_ref[...] + norm_back(
            unit, scale, gain_ref[0:1, :].astype(F32), incoming
        )

    row = pl.BlockSpec((blk, dim), lambda i: (i, 0))
    return pl.pallas_call(
        body,
        grid=(rows // blk,),
        in_specs=[row] * 5 + [pl.BlockSpec(gains.shape, lambda i: (0, 0))],
        out_specs=row,
        out_shape=jax.ShapeDtypeStruct((rows, dim), F32),
        compiler_params=pltpu.CompilerParams(vmem_limit_bytes=24 << 20),
        cost_estimate=pl.CostEstimate(flops=20 << 20, bytes_accessed=9 << 20, transcendentals=0),
        name="bottom",
    )(own, from_core, from_x, hidden, grad_middle, gains)


def up_end(c, mine, peer, shard, n, ff_half):
    wide = n * ff_half
    if ff_half % 128:
        first, second = jnp.where(c == 0, mine, peer), jnp.where(c == 0, peer, mine)
        blocks = [v.reshape(shard, n, ff_half) for v in (first, second)]
        return jnp.stack(blocks, axis=2).reshape(shard, 2 * wide)

    def body(c_ref, mine_ref, peer_ref, up_ref):
        def put(first, second):
            for s in range(n):
                at = slice(s * ff_half, (s + 1) * ff_half)
                up_ref[:, 2 * s * ff_half : (2 * s + 1) * ff_half] = first[:, at]
                up_ref[:, (2 * s + 1) * ff_half : (2 * s + 2) * ff_half] = second[:, at]

        @pl.when(c_ref[0] == 0)
        def _():
            put(mine_ref, peer_ref)

        @pl.when(c_ref[0] == 1)
        def _():
            put(peer_ref, mine_ref)

    return pl.pallas_call(
        body,
        in_specs=[SM, VM, VM],
        out_specs=VM,
        out_shape=jax.ShapeDtypeStruct((shard, 2 * wide), F32),
        compiler_params=pltpu.CompilerParams(vmem_limit_bytes=16 << 20),
        cost_estimate=pl.CostEstimate(flops=1 << 20, bytes_accessed=6 << 20, transcendentals=0),
        name="up_end",
    )(c[None], mine, peer)


def down_end(q, quarters):
    rows, dim = quarters.shape[1:]

    def body(q_ref, quarters_ref, down_ref):
        for b in range(4):
            at = ((b % 2) * 2 + b // 2) * rows
            down_ref[at : at + rows, :] = quarters_ref[lax.bitwise_xor(q_ref[0], b)].astype(F32)

    return pl.pallas_call(
        body,
        in_specs=[SM, VM],
        out_specs=VM,
        out_shape=jax.ShapeDtypeStruct((4 * rows, dim), F32),
        compiler_params=pltpu.CompilerParams(vmem_limit_bytes=16 << 20),
        cost_estimate=SMALL,
        name="down_end",
    )(q[None], quarters)


def last_end(q, quarters, w_qkv, own_gains, late, part):
    shard, wide = w_qkv.shape
    pairs = part // PAIR
    dim = wide // 3

    def body(q_ref, quarters_ref, weight_ref, gain_ref, late_ref, out_ref, attn_ref, gains_ref):
        total = jnp.zeros((shard, PAIR), F32)
        for b in range(4):
            block = quarters_ref[lax.bitwise_xor(q_ref[0], b)][:shard].astype(F32)
            for p in range(pairs):
                for t in range(3):
                    at = t * dim + b * part + p * PAIR
                    value = block[:, (3 * p + t) * PAIR : (3 * p + t + 1) * PAIR]
                    out_ref[:, at : at + PAIR] = value
                    total = total + value * weight_ref[:, at : at + PAIR].astype(F32)
            attn_ref[:, b * part : (b + 1) * part] = block[:, 3 * part :]
        first = jnp.sum(total, axis=1, keepdims=True) / gain_ref[:, 0:1].astype(F32)
        lane = lax.broadcasted_iota(jnp.int32, (shard, 4), 1)
        gains_ref[...] = jnp.where(lane == 0, first, late_ref[...])

    return pl.pallas_call(
        body,
        in_specs=[SM] + [VM] * 4,
        out_specs=[VM] * 3,
        out_shape=[
            jax.ShapeDtypeStruct((shard, wide), F32),
            jax.ShapeDtypeStruct((shard, dim), F32),
            jax.ShapeDtypeStruct((shard, 4), F32),
        ],
        compiler_params=pltpu.CompilerParams(vmem_limit_bytes=16 << 20),
        cost_estimate=SMALL,
        name="last_end",
    )(q[None], quarters, w_qkv, own_gains, late)


def per_device(n, hidden_in, cotangent, lengths, block_of, w_qkv, w_attn, w_up, w_down, norm_gains):
    own_rows, dim = hidden_in.shape[1:]
    rows = 4 * own_rows
    blk = own_rows // 2
    ff = w_up.shape[1]
    shard = dim // n
    ff_half = ff // n // 2
    part = dim // 4
    pairs = part // PAIR
    q = lax.axis_index("ctx")
    c = lax.rem(q, 2)

    gain_rows = jnp.pad(norm_gains.T, ((0, EXTRA - 4), (0, 0)))
    bundle = bundle_up(q, w_qkv, w_attn, gain_rows, part)

    def store_bundle(target, owner, block):
        to_qkv, to_attn, to_gains = target
        return (
            lax.dynamic_update_slice(to_qkv, block[:shard, : 3 * part], (owner * shard, 0)),
            lax.dynamic_update_slice(to_attn, block[:shard, 3 * part :], (owner * shard, 0)),
            lax.dynamic_update_slice(to_gains, block[shard:, :shard], (0, owner * shard)),
        )

    def store_rows(target, owner, block):
        return lax.dynamic_update_slice(target, block, (owner * block.shape[0], 0))

    lead = Gather(
        bundle,
        n,
        False,
        store_bundle,
        (blank((dim, 3 * part), BF), blank((dim, part), BF), blank((EXTRA, dim), BF)),
    )
    up_own = up_half(c, w_up, n)
    down_own = lax.dynamic_slice_in_dim(w_down, c * ff_half, ff_half, 0)
    bases = lax.dynamic_slice_in_dim(block_of, q, 1, 0)[0]
    tables = rotary_tables(blk, 8)
    hidden_b = hidden_in[0]
    cuts = (0, own_rows // 4, 5 * own_rows // 8, own_rows)

    def put_hidden(target, group, k, value):
        return lax.dynamic_update_slice(target, value, (group * own_rows + (cuts[k] if k else 0), 0))

    hidden_all = lax.dynamic_update_slice(blank((rows, dim), BF), hidden_b, (0, 0))
    mine = [hidden_b[cuts[k] : cuts[k + 1]] for k in range(3)]
    came, from_x, hidden_c, mine = tie(
        lead.send(), swap(mine[0], 2), swap(hidden_b, 1), mine
    )
    for k in range(3):
        lead.land(came)
        hidden_all = put_hidden(hidden_all, 2, k, from_x)
        if k == 0:
            hidden_all = put_hidden(hidden_all, 1, 0, hidden_c)
        came, next_x, from_d, mine, up_own, down_own = tie(
            lead.send(),
            swap(mine[k + 1], 2) if k < 2 else [],
            swap(from_x, 1),
            mine,
            up_own,
            down_own,
        )
        hidden_all = put_hidden(hidden_all, 3, k, from_d)
        from_x = next_x
    lead.land(came)
    qkv_w, attn_q, gains = lead.rest()

    up = Gather(up_own, n, False, store_rows, blank((dim, n * ff_half), BF))
    down = Gather(down_own, n, True, store_rows, blank((n * ff_half, dim), BF))
    normed, *qkv = project(q, block_of, hidden_all, qkv_w, gains, tables, blk)
    att, lse = attention(q, block_of, lengths, qkv, blk)
    came_up, came_down, attn_x, att, attn_q = tie(
        up.send(), down.send(), swap(attn_q, 2), att, attn_q
    )
    up.land(came_up)
    down.land(came_down)

    half_rows = rows // 2
    from_x = swap(jnp.stack([a[half_rows:] for a in att]), 2)
    from_core = swap(
        jnp.stack(
            [
                jnp.concatenate([a[own_rows:half_rows], from_x[p, own_rows:]], axis=0)
                for p, a in enumerate(att)
            ]
        ),
        1,
    )
    came_up, came_down, from_x, from_core, att, attn_x, attn_q = tie(
        up.send(), down.send(), from_x, from_core, att, attn_x, attn_q
    )
    up.land(came_up)
    down.land(came_down)
    attn_c = swap(jnp.stack([attn_q, attn_x]), 1)
    attn_parts = jnp.stack([attn_q, attn_c[0], attn_x, attn_c[1]])
    attn_w = jnp.concatenate(
        [
            lax.dynamic_index_in_dim(attn_parts, lax.bitwise_xor(q, b), 0, keepdims=False)
            for b in range(4)
        ],
        axis=1,
    )

    attended, branch, middle, normed_mid = attention_end(
        q, [a[:own_rows] for a in att], from_core, from_x, attn_w, hidden_b, gains, blk
    )
    came_up, came_down, normed_mid = tie(up.send(), down.send(), normed_mid)
    up.land(came_up)
    down.land(came_down)

    came_up, came_down, normed_mid_c, normed_mid = tie(
        up.send(), down.send(), swap(normed_mid, 1), normed_mid
    )
    up.land(came_up)
    down.land(came_down)
    normed_mid2 = jnp.concatenate([normed_mid, normed_mid_c], axis=0)
    up_w, down_w = up.rest(), down.rest()
    lifted = mm(normed_mid2, up_w)
    activated, slope = [v.astype(BF) for v in gelu_both(lifted)]
    lowered_c = swap(mm(activated[own_rows:], down_w), 1)
    lowered = mm(activated[:own_rows], down_w)
    result, grad_lowered, last_sum = top(
        bases, lengths, lowered, lowered_c, middle, cotangent[0], gains, blk
    )

    grad_lowered2 = jnp.concatenate([grad_lowered, swap(grad_lowered, 1)], axis=0)
    ff_part = ff_half // 2
    x = lax.div(q, 2)
    place = ring_place(lax.axis_index("fsdp"), n)
    owners = jnp.split(jnp.stack([ring_owner(place + offset, n) for offset in spots(n)]), 4)
    down_g = mm_tn(activated, grad_lowered2).astype(BF).reshape(n, 2, ff_part, dim)
    piece = picked(down_g, owners[0], 1 - x)
    piece, down_g, grad_lowered2 = tie(piece, down_g, grad_lowered2)

    from_x = []
    grad_lifted = lifted_back(grad_lowered2, down_w, slope)
    came_x, grad_lifted, piece, down_g = tie(
        swap(piece, 2), grad_lifted, picked(down_g, owners[1], 1 - x), down_g
    )
    from_x.append(came_x)

    down_ring = Scatter(down_pick(down_g, x, from_x, n), n, False)
    up_g = mm_tn(normed_mid2, grad_lifted).astype(BF)
    came_x, came_down, up_g, grad_lifted = tie(swap(piece, 2), down_ring.send(), up_g, grad_lifted)
    from_x.append(came_x)
    down_ring.land(came_down)

    up_ring = Scatter(rows_of(up_g, shard), n, True)
    piece = picked(down_g, owners[2], 1 - x)
    other_half = mm_nt(grad_lifted[own_rows:], up_w)
    came_up, other_half, grad_lifted, piece = tie(up_ring.send(), other_half, grad_lifted, piece)
    up_ring.land(came_up)
    grad_normed_mid_c, grad_normed_mid, piece = tie(
        swap(other_half, 1), mm_nt(grad_lifted[:own_rows], up_w), piece
    )

    grad_middle, grad_branch, pieces, sums = middle_back(
        q, bases, lengths, grad_normed_mid, grad_normed_mid_c, middle, branch, cotangent[0], gains,
        attn_w, last_sum, blk,
    )
    came_x, came_up, grad_branch, pieces = tie(swap(piece, 2), up_ring.send(), grad_branch, pieces)
    from_x.append(came_x)
    up_ring.land(came_up)

    pieces = pieces.reshape(pairs, rows, PAIR)
    attn_g = mm_tn(attended, grad_branch).astype(BF)
    half_cols = dim // 2
    attn_cols = jnp.concatenate(
        [attn_g[:, b * part : (b + 1) * part] for b in (0, 2, 1, 3)], axis=1
    )
    attn_own = lax.dynamic_slice_in_dim(attn_cols, c * half_cols, half_cols, 1)
    attn_other = lax.dynamic_slice_in_dim(attn_cols, (1 - c) * half_cols, half_cols, 1)
    went_x, came_up, attn_own, attn_other, pieces, piece = tie(
        swap(pieces[:, half_rows:], 2),
        up_ring.send(),
        attn_own,
        attn_other,
        pieces,
        picked(down_g, owners[3], 1 - x),
    )
    up_ring.land(came_up)

    went_core, attn_came, went_x, pieces, attn_own = tie(
        swap(jnp.concatenate([pieces[:, own_rows:half_rows], went_x[:, own_rows:]], axis=1), 1),
        swap(attn_other, 1),
        went_x,
        pieces,
        attn_own,
    )
    grad_out = jnp.concatenate(
        [pieces[:, :own_rows], went_core[:, :own_rows], went_x[:, :own_rows], went_core[:, own_rows:]],
        axis=1,
    )
    attn_half = (attn_own.astype(F32) + attn_came.astype(F32)).astype(BF)

    def back(p):
        return attention_back(
            q, block_of, lengths, qkv[p], grad_out[p], att[p], lse[p], tables, blk
        )

    mixed = [back(0)]
    came_x, came_up, mixed, grad_out, attn_half = tie(
        swap(piece, 2), up_ring.send(), mixed, grad_out, attn_half
    )
    from_x.append(came_x)
    up_ring.land(came_up)

    attn_x_own = lax.dynamic_slice_in_dim(attn_half, x * part, part, 1)
    attn_x_other = lax.dynamic_slice_in_dim(attn_half, (1 - x) * part, part, 1)
    mixed.append(back(1))
    attn_came, came_down, mixed, attn_x_own, up_sum = tie(
        swap(attn_x_other, 2), down_ring.send(), mixed, attn_x_own, up_ring.rest()
    )
    attn_g = (attn_x_own.astype(F32) + attn_came.astype(F32)).astype(BF)
    down_ring.land(came_down)

    def normed_back(g):
        at = slice(g * own_rows, (g + 1) * own_rows)
        wide = 3 * PAIR
        return sum(mm_nt(mixed[p][at], qkv_w[:, p * wide : (p + 1) * wide]) for p in range(pairs))

    qkv_g = jnp.concatenate([mm_tn(normed, m).astype(BF) for m in mixed], axis=1)
    to_core = jnp.concatenate([normed_back(1).astype(BF), normed_back(3).astype(BF)], axis=0)
    came_down, mixed, qkv_g, to_core, attn_g, up_sum = tie(
        down_ring.send(), mixed, qkv_g, to_core, attn_g, up_sum
    )
    down_ring.land(came_down)

    last_ring = Scatter(last_pick(qkv_g, attn_g, sums, shard), n, False)
    came_last, came_down, came_core, up_x, own_part, for_x, up_sum = tie(
        last_ring.send(),
        down_ring.send(),
        swap(to_core, 1),
        swap(up_sum, 2),
        normed_back(0),
        normed_back(2),
        up_sum,
    )
    last_ring.land(came_last)
    down_ring.land(came_down)
    down_sum = down_ring.rest()
    for_x = (for_x + came_core[own_rows:].astype(F32)).astype(BF)
    up_sum = up_sum.astype(F32) + up_x.astype(F32)

    quarter = own_rows // 2
    came_last, from_x0, up_c, up_sum, down_sum, for_x = tie(
        last_ring.send(), swap(for_x[:quarter], 2), swap(up_sum, 1), up_sum, down_sum, for_x
    )
    last_ring.land(came_last)
    up_out = up_end(c, up_sum, up_c, shard, n, ff_half)
    came_last, from_x1, up_out, down_sum = tie(
        last_ring.send(), swap(for_x[quarter:], 2), up_out, down_sum
    )
    last_ring.land(came_last)
    input_grad = bottom(
        own_part, came_core[:own_rows], jnp.concatenate([from_x0, from_x1], axis=0), hidden_b, grad_middle, gains, blk
    )

    came_last, down_x, input_grad, down_sum = tie(
        last_ring.send(), swap(down_sum, 2), input_grad, down_sum
    )
    last_ring.land(came_last)
    last = last_ring.rest()

    down_pair = jnp.stack([down_sum, down_x])
    last_x, down_c, last, down_pair = tie(swap(last, 2), swap(down_pair, 1), last, down_pair)
    down_out = down_end(q, jnp.stack([down_pair[0], down_c[0], down_pair[1], down_c[1]]))
    last_pair = jnp.stack([last, last_x])
    last_c, down_out, last_pair = tie(swap(last_pair, 1), down_out, last_pair)
    last_all = jnp.stack([last_pair[0], last_c[0], last_pair[1], last_c[1]])
    me = lax.axis_index("fsdp")
    late = lax.dynamic_slice(last_all, (0, shard, me * shard), (4, 4, shard)).astype(F32)
    late = (
        lax.dynamic_index_in_dim(late, q, 0, keepdims=False)
        + lax.dynamic_index_in_dim(late, lax.bitwise_xor(q, 1), 0, keepdims=False)
    ) + (
        lax.dynamic_index_in_dim(late, lax.bitwise_xor(q, 2), 0, keepdims=False)
        + lax.dynamic_index_in_dim(late, lax.bitwise_xor(q, 3), 0, keepdims=False)
    )
    late = jnp.roll(late, 1, axis=0).T
    qkv_out, attn_out, gains_out = last_end(q, last_all, w_qkv, norm_gains, late, part)
    return (
        result[None],
        input_grad[None],
        qkv_out,
        attn_out,
        up_out,
        down_out,
        gains_out,
    )


def solution(mesh):
    n = mesh.shape["fsdp"]

    def step(*args):
        return per_device(n, *args)

    rows = P("fsdp", "ctx", None)
    weight = P("fsdp", None)
    return jax.shard_map(
        step,
        mesh=mesh,
        in_specs=(rows, rows, P("fsdp"), P()) + (weight,) * 5,
        out_specs=(rows, rows) + (weight,) * 5,
        check_vma=False,
    )
```

```python
import math

import jax
import jax.numpy as jnp
import numpy as np
from jax import lax
from jax.experimental import pallas as pl
from jax.experimental.pallas import tpu as pltpu
from jax.sharding import PartitionSpec as P

HEAD_DIM = 64
PAIR = 2 * HEAD_DIM
EXTRA = 16
BF = jnp.bfloat16
F32 = jnp.float32
NEG = -1e30
EPS = 1e-05
VM = pl.BlockSpec(memory_space=pltpu.VMEM)
SM = pl.BlockSpec(memory_space=pltpu.SMEM)
SMALL = pl.CostEstimate(flops=1 << 10, bytes_accessed=1 << 10, transcendentals=0)


def mm(left, right):
    return jnp.dot(left, right, preferred_element_type=F32)


def mm_tn(left, right):
    return lax.dot_general(left, right, (((0,), (0,)), ((), ())), preferred_element_type=F32)


def mm_nt(left, right):
    return lax.dot_general(left, right, (((1,), (1,)), ((), ())), preferred_element_type=F32)


def swap(value, bit):
    return lax.ppermute(value, "ctx", [(i, i ^ bit) for i in range(4)])


def blank(shape, dtype):
    return pl.pallas_call(
        lambda out_ref: None,
        out_specs=pl.BlockSpec(memory_space=pl.ANY),
        out_shape=jax.ShapeDtypeStruct(shape, dtype),
        name="blank",
    )()


def ring_pairs(n):
    order = list(range(0, n, 2)) + list(range(n - 1, 0, -2))
    ahead = [(order[i], order[(i + 1) % n]) for i in range(n)]
    return ahead, [(b, a) for a, b in ahead]


def ring_owner(place, n):
    place = lax.rem(place + 2 * n, n)
    return jnp.where(place < n // 2, 2 * place, 2 * (n - place) - 1)


def ring_place(me, n):
    return jnp.where(lax.rem(me, 2) == 0, lax.div(me, 2), n - 1 - lax.div(me, 2))


HBM = pl.BlockSpec(memory_space=pltpu.HBM)


def tie(*trees):
    return lax.optimization_barrier(trees)


class Gather:
    def __init__(self, block, n, flip, store, target):
        self.ahead, self.back = ring_pairs(n)
        self.sign = -1
        if flip:
            self.ahead, self.back, self.sign = self.back, self.ahead, 1
        me = lax.axis_index("fsdp")
        self.n, self.place, self.count = n, ring_place(me, n), 0
        self.store, self.blocks = store, [block, block]
        self.target = store(target, me, block)

    def more(self):
        return self.count < self.n // 2

    def send(self):
        self.count += 1
        sent = [lax.ppermute(self.blocks[0], "fsdp", self.ahead)]
        if self.count <= (self.n - 1) // 2:
            sent.append(lax.ppermute(self.blocks[1], "fsdp", self.back))
        return sent

    def land(self, came):
        self.blocks = came
        for block, sign in zip(came, (self.sign, -self.sign)):
            owner = ring_owner(self.place + sign * self.count, self.n)
            self.target = self.store(self.target, owner, block)

    def rest(self):
        while self.more():
            self.land(tie(self.send())[0])
        return self.target


class Scatter:
    def __init__(self, pick, n, flip):
        self.ahead, self.back = ring_pairs(n)
        self.sign = 1
        if flip:
            self.ahead, self.back, self.sign = self.back, self.ahead, -1
        self.place = ring_place(lax.axis_index("fsdp"), n)
        self.n, self.pick, self.count = n, pick, 0
        self.blocks = [self.at(self.sign * (n // 2)), self.at(-self.sign * ((n - 1) // 2))]

    def at(self, offset, *blocks):
        return self.pick(offset, ring_owner(self.place + offset, self.n), *blocks)

    def more(self):
        return self.count < self.n // 2

    def send(self):
        self.count += 1
        sent = [lax.ppermute(self.blocks[0], "fsdp", self.ahead)]
        if self.count <= (self.n - 1) // 2:
            sent.append(lax.ppermute(self.blocks[1], "fsdp", self.back))
        return sent

    def land(self, came):
        one, two = self.n // 2 - self.count, (self.n - 1) // 2 - self.count
        if one > 0:
            self.blocks[0] = self.at(self.sign * one, came[0])
            if two > 0:
                self.blocks[1] = self.at(-self.sign * two, came[1])
            elif len(came) > 1:
                self.blocks[1] = came[1]
        else:
            self.total = self.at(0, came[0], came[1] if len(came) > 1 else self.blocks[1])

    def rest(self):
        while self.more():
            self.land(tie(self.send())[0])
        return self.total


def rows_of(array, size):
    def pick(offset, owner, *blocks):
        value = lax.dynamic_slice_in_dim(array, owner * size, size, 0)
        if not blocks:
            return value
        value = value.astype(F32)
        for block in blocks:
            value = value + block.astype(F32)
        return value.astype(BF)

    return pick


class MergedGather:
    def __init__(self, block, n, up_w, down_w):
        self.ahead, self.back = ring_pairs(n)
        me = lax.axis_index("fsdp")
        self.n, self.place, self.count = n, ring_place(me, n), 0
        self.half = block.shape[0] // 2
        self.blocks = [block, block]
        self.targets = [up_w, down_w]
        self.store([me, me], [block, block], [0])

    def store(self, owners, blocks, which):
        shard = self.half // 2
        dim = blocks[0].shape[1]

        def body(owners_ref, *refs):
            block_refs, (up_ref, down_ref) = refs[: len(blocks)], refs[len(blocks) + 2 :]

            def put(up_from, down_from):
                up_ref[:, :dim] = up_from[:shard, :]
                up_ref[:, dim:] = up_from[shard : 2 * shard, :]
                down_ref[...] = down_from[down_from.shape[0] - 2 * shard :, :]

            if len(which) == 1:
                put(*block_refs)
            else:
                for k in which:

                    @pl.when(pl.program_id(0) == k)
                    def _(k=k):
                        put(block_refs[k], block_refs[k])

        def whole(array):
            return pl.BlockSpec(array.shape, lambda i, o: (0, 0))

        self.targets = pl.pallas_call(
            body,
            grid_spec=pltpu.PrefetchScalarGridSpec(
                num_scalar_prefetch=1,
                grid=(len(which),),
                in_specs=[whole(b) for b in blocks] + [HBM, HBM],
                out_specs=[
                    pl.BlockSpec((shard, 2 * dim), lambda i, o: (o[i], 0)),
                    pl.BlockSpec((2 * shard, dim), lambda i, o: (o[i], 0)),
                ],
            ),
            out_shape=[pltpu.HBM(t.shape, t.dtype) for t in self.targets],
            input_output_aliases={1 + len(blocks): 0, 2 + len(blocks): 1},
            compiler_params=pltpu.CompilerParams(vmem_limit_bytes=16 << 20),
            cost_estimate=SMALL,
            name="store",
        )(jnp.stack(owners), *blocks, *self.targets)

    def more(self):
        return self.count < self.n // 2

    def send(self):
        self.count += 1
        one, two = self.blocks
        if not self.more():
            one, two = one[: self.half], two[self.half :]
        return [lax.ppermute(one, "fsdp", self.ahead), lax.ppermute(two, "fsdp", self.back)]

    def land(self, came):
        self.blocks = came
        owners = [ring_owner(self.place + sign * self.count, self.n) for sign in (-1, 1)]
        self.store(owners, came, [0, 1] if self.more() else [0])

    def rest(self):
        while self.more():
            self.land(tie(self.send())[0])
        return self.targets


class MergedScatter:
    def __init__(self, up_g, down_g, n):
        self.ahead, self.back = ring_pairs(n)
        self.place = ring_place(lax.axis_index("fsdp"), n)
        self.n, self.count, self.addends = n, 0, (up_g, down_g)
        self.half = 2 * up_g.shape[0] // n
        far = self.pick(n // 2, [])
        self.blocks = [far[: self.half], far[self.half :]]

    def pick(self, offset, adds):
        up_g, down_g = self.addends
        shard, dim = up_g.shape[0] // self.n, down_g.shape[1]
        half = self.half

        def body(owner_ref, up_ref, down_ref, *refs):
            out_ref = refs[-1]

            def put(start, size, value):
                value = value.astype(F32)
                for (first, block), ref in zip(adds, refs[:-1]):
                    if first <= start < first + block.shape[0]:
                        value = value + ref[start - first : start - first + size, :].astype(F32)
                out_ref[start : start + size, :] = value.astype(BF)

            put(0, shard, up_ref[:, :dim])
            put(shard, shard, up_ref[:, dim:])
            put(half, half, down_ref[...])

        return pl.pallas_call(
            body,
            grid_spec=pltpu.PrefetchScalarGridSpec(
                num_scalar_prefetch=1,
                grid=(1,),
                in_specs=[
                    pl.BlockSpec((shard, 2 * dim), lambda i, o: (o[0], 0)),
                    pl.BlockSpec((half, dim), lambda i, o: (o[0], 0)),
                ]
                + [pl.BlockSpec(b.shape, lambda i, o: (0, 0)) for _, b in adds],
                out_specs=pl.BlockSpec((2 * half, dim), lambda i, o: (0, 0)),
            ),
            out_shape=jax.ShapeDtypeStruct((2 * half, dim), BF),
            compiler_params=pltpu.CompilerParams(vmem_limit_bytes=16 << 20),
            cost_estimate=SMALL,
            name="merged_pick",
        )(ring_owner(self.place + offset, self.n)[None], up_g, down_g, *[b for _, b in adds])

    def more(self):
        return self.count < self.n // 2

    def send(self):
        self.count += 1
        return [
            lax.ppermute(self.blocks[0], "fsdp", self.ahead),
            lax.ppermute(self.blocks[1], "fsdp", self.back),
        ]

    def land(self, came):
        starts = (0, self.half) if self.count == 1 else (0, 0)
        if self.more():
            left = self.n // 2 - self.count
            self.blocks = [
                self.pick(sign * left, [(start, block)])
                for sign, start, block in zip((1, -1), starts, came)
            ]
        else:
            self.total = self.pick(0, list(zip(starts, came)))

    def rest(self):
        while self.more():
            self.land(tie(self.send())[0])
        return self.total


def last_pick(wide_g, narrow_g, sums, rows):
    wide, narrow = wide_g.shape[1], narrow_g.shape[1]

    def pick(offset, owner, *blocks):
        def body(owner_ref, wide_ref, narrow_ref, sums_ref, *refs):
            out_ref = refs[-1]

            def put(at_rows, at_cols, value):
                value = value.astype(F32)
                for ref in refs[:-1]:
                    value = value + ref[at_rows, at_cols].astype(F32)
                out_ref[at_rows, at_cols] = value.astype(BF)

            upper, lower = slice(0, rows), slice(rows, rows + EXTRA)
            put(upper, slice(0, wide), wide_ref[...])
            put(upper, slice(wide, wide + narrow), narrow_ref[...])
            put(lower, slice(0, wide + narrow), sums_ref[...])

        whole = pl.BlockSpec((rows + EXTRA, wide + narrow), lambda i, o: (0, 0))
        return pl.pallas_call(
            body,
            grid_spec=pltpu.PrefetchScalarGridSpec(
                num_scalar_prefetch=1,
                grid=(1,),
                in_specs=[
                    pl.BlockSpec((rows, wide), lambda i, o: (o[0], 0)),
                    pl.BlockSpec((rows, narrow), lambda i, o: (o[0], 0)),
                    pl.BlockSpec(sums.shape, lambda i, o: (0, 0)),
                ]
                + [whole] * len(blocks),
                out_specs=whole,
            ),
            out_shape=jax.ShapeDtypeStruct((rows + EXTRA, wide + narrow), BF),
            compiler_params=pltpu.CompilerParams(vmem_limit_bytes=8 << 20),
            cost_estimate=SMALL,
            name="last_pick",
        )(owner[None], wide_g, narrow_g, sums, *blocks)

    return pick


def normalize(values):
    average = jnp.mean(values, axis=-1, keepdims=True)
    centered = values - average
    variance = jnp.mean(centered * centered, axis=-1, keepdims=True)
    scale = lax.rsqrt(variance + EPS)
    return centered * scale, scale


def norm_back(unit, scale, gain, incoming):
    weighted = incoming * gain
    return (
        weighted
        - jnp.mean(weighted, axis=-1, keepdims=True)
        - unit * jnp.mean(weighted * unit, axis=-1, keepdims=True)
    ) * scale


def turned(value, cosine, sine_signed, inverse):
    width = value.shape[1]
    lane = lax.broadcasted_iota(jnp.int32, value.shape, 1)
    half = HEAD_DIM // 2
    other = jnp.where(
        lax.rem(lane, HEAD_DIM) < half,
        pltpu.roll(value, width - half, 1),
        pltpu.roll(value, half, 1),
    )
    repeat = width // cosine.shape[1]
    cosine = jnp.concatenate([cosine] * repeat, axis=1)
    sine_signed = jnp.concatenate([sine_signed] * repeat, axis=1)
    if inverse:
        return value * cosine - other * sine_signed
    return value * cosine + other * sine_signed


def block_at(q_ref, block_ref, k):
    return block_ref[lax.bitwise_xor(q_ref[0], lax.div(k, 2)), lax.rem(k, 2)]


def fill_order(order, q_ref, block_ref, count):
    def put(k, carry):
        order[block_at(q_ref, block_ref, k)] = k
        return carry

    lax.fori_loop(0, count, put, 0)


def rotary_tables(blk, count):
    lane = np.arange(PAIR)
    half = HEAD_DIM // 2
    inverse = np.exp(-2.0 * math.log(10000.0) / HEAD_DIM * (lane % half))
    sign = np.where(lane % HEAD_DIM < half, -1.0, 1.0)
    inside = np.arange(blk)[:, None] * inverse[None, :]
    starts = np.arange(count)[:, None] * blk * inverse[None, :]
    return [
        jnp.asarray(v, F32)
        for v in (np.cos(inside), np.sin(inside) * sign, np.cos(starts), np.sin(starts) * sign)
    ]


def tables_at(table_refs, block):
    cos_in, sin_in, cos_at, sin_at = table_refs
    cos_b, sin_b = cos_at[pl.ds(block, 1), :], sin_at[pl.ds(block, 1), :]
    cos_r, sin_r = cos_in[...], sin_in[...]
    return cos_r * cos_b - sin_r * sin_b, sin_r * cos_b + cos_r * sin_b


def project(q, block_of, hidden, weight, gains, tables, blk):
    rows, dim = hidden.shape
    width = weight.shape[1]
    pairs = width // (3 * PAIR)
    step = 2 * blk

    def body(q_ref, block_ref, hidden_ref, weight_ref, gain_ref, *refs):
        table_refs, normed_ref, out_refs = refs[:4], refs[4], refs[5:]
        unit, _ = normalize(hidden_ref[...].astype(F32))
        normed = (unit * gain_ref[0:1, :].astype(F32)).astype(BF)
        normed_ref[...] = normed
        mixed = mm(normed, weight_ref[...])
        halves = [
            tables_at(table_refs, block_at(q_ref, block_ref, 2 * pl.program_id(0) + k))
            for k in range(2)
        ]
        cos_part, sin_part = [jnp.concatenate(v, axis=0) for v in zip(*halves)]
        for p, out_ref in enumerate(out_refs):
            at = 3 * PAIR * p
            queries = turned(mixed[:, at : at + PAIR], cos_part, sin_part, False)
            out_ref[:, :PAIR] = (queries * (0.125 * math.log2(math.e))).astype(BF)
            out_ref[:, PAIR : 2 * PAIR] = turned(
                mixed[:, at + PAIR : at + 2 * PAIR], cos_part, sin_part, False
            ).astype(BF)
            out_ref[:, 2 * PAIR :] = mixed[:, at + 2 * PAIR : at + 3 * PAIR].astype(BF)

    def whole(array):
        return pl.BlockSpec(array.shape, lambda i: (0, 0))

    return pl.pallas_call(
        body,
        grid=(rows // step,),
        in_specs=[SM, SM, pl.BlockSpec((step, dim), lambda i: (i, 0)), whole(weight), whole(gains)]
        + [whole(t) for t in tables],
        out_specs=[pl.BlockSpec((step, dim), lambda i: (i, 0))]
        + [pl.BlockSpec((step, 3 * PAIR), lambda i: (i, 0))] * pairs,
        out_shape=[jax.ShapeDtypeStruct((rows, dim), BF)]
        + [jax.ShapeDtypeStruct((rows, 3 * PAIR), BF)] * pairs,
        compiler_params=pltpu.CompilerParams(vmem_limit_bytes=32 << 20),
        cost_estimate=pl.CostEstimate(
            flops=2 * rows * dim * width, bytes_accessed=12 << 20, transcendentals=rows
        ),
        name="project",
    )(q[None], block_of, hidden, weight, gains, *tables)


def folded(value, op):
    rows, cols = value.shape
    return op(value.reshape(rows // 8, 8, cols), axis=0)


def head_columns(target, p, value_t, heads):
    for h in range(heads):
        at = slice(h * HEAD_DIM, (h + 1) * HEAD_DIM)
        if h:
            target[p, h, : h * HEAD_DIM, :] = jnp.zeros((h * HEAD_DIM, value_t.shape[1]), BF)
        target[p, h, at, :] = value_t[at, :]
        rest = (heads - 1 - h) * HEAD_DIM
        if rest:
            target[p, h, (h + 1) * HEAD_DIM :, :] = jnp.zeros((rest, value_t.shape[1]), BF)


def tile_mask(i, j, live, blk):
    key = j * blk + lax.broadcasted_iota(jnp.int32, (blk, blk), 0)
    query = i * blk + lax.broadcasted_iota(jnp.int32, (blk, blk), 1)
    return (key <= query) & (key < live)


def open_tiles(edge, nb):
    return sum(jnp.minimum(i, edge) for i in range(nb))


def next_open(i, j, edge, nb):
    end = j + 1 >= jnp.minimum(i, edge)
    return jnp.minimum(jnp.where(end, i + 1, i), nb - 1), jnp.where(end, 0, j + 1)


def attention(q, block_of, length, qkv, blk):
    rows = qkv[0].shape[0]
    pairs = len(qkv)
    width = pairs * PAIR
    heads = width // HEAD_DIM
    nb = rows // blk

    def body(
        q_ref, block_ref, length_ref, *refs,
    ):
        qkv_refs, out_refs, lse_refs = refs[:pairs], refs[pairs : 2 * pairs], refs[2 * pairs : 3 * pairs]
        (keys, values_t, q_cols, even, odd, even_top, odd_top, total, tops, sums, order_ref) = refs[3 * pairs :]
        fill_order(order_ref, q_ref, block_ref, nb)
        live = length_ref[0]
        edge = lax.div(live, blk)

        def fill(p, carry):
            rows_at = pl.ds(pl.multiple_of(order_ref[p] * blk, blk), blk)
            keys[p] = jnp.concatenate([r[rows_at, PAIR : 2 * PAIR] for r in qkv_refs], axis=1)
            values_t[p] = jnp.transpose(
                jnp.concatenate([r[rows_at, 2 * PAIR :] for r in qkv_refs], axis=1)
            )
            queries = jnp.concatenate([r[rows_at, :PAIR] for r in qkv_refs], axis=1)
            head_columns(q_cols, p, jnp.transpose(queries), heads)
            return carry

        lax.fori_loop(0, nb, fill, 0)

        def ahead(i, j, into, top, masks):
            key_block = keys[j]
            for h in range(heads):
                s = mm(key_block, q_cols[i, h])
                if masks:
                    s = jnp.where(tile_mask(i, j, live, blk), s, NEG)
                into[h] = s
                top[h] = folded(s, jnp.max)

        def work(i, j, scores, top, first):
            for h in range(heads):
                new = jnp.broadcast_to(jnp.max(top[h], axis=0, keepdims=True), (8, blk))
                if not first:
                    old = tops[i, h]
                    new = jnp.maximum(old, new)
                    shrink = jnp.exp2(old - new)
                tops[i, h] = new
                p = jnp.exp2(scores[h] - new[0:1])
                added = folded(p, jnp.sum)
                sums[i, h] = added if first else sums[i, h] * shrink + added
                at = slice(h * HEAD_DIM, (h + 1) * HEAD_DIM)
                product = mm(values_t[j, at, :], p.astype(BF))
                total[i, at, :] = product if first else total[i, at, :] * shrink[0:1] + product

        ahead(0, 0, even, even_top, True)

        def masked_pair(t, carry):
            i0 = 2 * t
            i1 = i0 + 1
            i2 = jnp.minimum(i0 + 2, nb - 1)
            ahead(i1, jnp.minimum(i1, edge), odd, odd_top, True)
            work(i0, jnp.minimum(i0, edge), even, even_top, True)
            ahead(i2, jnp.minimum(i2, edge), even, even_top, True)
            work(i1, jnp.minimum(i1, edge), odd, odd_top, True)
            return carry

        lax.fori_loop(0, nb // 2, masked_pair, 0)

        ahead(1, 0, even, even_top, False)

        def pair(t, place):
            i0, j0 = place
            i1, j1 = next_open(i0, j0, edge, nb)
            ahead(i1, j1, odd, odd_top, False)
            work(i0, j0, even, even_top, False)
            i2, j2 = next_open(i1, j1, edge, nb)
            ahead(i2, j2, even, even_top, False)
            work(i1, j1, odd, odd_top, False)
            return (i2, j2)

        count = open_tiles(edge, nb)
        i_last, j_last = lax.fori_loop(0, lax.div(count, 2), pair, (jnp.int32(1), jnp.int32(0)))

        @pl.when(lax.rem(count, 2) == 1)
        def _():
            work(i_last, j_last, even, even_top, False)

        def drain(p, carry):
            rows_at = pl.ds(pl.multiple_of(order_ref[p] * blk, blk), blk)
            scaled = []
            for h in range(heads):
                sum_h = jnp.sum(sums[p, h], axis=0, keepdims=True)
                lse_refs[h // 2][p, h % 2 : h % 2 + 1, :] = tops[p, h][0:1] + jnp.log2(sum_h)
                scaled.append((total[p, h * HEAD_DIM : (h + 1) * HEAD_DIM, :] * (1.0 / sum_h)).astype(BF))
            both = jnp.transpose(jnp.concatenate(scaled, axis=0))
            for k, ref in enumerate(out_refs):
                ref[rows_at, :] = both[:, k * PAIR : (k + 1) * PAIR]
            return carry

        lax.fori_loop(0, nb, drain, 0)

    vm = pl.BlockSpec(memory_space=pltpu.VMEM)
    sm = pl.BlockSpec(memory_space=pltpu.SMEM)
    result = pl.pallas_call(
        body,
        in_specs=[sm, sm, sm] + [vm] * pairs,
        out_specs=[vm] * (2 * pairs),
        out_shape=[jax.ShapeDtypeStruct((rows, PAIR), BF)] * pairs
        + [jax.ShapeDtypeStruct((nb, 8, blk), F32)] * pairs,
        scratch_shapes=[
            pltpu.VMEM((nb, blk, width), BF),
            pltpu.VMEM((nb, width, blk), BF),
            pltpu.VMEM((nb, heads, width, blk), BF),
            pltpu.VMEM((heads, blk, blk), F32),
            pltpu.VMEM((heads, blk, blk), F32),
            pltpu.VMEM((heads, 8, blk), F32),
            pltpu.VMEM((heads, 8, blk), F32),
            pltpu.VMEM((nb, width, blk), F32),
            pltpu.VMEM((nb, heads, 8, blk), F32),
            pltpu.VMEM((nb, heads, 8, blk), F32),
            pltpu.SMEM((nb,), jnp.int32),
        ],
        compiler_params=pltpu.CompilerParams(vmem_limit_bytes=24 << 20),
        cost_estimate=pl.CostEstimate(
            flops=heads * 4500000000, bytes_accessed=3 << 20, transcendentals=heads << 21
        ),
        name="attention",
    )(q[None], block_of, length, *qkv)
    return result[:pairs], result[pairs:]


def attention_back(q, block_of, length, qkv, grad_out, out, lse, tables, blk):
    rows = qkv.shape[0]
    width = qkv.shape[1] // 3
    heads = width // HEAD_DIM
    nb = rows // blk

    def body(
        q_ref, block_ref, length_ref, qkv_ref, gout_ref, att_ref, lse_ref, cos_in, sin_in, cos_at, sin_at, result_ref,
        keys, keys_t, values, q_cols, q_rows, g_cols, g_rows, grad_q, grad_k, grad_v, inner,
        even_p, even_d, odd_p, odd_d, order_ref,
    ):
        fill_order(order_ref, q_ref, block_ref, nb)
        live = length_ref[0]
        edge = lax.div(live, blk)
        lane_head = lax.div(lax.broadcasted_iota(jnp.int32, (1, width), 1), HEAD_DIM)
        picks = [jnp.where(lane_head == h, 1.0, 0.0).astype(BF) for h in range(heads)]

        def fill(p, carry):
            rows_at = pl.ds(pl.multiple_of(order_ref[p] * blk, blk), blk)
            key_block = qkv_ref[rows_at, width : 2 * width]
            keys[p] = key_block
            keys_t[p] = jnp.transpose(key_block)
            values[p] = qkv_ref[rows_at, 2 * width :]
            grad_k[p] = jnp.zeros((blk, width), F32)
            grad_v[p] = jnp.zeros((blk, width), F32)
            query = qkv_ref[rows_at, :width]
            gout = gout_ref[rows_at, :]
            inner_t = jnp.transpose(gout.astype(F32) * att_ref[rows_at, :].astype(F32))
            head_columns(q_cols, p, jnp.transpose(query), heads)
            head_columns(g_cols, p, jnp.transpose(gout), heads)
            for h in range(heads):
                at = slice(h * blk, (h + 1) * blk)
                q_rows[p, at, :] = query * picks[h]
                g_rows[p, at, :] = gout * picks[h]
                inner[p, h : h + 1, :] = jnp.sum(
                    inner_t[h * HEAD_DIM : (h + 1) * HEAD_DIM, :], axis=0, keepdims=True
                )
            return carry

        lax.fori_loop(0, nb, fill, 0)

        def make(i, j, to_p, to_d, masks):
            key_block, value_block = keys[j], values[j]
            for h in range(heads):
                s = mm(key_block, q_cols[i, h])
                if masks:
                    s = jnp.where(tile_mask(i, j, live, blk), s, NEG)
                p = jnp.exp2(s - lse_ref[i, h : h + 1, :])
                d = p * (mm(value_block, g_cols[i, h]) - inner[i, h : h + 1, :])
                to_p[:, h * blk : (h + 1) * blk] = p.astype(BF)
                to_d[:, h * blk : (h + 1) * blk] = d.astype(BF)

        def use(i, j, from_p, from_d, first):
            grad_v[j] += mm(from_p[...], g_rows[i])
            grad_k[j] += mm(from_d[...], q_rows[i])
            for h in range(heads):
                at = slice(h * HEAD_DIM, (h + 1) * HEAD_DIM)
                product = mm(keys_t[j, at, :], from_d[:, h * blk : (h + 1) * blk])
                if first:
                    grad_q[i, at, :] = product
                else:
                    grad_q[i, at, :] += product

        make(0, 0, even_p, even_d, True)

        def masked_pair(t, carry):
            i0 = 2 * t
            i1 = i0 + 1
            i2 = jnp.minimum(i0 + 2, nb - 1)
            make(i1, jnp.minimum(i1, edge), odd_p, odd_d, True)
            use(i0, jnp.minimum(i0, edge), even_p, even_d, True)
            make(i2, jnp.minimum(i2, edge), even_p, even_d, True)
            use(i1, jnp.minimum(i1, edge), odd_p, odd_d, True)
            return carry

        lax.fori_loop(0, nb // 2, masked_pair, 0)

        make(1, 0, even_p, even_d, False)

        def pair(t, place):
            i0, j0 = place
            i1, j1 = next_open(i0, j0, edge, nb)
            make(i1, j1, odd_p, odd_d, False)
            use(i0, j0, even_p, even_d, False)
            i2, j2 = next_open(i1, j1, edge, nb)
            make(i2, j2, even_p, even_d, False)
            use(i1, j1, odd_p, odd_d, False)
            return (i2, j2)

        count = open_tiles(edge, nb)
        i_last, j_last = lax.fori_loop(0, lax.div(count, 2), pair, (jnp.int32(1), jnp.int32(0)))

        @pl.when(lax.rem(count, 2) == 1)
        def _():
            use(i_last, j_last, even_p, even_d, False)

        def drain(p, carry):
            rows_at = pl.ds(pl.multiple_of(order_ref[p] * blk, blk), blk)
            cos_part, sin_part = tables_at((cos_in, sin_in, cos_at, sin_at), p)
            result_ref[rows_at, :width] = turned(jnp.transpose(grad_q[p]) * 0.125, cos_part, sin_part, True).astype(BF)
            result_ref[rows_at, width : 2 * width] = turned(grad_k[p] * math.log(2.0), cos_part, sin_part, True).astype(BF)
            result_ref[rows_at, 2 * width :] = grad_v[p].astype(BF)
            return carry

        lax.fori_loop(0, nb, drain, 0)

    vm = pl.BlockSpec(memory_space=pltpu.VMEM)
    sm = pl.BlockSpec(memory_space=pltpu.SMEM)
    return pl.pallas_call(
        body,
        in_specs=[sm] * 3 + [vm] * 8,
        out_specs=vm,
        out_shape=jax.ShapeDtypeStruct((rows, 3 * width), BF),
        scratch_shapes=[
            pltpu.VMEM((nb, blk, width), BF),
            pltpu.VMEM((nb, width, blk), BF),
            pltpu.VMEM((nb, blk, width), BF),
            pltpu.VMEM((nb, heads, width, blk), BF),
            pltpu.VMEM((nb, heads * blk, width), BF),
            pltpu.VMEM((nb, heads, width, blk), BF),
            pltpu.VMEM((nb, heads * blk, width), BF),
            pltpu.VMEM((nb, width, blk), F32),
            pltpu.VMEM((nb, blk, width), F32),
            pltpu.VMEM((nb, blk, width), F32),
            pltpu.VMEM((nb, 8, blk), F32),
            pltpu.VMEM((blk, heads * blk), BF),
            pltpu.VMEM((blk, heads * blk), BF),
            pltpu.VMEM((blk, heads * blk), BF),
            pltpu.VMEM((blk, heads * blk), BF),
            pltpu.SMEM((nb,), jnp.int32),
        ],
        compiler_params=pltpu.CompilerParams(vmem_limit_bytes=36 << 20),
        cost_estimate=pl.CostEstimate(
            flops=heads * 9000000000, bytes_accessed=6 << 20, transcendentals=heads << 21
        ),
        name="attention_back",
    )(q[None], block_of, length, qkv, grad_out, out, lse, *tables)


def gelu_both(u):
    scale = math.sqrt(2.0 / math.pi)
    inside = jnp.tanh(scale * (u + 0.044715 * u * u * u))
    value = 0.5 * u * (1.0 + inside)
    slope = 0.5 * (1.0 + inside) + 0.5 * u * (1.0 - inside * inside) * scale * (
        1.0 + 3.0 * 0.044715 * u * u
    )
    return value, slope


def bundle_up(q, w_qkv, w_attn, gain_rows, part):
    shard, dim = w_attn.shape
    pairs = part // PAIR

    def body(q_ref, qkv_ref, attn_ref, gain_ref, out_ref):
        at = q_ref[0] * part
        for p in range(pairs):
            for t in range(3):
                to = (3 * p + t) * PAIR
                out_ref[:shard, to : to + PAIR] = qkv_ref[
                    :, pl.ds(pl.multiple_of(t * dim + at + p * PAIR, PAIR), PAIR)
                ]
        out_ref[:shard, 3 * part :] = attn_ref[:, pl.ds(pl.multiple_of(at, part), part)]
        out_ref[shard:, :] = jnp.zeros((EXTRA, dim), BF)
        out_ref[shard:, : gain_ref.shape[1]] = gain_ref[...]

    return pl.pallas_call(
        body,
        in_specs=[SM, VM, VM, VM],
        out_specs=VM,
        out_shape=jax.ShapeDtypeStruct((shard + EXTRA, dim), BF),
        compiler_params=pltpu.CompilerParams(vmem_limit_bytes=8 << 20),
        name="bundle_up",
    )(q[None], w_qkv, w_attn, gain_rows)


def mlp_half(c, w_up, w_down, n):
    shard, ff = w_up.shape
    dim = w_down.shape[1]
    half = ff // n // 2
    if half % 128:
        up = lax.dynamic_index_in_dim(
            w_up.reshape(shard, n, 2, half), c, 2, keepdims=False
        ).reshape(shard, n * half)
        down = lax.dynamic_slice_in_dim(w_down, c * half, half, 0)
        return jnp.concatenate([up[:, :dim], up[:, dim:], down], axis=0)

    def body(c_ref, up_ref, down_ref, to_ref):
        for core in range(2):

            @pl.when(c_ref[0] == core)
            def _(core=core):
                for s in range(n):
                    at = (2 * s + core) * half
                    to_row, to_col = divmod(s * half, dim)
                    to_ref[to_row * shard : (to_row + 1) * shard, to_col : to_col + half] = up_ref[
                        :, at : at + half
                    ]
                to_ref[2 * shard :, :] = down_ref[core * half : (core + 1) * half, :]

    return pl.pallas_call(
        body,
        in_specs=[SM, VM, VM],
        out_specs=VM,
        out_shape=jax.ShapeDtypeStruct((2 * shard + half, dim), w_up.dtype),
        compiler_params=pltpu.CompilerParams(vmem_limit_bytes=8 << 20),
        cost_estimate=SMALL,
        name="mlp_half",
    )(c[None], w_up, w_down)


def attention_end(q, att, from_core, from_x, attn_w, hidden, gains, blk):
    rows, dim = hidden.shape
    pairs = len(att)
    part = pairs * PAIR
    steps = rows // blk

    def body(q_ref, *refs):
        own_refs = refs[:pairs]
        (
            one_ref, two_ref, three_ref, weight_ref, hidden_ref, gain_ref, att_ref, branch_ref, middle_ref, normed_ref,
        ) = refs[pairs:]
        for p in range(pairs):
            senders = (own_refs[p][...], one_ref[p], two_ref[p], three_ref[p])
            for g, block in enumerate(senders):
                at = lax.bitwise_xor(q_ref[0], g) * part + p * PAIR
                att_ref[:, pl.ds(pl.multiple_of(at, PAIR), PAIR)] = block
        branch = mm(att_ref[...], weight_ref[...])
        branch_ref[...] = branch
        middle = hidden_ref[...].astype(F32) + normalize(branch)[0] * gain_ref[1:2, :].astype(F32)
        middle_ref[...] = middle
        normed_ref[...] = (normalize(middle)[0] * gain_ref[2:3, :].astype(F32)).astype(BF)

    row = pl.BlockSpec((blk, dim), lambda i: (i, 0))
    first = pl.BlockSpec((pairs, blk, PAIR), lambda i: (0, i, 0))
    second = pl.BlockSpec((pairs, blk, PAIR), lambda i: (0, steps + i, 0))
    return pl.pallas_call(
        body,
        grid=(steps,),
        in_specs=[SM]
        + [pl.BlockSpec((blk, PAIR), lambda i: (i, 0))] * pairs
        + [
            first,
            first,
            second,
            pl.BlockSpec(attn_w.shape, lambda i: (0, 0)),
            row,
            pl.BlockSpec(gains.shape, lambda i: (0, 0)),
        ],
        out_specs=[row] * 4,
        out_shape=[
            jax.ShapeDtypeStruct((rows, dim), BF),
            jax.ShapeDtypeStruct((rows, dim), F32),
            jax.ShapeDtypeStruct((rows, dim), F32),
            jax.ShapeDtypeStruct((rows, dim), BF),
        ],
        compiler_params=pltpu.CompilerParams(vmem_limit_bytes=24 << 20),
        cost_estimate=SMALL,
        name="attention_end",
    )(q[None], *att, from_core, from_x, from_core, attn_w, hidden, gains)


def lifted_back(grad_lowered, down_w, slope):
    rows, dim = grad_lowered.shape
    wide = down_w.shape[0]
    step = 512

    def body(grad_ref, weight_ref, slope_ref, out_ref):
        out_ref[...] = (
            mm_nt(grad_ref[...], weight_ref[...]) * slope_ref[...].astype(F32)
        ).astype(BF)

    return pl.pallas_call(
        body,
        grid=(wide // step,),
        in_specs=[
            pl.BlockSpec((rows, dim), lambda i: (0, 0)),
            pl.BlockSpec((step, dim), lambda i: (i, 0)),
            pl.BlockSpec((rows, step), lambda i: (0, i)),
        ],
        out_specs=pl.BlockSpec((rows, step), lambda i: (0, i)),
        out_shape=jax.ShapeDtypeStruct((rows, wide), BF),
        compiler_params=pltpu.CompilerParams(vmem_limit_bytes=32 << 20),
        cost_estimate=SMALL,
        name="lifted_back",
    )(grad_lowered, down_w, slope)


def upstream_of(base_ref, length_ref, cotangent_ref, blk):
    pos = base_ref[pl.program_id(0)] * blk + lax.broadcasted_iota(jnp.int32, (blk, 1), 0)
    return cotangent_ref[...].astype(F32) * jnp.where(pos < length_ref[0], 1.0, 0.0)


def column_sums(value):
    return jnp.sum(value, axis=0, keepdims=True)


def top(bases, length, own, came, middle, cotangent, gains, blk):
    rows, dim = middle.shape

    def body(base_ref, length_ref, own_ref, came_ref, middle_ref, cot_ref, gain_ref, result_ref, grad_ref, sum_ref):
        gain = gain_ref[3:4, :].astype(F32)
        unit, scale = normalize(own_ref[...] + came_ref[...])
        result_ref[...] = (middle_ref[...] + unit * gain).astype(BF)
        upstream = upstream_of(base_ref, length_ref, cot_ref, blk)
        grad_ref[...] = norm_back(unit, scale, gain, upstream).astype(BF)

        @pl.when(pl.program_id(0) == 0)
        def _():
            sum_ref[...] = jnp.zeros_like(sum_ref)

        sum_ref[0:1, :] += column_sums(upstream * unit)

    row = pl.BlockSpec((blk, dim), lambda i: (i, 0))
    return pl.pallas_call(
        body,
        grid=(rows // blk,),
        in_specs=[SM, SM, row, row, row, row, pl.BlockSpec(gains.shape, lambda i: (0, 0))],
        out_specs=[row, row, pl.BlockSpec((8, dim), lambda i: (0, 0))],
        out_shape=[
            jax.ShapeDtypeStruct((rows, dim), BF),
            jax.ShapeDtypeStruct((rows, dim), BF),
            jax.ShapeDtypeStruct((8, dim), F32),
        ],
        compiler_params=pltpu.CompilerParams(vmem_limit_bytes=24 << 20),
        cost_estimate=pl.CostEstimate(flops=20 << 20, bytes_accessed=9 << 20, transcendentals=0),
        name="top",
    )(bases, length, own, came, middle, cotangent, gains)


def middle_back(q, bases, length, own, came, middle, branch, cotangent, gains, attn_w, last_sum, blk):
    rows, dim = middle.shape
    part = dim // 4
    pairs = part // PAIR
    steps = rows // blk

    def body(
        q_ref, base_ref, length_ref, own_ref, came_ref, middle_ref, branch_ref, cot_ref, gain_ref, weight_ref,
        last_ref, middle_out, branch_out, pieces_out, sums_out, attended, sums,
    ):
        i = pl.program_id(0)
        incoming = own_ref[...] + came_ref[...]
        unit, scale = normalize(middle_ref[...])
        grad_middle = upstream_of(base_ref, length_ref, cot_ref, blk) + norm_back(
            unit, scale, gain_ref[2:3, :].astype(F32), incoming
        )
        middle_out[...] = grad_middle
        sum2 = column_sums(incoming * unit)
        unit, scale = normalize(branch_ref[...])
        sum1 = column_sums(grad_middle * unit)
        grad_branch = norm_back(unit, scale, gain_ref[1:2, :].astype(F32), grad_middle).astype(BF)
        branch_out[...] = grad_branch
        attended[...] = mm_nt(grad_branch, weight_ref[...]).astype(BF)
        for g in range(4):
            at = lax.bitwise_xor(q_ref[0], g) * part
            for p in range(pairs):
                pieces_out[p, g] = attended[:, pl.ds(pl.multiple_of(at + p * PAIR, PAIR), PAIR)]

        @pl.when(i == 0)
        def _():
            sums[...] = jnp.zeros_like(sums)

        sums[0:1, :] += sum1
        sums[1:2, :] += sum2

        @pl.when(i == steps - 1)
        def _():
            sums[2:3, :] = last_ref[0:1, :]
            sums_out[...] = sums[...].astype(BF)

    row = pl.BlockSpec((blk, dim), lambda i: (i, 0))

    def whole(array):
        return pl.BlockSpec(array.shape, lambda i: (0, 0))

    return pl.pallas_call(
        body,
        grid=(steps,),
        in_specs=[SM, SM, SM, row, row, row, row, row, whole(gains), whole(attn_w), whole(last_sum)],
        out_specs=[
            row,
            row,
            pl.BlockSpec((pairs, 4, blk, PAIR), lambda i: (0, 0, i, 0)),
            pl.BlockSpec((EXTRA, dim), lambda i: (0, 0)),
        ],
        out_shape=[
            jax.ShapeDtypeStruct((rows, dim), F32),
            jax.ShapeDtypeStruct((rows, dim), BF),
            jax.ShapeDtypeStruct((pairs, 4, rows, PAIR), BF),
            jax.ShapeDtypeStruct((EXTRA, dim), BF),
        ],
        scratch_shapes=[pltpu.VMEM((blk, dim), BF), pltpu.VMEM((EXTRA, dim), F32)],
        compiler_params=pltpu.CompilerParams(vmem_limit_bytes=32 << 20),
        cost_estimate=pl.CostEstimate(
            flops=2 * rows * dim * dim, bytes_accessed=16 << 20, transcendentals=0
        ),
        name="middle_back",
    )(q[None], bases, length, own, came, middle, branch, cotangent, gains, attn_w, last_sum)


def bottom(own, from_core, from_x, hidden, grad_middle, gains, blk):
    rows, dim = hidden.shape

    def body(own_ref, core_ref, x_ref, hidden_ref, middle_ref, gain_ref, out_ref):
        incoming = own_ref[...] + core_ref[...].astype(F32) + x_ref[...].astype(F32)
        unit, scale = normalize(hidden_ref[...].astype(F32))
        out_ref[...] = middle_ref[...] + norm_back(
            unit, scale, gain_ref[0:1, :].astype(F32), incoming
        )

    row = pl.BlockSpec((blk, dim), lambda i: (i, 0))
    return pl.pallas_call(
        body,
        grid=(rows // blk,),
        in_specs=[row] * 5 + [pl.BlockSpec(gains.shape, lambda i: (0, 0))],
        out_specs=row,
        out_shape=jax.ShapeDtypeStruct((rows, dim), F32),
        compiler_params=pltpu.CompilerParams(vmem_limit_bytes=24 << 20),
        cost_estimate=pl.CostEstimate(flops=20 << 20, bytes_accessed=9 << 20, transcendentals=0),
        name="bottom",
    )(own, from_core, from_x, hidden, grad_middle, gains)


def up_end(c, mine, peer, shard, n, ff_half):
    wide = n * ff_half
    dim = wide // 2
    if ff_half % 128:
        mine, peer = [jnp.concatenate([v[:shard], v[shard:]], axis=1) for v in (mine, peer)]
        first, second = jnp.where(c == 0, mine, peer), jnp.where(c == 0, peer, mine)
        blocks = [v.reshape(shard, n, ff_half) for v in (first, second)]
        return jnp.stack(blocks, axis=2).reshape(shard, 2 * wide)

    def body(c_ref, mine_ref, peer_ref, up_ref):
        def put(first, second):
            for s in range(n):
                row, col = divmod(s * ff_half, dim)
                at = (slice(row * shard, (row + 1) * shard), slice(col, col + ff_half))
                up_ref[:, 2 * s * ff_half : (2 * s + 1) * ff_half] = first[at]
                up_ref[:, (2 * s + 1) * ff_half : (2 * s + 2) * ff_half] = second[at]

        @pl.when(c_ref[0] == 0)
        def _():
            put(mine_ref, peer_ref)

        @pl.when(c_ref[0] == 1)
        def _():
            put(peer_ref, mine_ref)

    return pl.pallas_call(
        body,
        in_specs=[SM, VM, VM],
        out_specs=VM,
        out_shape=jax.ShapeDtypeStruct((shard, 2 * wide), F32),
        compiler_params=pltpu.CompilerParams(vmem_limit_bytes=16 << 20),
        cost_estimate=SMALL,
        name="up_end",
    )(c[None], mine, peer)


def last_end(q, quarters, w_qkv, own_gains, late, part):
    shard, wide = w_qkv.shape
    pairs = part // PAIR
    dim = wide // 3

    def body(q_ref, quarters_ref, weight_ref, gain_ref, late_ref, out_ref, attn_ref, gains_ref):
        total = jnp.zeros((shard, PAIR), F32)
        for b in range(4):
            block = quarters_ref[lax.bitwise_xor(q_ref[0], b)][:shard].astype(F32)
            for p in range(pairs):
                for t in range(3):
                    at = t * dim + b * part + p * PAIR
                    value = block[:, (3 * p + t) * PAIR : (3 * p + t + 1) * PAIR]
                    out_ref[:, at : at + PAIR] = value
                    total = total + value * weight_ref[:, at : at + PAIR].astype(F32)
            attn_ref[:, b * part : (b + 1) * part] = block[:, 3 * part :]
        first = jnp.sum(total, axis=1, keepdims=True) / gain_ref[:, 0:1].astype(F32)
        lane = lax.broadcasted_iota(jnp.int32, (shard, 4), 1)
        gains_ref[...] = jnp.where(lane == 0, first, late_ref[...])

    return pl.pallas_call(
        body,
        in_specs=[SM] + [VM] * 4,
        out_specs=[VM] * 3,
        out_shape=[
            jax.ShapeDtypeStruct((shard, wide), F32),
            jax.ShapeDtypeStruct((shard, dim), F32),
            jax.ShapeDtypeStruct((shard, 4), F32),
        ],
        compiler_params=pltpu.CompilerParams(vmem_limit_bytes=16 << 20),
        cost_estimate=SMALL,
        name="last_end",
    )(q[None], quarters, w_qkv, own_gains, late)


def per_device(n, hidden_in, cotangent, lengths, block_of, w_qkv, w_attn, w_up, w_down, norm_gains):
    own_rows, dim = hidden_in.shape[1:]
    rows = 4 * own_rows
    blk = own_rows // 2
    ff = w_up.shape[1]
    shard = dim // n
    ff_half = ff // n // 2
    part = dim // 4
    pairs = part // PAIR
    q = lax.axis_index("ctx")
    c = lax.rem(q, 2)

    gain_rows = jnp.pad(norm_gains.T, ((0, EXTRA - 4), (0, 0)))
    bundle = bundle_up(q, w_qkv, w_attn, gain_rows, part)

    def store_bundle(target, owner, block):
        to_qkv, to_attn, to_gains = target
        return (
            lax.dynamic_update_slice(to_qkv, block[:shard, : 3 * part], (owner * shard, 0)),
            lax.dynamic_update_slice(to_attn, block[:shard, 3 * part :], (owner * shard, 0)),
            lax.dynamic_update_slice(to_gains, block[shard:, :shard], (0, owner * shard)),
        )

    def store_rows(target, owner, block):
        return lax.dynamic_update_slice(target, block, (owner * block.shape[0], 0))

    lead = Gather(
        bundle,
        n,
        False,
        store_bundle,
        (blank((dim, 3 * part), BF), blank((dim, part), BF), blank((EXTRA, dim), BF)),
    )
    mlp_own = mlp_half(c, w_up, w_down, n)
    bases = lax.dynamic_slice_in_dim(block_of, q, 1, 0)[0]
    tables = rotary_tables(blk, 8)
    hidden_b = hidden_in[0]

    hidden_all = lax.dynamic_update_slice(blank((rows, dim), BF), hidden_b, (0, 0))
    hidden_x = swap(hidden_b, 2)
    came, hidden_c = tie(lead.send(), swap(hidden_b, 1))
    lead.land(came)
    hidden_all = lax.dynamic_update_slice(hidden_all, hidden_c, (own_rows, 0))
    came, mlp_own = tie(lead.send(), mlp_own)
    lead.land(came)
    came, hidden_x = tie(lead.send(), hidden_x)
    lead.land(came)
    hidden_all = lax.dynamic_update_slice(hidden_all, hidden_x, (2 * own_rows, 0))
    came, hidden_d, mlp_own = tie(lead.send(), swap(hidden_x, 1), mlp_own)
    hidden_all = lax.dynamic_update_slice(hidden_all, hidden_d, (3 * own_rows, 0))
    lead.land(came)
    qkv_w, attn_q, gains = lead.rest()

    mlp = MergedGather(
        mlp_own, n, blank((dim, n * ff_half), BF), blank((n * ff_half, dim), BF)
    )
    normed, *qkv = project(q, block_of, hidden_all, qkv_w, gains, tables, blk)
    att, lse = attention(q, block_of, lengths, qkv, blk)
    came_mlp, attn_x, att, attn_q, mlp.targets = tie(
        mlp.send(), swap(attn_q, 2), att, attn_q, mlp.targets
    )
    mlp.land(came_mlp)

    half_rows = rows // 2
    from_x = swap(jnp.stack([a[half_rows:] for a in att]), 2)
    from_core = swap(
        jnp.stack(
            [
                jnp.concatenate([a[own_rows:half_rows], from_x[p, own_rows:]], axis=0)
                for p, a in enumerate(att)
            ]
        ),
        1,
    )
    attn_c = swap(jnp.stack([attn_q, attn_x]), 1)
    came_mlp, from_x, from_core, att, attn_x, attn_q, attn_c, mlp.targets = tie(
        mlp.send(), from_x, from_core, att, attn_x, attn_q, attn_c, mlp.targets
    )
    mlp.land(came_mlp)
    attn_parts = jnp.stack([attn_q, attn_c[0], attn_x, attn_c[1]])
    attn_w = jnp.concatenate(
        [
            lax.dynamic_index_in_dim(attn_parts, lax.bitwise_xor(q, b), 0, keepdims=False)
            for b in range(4)
        ],
        axis=1,
    )

    attended, branch, middle, normed_mid = attention_end(
        q, [a[:own_rows] for a in att], from_core, from_x, attn_w, hidden_b, gains, blk
    )
    came_mlp, normed_mid, normed_mid_c, mlp.targets = tie(
        mlp.send(), normed_mid, swap(normed_mid, 1), mlp.targets
    )
    mlp.land(came_mlp)

    came_mlp, normed_mid, normed_mid_c, mlp.targets = tie(
        mlp.send(), normed_mid, normed_mid_c, mlp.targets
    )
    mlp.land(came_mlp)
    normed_mid2 = jnp.concatenate([normed_mid, normed_mid_c], axis=0)
    up_w, down_w = mlp.rest()
    lifted = mm(normed_mid2, up_w)
    activated, slope = [v.astype(BF) for v in gelu_both(lifted)]
    lowered_c = swap(mm(activated[own_rows:], down_w), 1)
    lowered = mm(activated[:own_rows], down_w)
    result, grad_lowered, last_sum = top(
        bases, lengths, lowered, lowered_c, middle, cotangent[0], gains, blk
    )

    grad_lowered2 = jnp.concatenate([grad_lowered, swap(grad_lowered, 1)], axis=0)
    x = lax.div(q, 2)
    down_g = mm_tn(activated, grad_lowered2).astype(BF)
    grad_lifted = lifted_back(grad_lowered2, down_w, slope)
    up_g = mm_tn(normed_mid2, grad_lifted).astype(BF)
    mlp_ring = MergedScatter(up_g, down_g, n)
    mlp_ring.blocks, grad_lifted = tie(mlp_ring.blocks, grad_lifted)

    grad_normed_mid_c = swap(mm_nt(grad_lifted[own_rows:], up_w), 1)
    grad_normed_mid = mm_nt(grad_lifted[:own_rows], up_w)
    grad_middle, grad_branch, pieces, sums = middle_back(
        q, bases, lengths, grad_normed_mid, grad_normed_mid_c, middle, branch, cotangent[0], gains,
        attn_w, last_sum, blk,
    )
    came_mlp, grad_branch, pieces = tie(mlp_ring.send(), grad_branch, pieces)
    mlp_ring.land(came_mlp)

    pieces = pieces.reshape(pairs, rows, PAIR)
    went_x = swap(pieces[:, half_rows:], 2)
    went_core = swap(
        jnp.concatenate([pieces[:, own_rows:half_rows], went_x[:, own_rows:]], axis=1), 1
    )
    attn_g = mm_tn(attended, grad_branch).astype(BF)
    half_cols = dim // 2
    attn_cols = jnp.concatenate(
        [attn_g[:, b * part : (b + 1) * part] for b in (0, 2, 1, 3)], axis=1
    )
    attn_own = lax.dynamic_slice_in_dim(attn_cols, c * half_cols, half_cols, 1)
    attn_came = swap(lax.dynamic_slice_in_dim(attn_cols, (1 - c) * half_cols, half_cols, 1), 1)
    came_mlp, went_x, went_core, pieces, attn_own, attn_came = tie(
        mlp_ring.send(), went_x, went_core, pieces, attn_own, attn_came
    )
    mlp_ring.land(came_mlp)
    grad_out = jnp.concatenate(
        [pieces[:, :own_rows], went_core[:, :own_rows], went_x[:, :own_rows], went_core[:, own_rows:]],
        axis=1,
    )
    attn_half = (attn_own.astype(F32) + attn_came.astype(F32)).astype(BF)

    def back(p):
        return attention_back(
            q, block_of, lengths, qkv[p], grad_out[p], att[p], lse[p], tables, blk
        )

    attn_x_own = lax.dynamic_slice_in_dim(attn_half, x * part, part, 1)
    attn_x_other = lax.dynamic_slice_in_dim(attn_half, (1 - x) * part, part, 1)
    mixed = [back(0)]
    attn_came, came_mlp, mixed, grad_out, attn_x_own = tie(
        swap(attn_x_other, 2), mlp_ring.send(), mixed, grad_out, attn_x_own
    )
    mlp_ring.land(came_mlp)
    attn_g = (attn_x_own.astype(F32) + attn_came.astype(F32)).astype(BF)

    mixed.append(back(1))
    came_mlp, mixed, attn_g = tie(mlp_ring.send(), mixed, attn_g)
    mlp_ring.land(came_mlp)
    mlp_sum = mlp_ring.rest()
    up_sum, down_sum = mlp_sum[: 2 * shard], mlp_sum[2 * shard :]

    def normed_back(g):
        at = slice(g * own_rows, (g + 1) * own_rows)
        wide = 3 * PAIR
        return sum(mm_nt(mixed[p][at], qkv_w[:, p * wide : (p + 1) * wide]) for p in range(pairs))

    qkv_g = jnp.concatenate([mm_tn(normed, m).astype(BF) for m in mixed], axis=1)
    to_core = jnp.concatenate([normed_back(1).astype(BF), normed_back(3).astype(BF)], axis=0)
    up_x, mixed, qkv_g, to_core, attn_g, up_sum, down_sum = tie(
        swap(up_sum, 2), mixed, qkv_g, to_core, attn_g, up_sum, down_sum
    )
    up_sum = up_sum.astype(F32) + up_x.astype(F32)

    last_ring = Scatter(last_pick(qkv_g, attn_g, sums, shard), n, False)
    came_last, came_core, down_x, own_part, for_x, up_sum, down_sum = tie(
        last_ring.send(),
        swap(to_core, 1),
        swap(down_sum, 2),
        normed_back(0),
        normed_back(2),
        up_sum,
        down_sum,
    )
    last_ring.land(came_last)
    for_x = (for_x + came_core[own_rows:].astype(F32)).astype(BF)
    down_sum = down_sum.astype(F32) + down_x.astype(F32)

    quarter = own_rows // 2
    came_last, from_x0, mlp_c, up_sum, down_sum, for_x = tie(
        last_ring.send(),
        swap(for_x[:quarter], 2),
        swap(jnp.concatenate([up_sum, down_sum], axis=0), 1),
        up_sum,
        down_sum,
        for_x,
    )
    last_ring.land(came_last)
    up_out = up_end(c, up_sum, mlp_c[: 2 * shard], shard, n, ff_half)
    down_c = mlp_c[2 * shard :]
    down_out = jnp.concatenate(
        [jnp.where(c == 0, down_sum, down_c), jnp.where(c == 0, down_c, down_sum)], axis=0
    )
    came_last, from_x1, up_out, down_out = tie(
        last_ring.send(), swap(for_x[quarter:], 2), up_out, down_out
    )
    last_ring.land(came_last)
    input_grad = bottom(
        own_part, came_core[:own_rows], jnp.concatenate([from_x0, from_x1], axis=0), hidden_b, grad_middle, gains, blk
    )

    came_last, input_grad = tie(last_ring.send(), input_grad)
    last_ring.land(came_last)
    last = last_ring.rest()

    last_x, last = tie(swap(last, 2), last)
    last_pair = jnp.stack([last, last_x])
    last_c, last_pair = tie(swap(last_pair, 1), last_pair)
    last_all = jnp.stack([last_pair[0], last_c[0], last_pair[1], last_c[1]])
    me = lax.axis_index("fsdp")
    late = lax.dynamic_slice(last_all, (0, shard, me * shard), (4, 4, shard)).astype(F32)
    late = (
        lax.dynamic_index_in_dim(late, q, 0, keepdims=False)
        + lax.dynamic_index_in_dim(late, lax.bitwise_xor(q, 1), 0, keepdims=False)
    ) + (
        lax.dynamic_index_in_dim(late, lax.bitwise_xor(q, 2), 0, keepdims=False)
        + lax.dynamic_index_in_dim(late, lax.bitwise_xor(q, 3), 0, keepdims=False)
    )
    late = jnp.roll(late, 1, axis=0).T
    qkv_out, attn_out, gains_out = last_end(q, last_all, w_qkv, norm_gains, late, part)
    return (
        result[None],
        input_grad[None],
        qkv_out,
        attn_out,
        up_out,
        down_out,
        gains_out,
    )


def solution(mesh):
    n = mesh.shape["fsdp"]

    def step(*args):
        return per_device(n, *args)

    rows = P("fsdp", "ctx", None)
    weight = P("fsdp", None)
    return jax.shard_map(
        step,
        mesh=mesh,
        in_specs=(rows, rows, P("fsdp"), P()) + (weight,) * 5,
        out_specs=(rows, rows) + (weight,) * 5,
        check_vma=False,
    )
```

```python
import math

import jax
import jax.numpy as jnp
import numpy as np
from jax import lax
from jax.experimental import pallas as pl
from jax.experimental.pallas import tpu as pltpu
from jax.sharding import PartitionSpec as P

HEAD_DIM = 64
PAIR = 2 * HEAD_DIM
EXTRA = 16
BF = jnp.bfloat16
F32 = jnp.float32
NEG = -1e30
EPS = 1e-05
VM = pl.BlockSpec(memory_space=pltpu.VMEM)
SM = pl.BlockSpec(memory_space=pltpu.SMEM)
SMALL = pl.CostEstimate(flops=1 << 10, bytes_accessed=1 << 10, transcendentals=0)


def mm(left, right):
    return jnp.dot(left, right, preferred_element_type=F32)


def mm_tn(left, right):
    return lax.dot_general(left, right, (((0,), (0,)), ((), ())), preferred_element_type=F32)


def mm_nt(left, right):
    return lax.dot_general(left, right, (((1,), (1,)), ((), ())), preferred_element_type=F32)


def swap(value, bit):
    return lax.ppermute(value, "ctx", [(i, i ^ bit) for i in range(4)])


def blank(shape, dtype):
    return pl.pallas_call(
        lambda out_ref: None,
        out_specs=pl.BlockSpec(memory_space=pl.ANY),
        out_shape=jax.ShapeDtypeStruct(shape, dtype),
        name="blank",
    )()


def ring_pairs(n):
    order = list(range(0, n, 2)) + list(range(n - 1, 0, -2))
    ahead = [(order[i], order[(i + 1) % n]) for i in range(n)]
    return ahead, [(b, a) for a, b in ahead]


def ring_owner(place, n):
    place = lax.rem(place + 2 * n, n)
    return jnp.where(place < n // 2, 2 * place, 2 * (n - place) - 1)


def ring_place(me, n):
    return jnp.where(lax.rem(me, 2) == 0, lax.div(me, 2), n - 1 - lax.div(me, 2))


HBM = pl.BlockSpec(memory_space=pltpu.HBM)


def in_hbm(array):
    return pltpu.with_memory_space_constraint(array, pltpu.HBM)


def tie(*trees):
    return lax.optimization_barrier(trees)


class Gather:
    def __init__(self, block, n, flip, store, target):
        self.ahead, self.back = ring_pairs(n)
        self.sign = -1
        if flip:
            self.ahead, self.back, self.sign = self.back, self.ahead, 1
        me = lax.axis_index("fsdp")
        self.n, self.place, self.count = n, ring_place(me, n), 0
        self.store, self.blocks = store, [block, block]
        self.target = store(target, me, block)

    def more(self):
        return self.count < self.n // 2

    def send(self):
        self.count += 1
        sent = [lax.ppermute(self.blocks[0], "fsdp", self.ahead)]
        if self.count <= (self.n - 1) // 2:
            sent.append(lax.ppermute(self.blocks[1], "fsdp", self.back))
        return sent

    def land(self, came):
        self.blocks = came
        for block, sign in zip(came, (self.sign, -self.sign)):
            owner = ring_owner(self.place + sign * self.count, self.n)
            self.target = self.store(self.target, owner, block)

    def rest(self):
        while self.more():
            self.land(tie(self.send())[0])
        return self.target


class Scatter:
    def __init__(self, pick, n, flip):
        self.ahead, self.back = ring_pairs(n)
        self.sign = 1
        if flip:
            self.ahead, self.back, self.sign = self.back, self.ahead, -1
        self.place = ring_place(lax.axis_index("fsdp"), n)
        self.n, self.pick, self.count = n, pick, 0
        self.blocks = [self.at(self.sign * (n // 2)), self.at(-self.sign * ((n - 1) // 2))]

    def at(self, offset, *blocks):
        return self.pick(offset, ring_owner(self.place + offset, self.n), *blocks)

    def more(self):
        return self.count < self.n // 2

    def send(self):
        self.count += 1
        sent = [lax.ppermute(self.blocks[0], "fsdp", self.ahead)]
        if self.count <= (self.n - 1) // 2:
            sent.append(lax.ppermute(self.blocks[1], "fsdp", self.back))
        return sent

    def land(self, came):
        one, two = self.n // 2 - self.count, (self.n - 1) // 2 - self.count
        if one > 0:
            self.blocks[0] = self.at(self.sign * one, came[0])
            if two > 0:
                self.blocks[1] = self.at(-self.sign * two, came[1])
            elif len(came) > 1:
                self.blocks[1] = came[1]
        else:
            self.total = self.at(0, came[0], came[1] if len(came) > 1 else self.blocks[1])

    def rest(self):
        while self.more():
            self.land(tie(self.send())[0])
        return self.total


def rows_of(array, size):
    def pick(offset, owner, *blocks):
        value = lax.dynamic_slice_in_dim(array, owner * size, size, 0)
        if not blocks:
            return value
        value = value.astype(F32)
        for block in blocks:
            value = value + block.astype(F32)
        return value.astype(BF)

    return pick


class MergedGather:
    def __init__(self, block, n, up_w, down_w):
        self.ahead, self.back = ring_pairs(n)
        me = lax.axis_index("fsdp")
        self.n, self.place, self.count = n, ring_place(me, n), 0
        self.half = block.shape[0] // 2
        self.blocks = [block, block]
        self.targets = [up_w, down_w]
        self.store([me, me], [block, block], [0])

    def store(self, owners, blocks, which):
        shard = self.half // 2
        dim = blocks[0].shape[1]

        def body(owners_ref, *refs):
            block_refs, (up_ref, down_ref) = refs[: len(blocks)], refs[len(blocks) + 2 :]

            def put(up_from, down_from):
                up_ref[:, :dim] = up_from[:shard, :]
                up_ref[:, dim:] = up_from[shard : 2 * shard, :]
                down_ref[...] = down_from[down_from.shape[0] - 2 * shard :, :]

            if len(which) == 1:
                put(*block_refs)
            else:
                for k in which:

                    @pl.when(pl.program_id(0) == k)
                    def _(k=k):
                        put(block_refs[k], block_refs[k])

        def whole(array):
            return pl.BlockSpec(array.shape, lambda i, o: (0, 0))

        self.targets = pl.pallas_call(
            body,
            grid_spec=pltpu.PrefetchScalarGridSpec(
                num_scalar_prefetch=1,
                grid=(len(which),),
                in_specs=[whole(b) for b in blocks] + [HBM, HBM],
                out_specs=[
                    pl.BlockSpec((shard, 2 * dim), lambda i, o: (o[i], 0)),
                    pl.BlockSpec((2 * shard, dim), lambda i, o: (o[i], 0)),
                ],
            ),
            out_shape=[pltpu.HBM(t.shape, t.dtype) for t in self.targets],
            input_output_aliases={1 + len(blocks): 0, 2 + len(blocks): 1},
            compiler_params=pltpu.CompilerParams(vmem_limit_bytes=16 << 20),
            cost_estimate=SMALL,
            name="store",
        )(jnp.stack(owners), *blocks, *self.targets)

    def more(self):
        return self.count < self.n // 2

    def send(self):
        self.count += 1
        one, two = self.blocks
        if not self.more():
            one, two = one[: self.half], two[self.half :]
        return [lax.ppermute(one, "fsdp", self.ahead), lax.ppermute(two, "fsdp", self.back)]

    def land(self, came):
        self.blocks = came
        owners = [ring_owner(self.place + sign * self.count, self.n) for sign in (-1, 1)]
        self.store(owners, came, [0, 1] if self.more() else [0])

    def rest(self):
        while self.more():
            self.land(tie(self.send())[0])
        return self.targets


class MergedScatter:
    def __init__(self, up_g, down_g, n):
        self.ahead, self.back = ring_pairs(n)
        self.place = ring_place(lax.axis_index("fsdp"), n)
        self.n, self.count, self.addends = n, 0, (up_g, down_g)
        self.half = 2 * up_g.shape[0] // n
        far = self.pick(n // 2, [])
        self.blocks = [far[: self.half], far[self.half :]]

    def pick(self, offset, adds):
        up_g, down_g = self.addends
        shard, dim = up_g.shape[0] // self.n, down_g.shape[1]
        half = self.half

        def body(owner_ref, up_ref, down_ref, *refs):
            out_ref = refs[-1]

            def put(start, size, value):
                value = value.astype(F32)
                for (first, block), ref in zip(adds, refs[:-1]):
                    if first <= start < first + block.shape[0]:
                        value = value + ref[start - first : start - first + size, :].astype(F32)
                out_ref[start : start + size, :] = value.astype(BF)

            put(0, shard, up_ref[:, :dim])
            put(shard, shard, up_ref[:, dim:])
            put(half, half, down_ref[...])

        return pl.pallas_call(
            body,
            grid_spec=pltpu.PrefetchScalarGridSpec(
                num_scalar_prefetch=1,
                grid=(1,),
                in_specs=[
                    pl.BlockSpec((shard, 2 * dim), lambda i, o: (o[0], 0)),
                    pl.BlockSpec((half, dim), lambda i, o: (o[0], 0)),
                ]
                + [pl.BlockSpec(b.shape, lambda i, o: (0, 0)) for _, b in adds],
                out_specs=pl.BlockSpec((2 * half, dim), lambda i, o: (0, 0)),
            ),
            out_shape=jax.ShapeDtypeStruct((2 * half, dim), BF),
            compiler_params=pltpu.CompilerParams(vmem_limit_bytes=16 << 20),
            cost_estimate=SMALL,
            name="merged_pick",
        )(ring_owner(self.place + offset, self.n)[None], up_g, down_g, *[b for _, b in adds])

    def more(self):
        return self.count < self.n // 2

    def send(self):
        self.count += 1
        return [
            lax.ppermute(self.blocks[0], "fsdp", self.ahead),
            lax.ppermute(self.blocks[1], "fsdp", self.back),
        ]

    def land(self, came):
        starts = (0, self.half) if self.count == 1 else (0, 0)
        if self.more():
            left = self.n // 2 - self.count
            self.blocks = [
                self.pick(sign * left, [(start, block)])
                for sign, start, block in zip((1, -1), starts, came)
            ]
        else:
            self.total = self.pick(0, list(zip(starts, came)))

    def rest(self):
        while self.more():
            self.land(tie(self.send())[0])
        return self.total


def last_pick(wide_g, narrow_g, sums, rows):
    wide, narrow = wide_g.shape[1], narrow_g.shape[1]

    def pick(offset, owner, *blocks):
        def body(owner_ref, wide_ref, narrow_ref, sums_ref, *refs):
            out_ref = refs[-1]

            def put(at_rows, at_cols, value):
                value = value.astype(F32)
                for ref in refs[:-1]:
                    value = value + ref[at_rows, at_cols].astype(F32)
                out_ref[at_rows, at_cols] = value.astype(BF)

            upper, lower = slice(0, rows), slice(rows, rows + EXTRA)
            put(upper, slice(0, wide), wide_ref[...])
            put(upper, slice(wide, wide + narrow), narrow_ref[...])
            put(lower, slice(0, wide + narrow), sums_ref[...])

        whole = pl.BlockSpec((rows + EXTRA, wide + narrow), lambda i, o: (0, 0))
        return pl.pallas_call(
            body,
            grid_spec=pltpu.PrefetchScalarGridSpec(
                num_scalar_prefetch=1,
                grid=(1,),
                in_specs=[
                    pl.BlockSpec((rows, wide), lambda i, o: (o[0], 0)),
                    pl.BlockSpec((rows, narrow), lambda i, o: (o[0], 0)),
                    pl.BlockSpec(sums.shape, lambda i, o: (0, 0)),
                ]
                + [whole] * len(blocks),
                out_specs=whole,
            ),
            out_shape=jax.ShapeDtypeStruct((rows + EXTRA, wide + narrow), BF),
            compiler_params=pltpu.CompilerParams(vmem_limit_bytes=8 << 20),
            cost_estimate=SMALL,
            name="last_pick",
        )(owner[None], wide_g, narrow_g, sums, *blocks)

    return pick


def normalize(values):
    average = jnp.mean(values, axis=-1, keepdims=True)
    centered = values - average
    variance = jnp.mean(centered * centered, axis=-1, keepdims=True)
    scale = lax.rsqrt(variance + EPS)
    return centered * scale, scale


def norm_back(unit, scale, gain, incoming):
    weighted = incoming * gain
    return (
        weighted
        - jnp.mean(weighted, axis=-1, keepdims=True)
        - unit * jnp.mean(weighted * unit, axis=-1, keepdims=True)
    ) * scale


def turned(value, cosine, sine_signed, inverse):
    width = value.shape[1]
    lane = lax.broadcasted_iota(jnp.int32, value.shape, 1)
    half = HEAD_DIM // 2
    other = jnp.where(
        lax.rem(lane, HEAD_DIM) < half,
        pltpu.roll(value, width - half, 1),
        pltpu.roll(value, half, 1),
    )
    repeat = width // cosine.shape[1]
    cosine = jnp.concatenate([cosine] * repeat, axis=1)
    sine_signed = jnp.concatenate([sine_signed] * repeat, axis=1)
    if inverse:
        return value * cosine - other * sine_signed
    return value * cosine + other * sine_signed


def block_at(q_ref, block_ref, k):
    return block_ref[lax.bitwise_xor(q_ref[0], lax.div(k, 2)), lax.rem(k, 2)]


def fill_order(order, q_ref, block_ref, count):
    def put(k, carry):
        order[block_at(q_ref, block_ref, k)] = k
        return carry

    lax.fori_loop(0, count, put, 0)


def rotary_tables(blk, count):
    lane = np.arange(PAIR)
    half = HEAD_DIM // 2
    inverse = np.exp(-2.0 * math.log(10000.0) / HEAD_DIM * (lane % half))
    sign = np.where(lane % HEAD_DIM < half, -1.0, 1.0)
    inside = np.arange(blk)[:, None] * inverse[None, :]
    starts = np.arange(count)[:, None] * blk * inverse[None, :]
    return [
        jnp.asarray(v, F32)
        for v in (np.cos(inside), np.sin(inside) * sign, np.cos(starts), np.sin(starts) * sign)
    ]


def tables_at(table_refs, block):
    cos_in, sin_in, cos_at, sin_at = table_refs
    cos_b, sin_b = cos_at[pl.ds(block, 1), :], sin_at[pl.ds(block, 1), :]
    cos_r, sin_r = cos_in[...], sin_in[...]
    return cos_r * cos_b - sin_r * sin_b, sin_r * cos_b + cos_r * sin_b


def project(q, block_of, hidden, weight, gains, tables, blk):
    rows, dim = hidden.shape
    width = weight.shape[1]
    pairs = width // (3 * PAIR)
    step = 2 * blk

    def body(q_ref, block_ref, hidden_ref, weight_ref, gain_ref, *refs):
        table_refs, normed_ref, out_refs = refs[:4], refs[4], refs[5:]
        unit, _ = normalize(hidden_ref[...].astype(F32))
        normed = (unit * gain_ref[0:1, :].astype(F32)).astype(BF)
        normed_ref[...] = normed
        mixed = mm(normed, weight_ref[...])
        halves = [
            tables_at(table_refs, block_at(q_ref, block_ref, 2 * pl.program_id(0) + k))
            for k in range(2)
        ]
        cos_part, sin_part = [jnp.concatenate(v, axis=0) for v in zip(*halves)]
        for p, out_ref in enumerate(out_refs):
            at = 3 * PAIR * p
            queries = turned(mixed[:, at : at + PAIR], cos_part, sin_part, False)
            out_ref[:, :PAIR] = (queries * (0.125 * math.log2(math.e))).astype(BF)
            out_ref[:, PAIR : 2 * PAIR] = turned(
                mixed[:, at + PAIR : at + 2 * PAIR], cos_part, sin_part, False
            ).astype(BF)
            out_ref[:, 2 * PAIR :] = mixed[:, at + 2 * PAIR : at + 3 * PAIR].astype(BF)

    def whole(array):
        return pl.BlockSpec(array.shape, lambda i: (0, 0))

    return pl.pallas_call(
        body,
        grid=(rows // step,),
        in_specs=[SM, SM, pl.BlockSpec((step, dim), lambda i: (i, 0)), whole(weight), whole(gains)]
        + [whole(t) for t in tables],
        out_specs=[pl.BlockSpec((step, dim), lambda i: (i, 0))]
        + [pl.BlockSpec((step, 3 * PAIR), lambda i: (i, 0))] * pairs,
        out_shape=[jax.ShapeDtypeStruct((rows, dim), BF)]
        + [jax.ShapeDtypeStruct((rows, 3 * PAIR), BF)] * pairs,
        compiler_params=pltpu.CompilerParams(vmem_limit_bytes=32 << 20),
        cost_estimate=pl.CostEstimate(
            flops=2 * rows * dim * width, bytes_accessed=12 << 20, transcendentals=rows
        ),
        name="project",
    )(q[None], block_of, in_hbm(hidden), weight, gains, *tables)


def folded(value, op):
    rows, cols = value.shape
    return op(value.reshape(rows // 8, 8, cols), axis=0)


def head_columns(target, p, value_t, heads):
    for h in range(heads):
        at = slice(h * HEAD_DIM, (h + 1) * HEAD_DIM)
        if h:
            target[p, h, : h * HEAD_DIM, :] = jnp.zeros((h * HEAD_DIM, value_t.shape[1]), BF)
        target[p, h, at, :] = value_t[at, :]
        rest = (heads - 1 - h) * HEAD_DIM
        if rest:
            target[p, h, (h + 1) * HEAD_DIM :, :] = jnp.zeros((rest, value_t.shape[1]), BF)


def tile_mask(i, j, live, blk):
    key = j * blk + lax.broadcasted_iota(jnp.int32, (blk, blk), 0)
    query = i * blk + lax.broadcasted_iota(jnp.int32, (blk, blk), 1)
    return (key <= query) & (key < live)


def open_tiles(edge, nb):
    return sum(jnp.minimum(i, edge) for i in range(nb))


def next_open(i, j, edge, nb):
    end = j + 1 >= jnp.minimum(i, edge)
    return jnp.minimum(jnp.where(end, i + 1, i), nb - 1), jnp.where(end, 0, j + 1)


def attention(q, block_of, length, qkv, blk):
    rows = qkv[0].shape[0]
    pairs = len(qkv)
    width = pairs * PAIR
    heads = width // HEAD_DIM
    nb = rows // blk

    def body(
        q_ref, block_ref, length_ref, *refs,
    ):
        qkv_refs, out_refs, lse_refs = refs[:pairs], refs[pairs : 2 * pairs], refs[2 * pairs : 3 * pairs]
        (keys, values_t, q_cols, even, odd, even_top, odd_top, total, tops, sums, order_ref) = refs[3 * pairs :]
        fill_order(order_ref, q_ref, block_ref, nb)
        live = length_ref[0]
        edge = lax.div(live, blk)

        def fill(p, carry):
            rows_at = pl.ds(pl.multiple_of(order_ref[p] * blk, blk), blk)
            keys[p] = jnp.concatenate([r[rows_at, PAIR : 2 * PAIR] for r in qkv_refs], axis=1)
            values_t[p] = jnp.transpose(
                jnp.concatenate([r[rows_at, 2 * PAIR :] for r in qkv_refs], axis=1)
            )
            queries = jnp.concatenate([r[rows_at, :PAIR] for r in qkv_refs], axis=1)
            head_columns(q_cols, p, jnp.transpose(queries), heads)
            return carry

        lax.fori_loop(0, nb, fill, 0)

        def ahead(i, j, into, top, masks):
            key_block = keys[j]
            for h in range(heads):
                s = mm(key_block, q_cols[i, h])
                if masks:
                    s = jnp.where(tile_mask(i, j, live, blk), s, NEG)
                into[h] = s
                top[h] = folded(s, jnp.max)

        def work(i, j, scores, top, first):
            for h in range(heads):
                new = jnp.broadcast_to(jnp.max(top[h], axis=0, keepdims=True), (8, blk))
                if not first:
                    old = tops[i, h]
                    new = jnp.maximum(old, new)
                    shrink = jnp.exp2(old - new)
                tops[i, h] = new
                p = jnp.exp2(scores[h] - new[0:1])
                added = folded(p, jnp.sum)
                sums[i, h] = added if first else sums[i, h] * shrink + added
                at = slice(h * HEAD_DIM, (h + 1) * HEAD_DIM)
                product = mm(values_t[j, at, :], p.astype(BF))
                total[i, at, :] = product if first else total[i, at, :] * shrink[0:1] + product

        ahead(0, 0, even, even_top, True)

        def masked_pair(t, carry):
            i0 = 2 * t
            i1 = i0 + 1
            i2 = jnp.minimum(i0 + 2, nb - 1)
            ahead(i1, jnp.minimum(i1, edge), odd, odd_top, True)
            work(i0, jnp.minimum(i0, edge), even, even_top, True)
            ahead(i2, jnp.minimum(i2, edge), even, even_top, True)
            work(i1, jnp.minimum(i1, edge), odd, odd_top, True)
            return carry

        lax.fori_loop(0, nb // 2, masked_pair, 0)

        ahead(1, 0, even, even_top, False)

        def pair(t, place):
            i0, j0 = place
            i1, j1 = next_open(i0, j0, edge, nb)
            ahead(i1, j1, odd, odd_top, False)
            work(i0, j0, even, even_top, False)
            i2, j2 = next_open(i1, j1, edge, nb)
            ahead(i2, j2, even, even_top, False)
            work(i1, j1, odd, odd_top, False)
            return (i2, j2)

        count = open_tiles(edge, nb)
        i_last, j_last = lax.fori_loop(0, lax.div(count, 2), pair, (jnp.int32(1), jnp.int32(0)))

        @pl.when(lax.rem(count, 2) == 1)
        def _():
            work(i_last, j_last, even, even_top, False)

        def drain(p, carry):
            rows_at = pl.ds(pl.multiple_of(order_ref[p] * blk, blk), blk)
            scaled = []
            for h in range(heads):
                sum_h = jnp.sum(sums[p, h], axis=0, keepdims=True)
                lse_refs[h // 2][p, h % 2 : h % 2 + 1, :] = tops[p, h][0:1] + jnp.log2(sum_h)
                scaled.append((total[p, h * HEAD_DIM : (h + 1) * HEAD_DIM, :] * (1.0 / sum_h)).astype(BF))
            both = jnp.transpose(jnp.concatenate(scaled, axis=0))
            for k, ref in enumerate(out_refs):
                ref[rows_at, :] = both[:, k * PAIR : (k + 1) * PAIR]
            return carry

        lax.fori_loop(0, nb, drain, 0)

    vm = pl.BlockSpec(memory_space=pltpu.VMEM)
    sm = pl.BlockSpec(memory_space=pltpu.SMEM)
    result = pl.pallas_call(
        body,
        in_specs=[sm, sm, sm] + [vm] * pairs,
        out_specs=[vm] * (2 * pairs),
        out_shape=[jax.ShapeDtypeStruct((rows, PAIR), BF)] * pairs
        + [jax.ShapeDtypeStruct((nb, 8, blk), F32)] * pairs,
        scratch_shapes=[
            pltpu.VMEM((nb, blk, width), BF),
            pltpu.VMEM((nb, width, blk), BF),
            pltpu.VMEM((nb, heads, width, blk), BF),
            pltpu.VMEM((heads, blk, blk), F32),
            pltpu.VMEM((heads, blk, blk), F32),
            pltpu.VMEM((heads, 8, blk), F32),
            pltpu.VMEM((heads, 8, blk), F32),
            pltpu.VMEM((nb, width, blk), F32),
            pltpu.VMEM((nb, heads, 8, blk), F32),
            pltpu.VMEM((nb, heads, 8, blk), F32),
            pltpu.SMEM((nb,), jnp.int32),
        ],
        compiler_params=pltpu.CompilerParams(vmem_limit_bytes=24 << 20),
        cost_estimate=pl.CostEstimate(
            flops=heads * 4500000000, bytes_accessed=3 << 20, transcendentals=heads << 21
        ),
        name="attention",
    )(q[None], block_of, length, *qkv)
    return result[:pairs], result[pairs:]


def attention_back(q, block_of, length, qkv, grad_out, out, lse, tables, blk):
    rows = qkv.shape[0]
    width = qkv.shape[1] // 3
    heads = width // HEAD_DIM
    nb = rows // blk

    def body(
        q_ref, block_ref, length_ref, qkv_ref, gout_ref, att_ref, lse_ref, cos_in, sin_in, cos_at, sin_at, result_ref,
        keys, keys_t, values, q_cols, q_rows, g_cols, g_rows, grad_q, grad_k, grad_v, inner,
        even_p, even_d, odd_p, odd_d, order_ref,
    ):
        fill_order(order_ref, q_ref, block_ref, nb)
        live = length_ref[0]
        edge = lax.div(live, blk)
        lane_head = lax.div(lax.broadcasted_iota(jnp.int32, (1, width), 1), HEAD_DIM)
        picks = [jnp.where(lane_head == h, 1.0, 0.0).astype(BF) for h in range(heads)]

        def fill(p, carry):
            rows_at = pl.ds(pl.multiple_of(order_ref[p] * blk, blk), blk)
            key_block = qkv_ref[rows_at, width : 2 * width]
            keys[p] = key_block
            keys_t[p] = jnp.transpose(key_block)
            values[p] = qkv_ref[rows_at, 2 * width :]
            grad_k[p] = jnp.zeros((blk, width), F32)
            grad_v[p] = jnp.zeros((blk, width), F32)
            query = qkv_ref[rows_at, :width]
            gout = gout_ref[rows_at, :]
            inner_t = jnp.transpose(gout.astype(F32) * att_ref[rows_at, :].astype(F32))
            head_columns(q_cols, p, jnp.transpose(query), heads)
            head_columns(g_cols, p, jnp.transpose(gout), heads)
            for h in range(heads):
                at = slice(h * blk, (h + 1) * blk)
                q_rows[p, at, :] = query * picks[h]
                g_rows[p, at, :] = gout * picks[h]
                inner[p, h : h + 1, :] = jnp.sum(
                    inner_t[h * HEAD_DIM : (h + 1) * HEAD_DIM, :], axis=0, keepdims=True
                )
            return carry

        lax.fori_loop(0, nb, fill, 0)

        def make(i, j, to_p, to_d, masks):
            key_block, value_block = keys[j], values[j]
            for h in range(heads):
                s = mm(key_block, q_cols[i, h])
                if masks:
                    s = jnp.where(tile_mask(i, j, live, blk), s, NEG)
                p = jnp.exp2(s - lse_ref[i, h : h + 1, :])
                d = p * (mm(value_block, g_cols[i, h]) - inner[i, h : h + 1, :])
                to_p[:, h * blk : (h + 1) * blk] = p.astype(BF)
                to_d[:, h * blk : (h + 1) * blk] = d.astype(BF)

        def use(i, j, from_p, from_d, first):
            grad_v[j] += mm(from_p[...], g_rows[i])
            grad_k[j] += mm(from_d[...], q_rows[i])
            for h in range(heads):
                at = slice(h * HEAD_DIM, (h + 1) * HEAD_DIM)
                product = mm(keys_t[j, at, :], from_d[:, h * blk : (h + 1) * blk])
                if first:
                    grad_q[i, at, :] = product
                else:
                    grad_q[i, at, :] += product

        make(0, 0, even_p, even_d, True)

        def masked_pair(t, carry):
            i0 = 2 * t
            i1 = i0 + 1
            i2 = jnp.minimum(i0 + 2, nb - 1)
            make(i1, jnp.minimum(i1, edge), odd_p, odd_d, True)
            use(i0, jnp.minimum(i0, edge), even_p, even_d, True)
            make(i2, jnp.minimum(i2, edge), even_p, even_d, True)
            use(i1, jnp.minimum(i1, edge), odd_p, odd_d, True)
            return carry

        lax.fori_loop(0, nb // 2, masked_pair, 0)

        make(1, 0, even_p, even_d, False)

        def pair(t, place):
            i0, j0 = place
            i1, j1 = next_open(i0, j0, edge, nb)
            make(i1, j1, odd_p, odd_d, False)
            use(i0, j0, even_p, even_d, False)
            i2, j2 = next_open(i1, j1, edge, nb)
            make(i2, j2, even_p, even_d, False)
            use(i1, j1, odd_p, odd_d, False)
            return (i2, j2)

        count = open_tiles(edge, nb)
        i_last, j_last = lax.fori_loop(0, lax.div(count, 2), pair, (jnp.int32(1), jnp.int32(0)))

        @pl.when(lax.rem(count, 2) == 1)
        def _():
            use(i_last, j_last, even_p, even_d, False)

        def drain(p, carry):
            rows_at = pl.ds(pl.multiple_of(order_ref[p] * blk, blk), blk)
            cos_part, sin_part = tables_at((cos_in, sin_in, cos_at, sin_at), p)
            result_ref[rows_at, :width] = turned(jnp.transpose(grad_q[p]) * 0.125, cos_part, sin_part, True).astype(BF)
            result_ref[rows_at, width : 2 * width] = turned(grad_k[p] * math.log(2.0), cos_part, sin_part, True).astype(BF)
            result_ref[rows_at, 2 * width :] = grad_v[p].astype(BF)
            return carry

        lax.fori_loop(0, nb, drain, 0)

    vm = pl.BlockSpec(memory_space=pltpu.VMEM)
    sm = pl.BlockSpec(memory_space=pltpu.SMEM)
    return pl.pallas_call(
        body,
        in_specs=[sm] * 3 + [vm] * 8,
        out_specs=vm,
        out_shape=jax.ShapeDtypeStruct((rows, 3 * width), BF),
        scratch_shapes=[
            pltpu.VMEM((nb, blk, width), BF),
            pltpu.VMEM((nb, width, blk), BF),
            pltpu.VMEM((nb, blk, width), BF),
            pltpu.VMEM((nb, heads, width, blk), BF),
            pltpu.VMEM((nb, heads * blk, width), BF),
            pltpu.VMEM((nb, heads, width, blk), BF),
            pltpu.VMEM((nb, heads * blk, width), BF),
            pltpu.VMEM((nb, width, blk), F32),
            pltpu.VMEM((nb, blk, width), F32),
            pltpu.VMEM((nb, blk, width), F32),
            pltpu.VMEM((nb, 8, blk), F32),
            pltpu.VMEM((blk, heads * blk), BF),
            pltpu.VMEM((blk, heads * blk), BF),
            pltpu.VMEM((blk, heads * blk), BF),
            pltpu.VMEM((blk, heads * blk), BF),
            pltpu.SMEM((nb,), jnp.int32),
        ],
        compiler_params=pltpu.CompilerParams(vmem_limit_bytes=36 << 20),
        cost_estimate=pl.CostEstimate(
            flops=heads * 9000000000, bytes_accessed=6 << 20, transcendentals=heads << 21
        ),
        name="attention_back",
    )(q[None], block_of, length, qkv, grad_out, out, lse, *tables)


def gelu_both(u):
    scale = math.sqrt(2.0 / math.pi)
    cubic = (0.044715 * scale) * (u * u)
    inside = jnp.tanh(u * (scale + cubic))
    half = 0.5 + 0.5 * inside
    value = u * half
    return value, half + value * (1.0 - inside) * (scale + 3.0 * cubic)


def bundle_up(q, w_qkv, w_attn, gain_rows, part):
    shard, dim = w_attn.shape
    pairs = part // PAIR

    def body(q_ref, qkv_ref, attn_ref, gain_ref, out_ref):
        at = q_ref[0] * part
        for p in range(pairs):
            for t in range(3):
                to = (3 * p + t) * PAIR
                out_ref[:shard, to : to + PAIR] = qkv_ref[
                    :, pl.ds(pl.multiple_of(t * dim + at + p * PAIR, PAIR), PAIR)
                ]
        out_ref[:shard, 3 * part :] = attn_ref[:, pl.ds(pl.multiple_of(at, part), part)]
        out_ref[shard:, :] = jnp.zeros((EXTRA, dim), BF)
        out_ref[shard:, : gain_ref.shape[1]] = gain_ref[...]

    return pl.pallas_call(
        body,
        in_specs=[SM, VM, VM, VM],
        out_specs=VM,
        out_shape=jax.ShapeDtypeStruct((shard + EXTRA, dim), BF),
        compiler_params=pltpu.CompilerParams(vmem_limit_bytes=8 << 20),
        name="bundle_up",
    )(q[None], w_qkv, w_attn, gain_rows)


def mlp_half(c, w_up, w_down, n):
    shard, ff = w_up.shape
    dim = w_down.shape[1]
    half = ff // n // 2
    if half % 128:
        up = lax.dynamic_index_in_dim(
            w_up.reshape(shard, n, 2, half), c, 2, keepdims=False
        ).reshape(shard, n * half)
        down = lax.dynamic_slice_in_dim(w_down, c * half, half, 0)
        return jnp.concatenate([up[:, :dim], up[:, dim:], down], axis=0)

    def body(c_ref, up_ref, down_ref, to_ref):
        for core in range(2):

            @pl.when(c_ref[0] == core)
            def _(core=core):
                for s in range(n):
                    at = (2 * s + core) * half
                    to_row, to_col = divmod(s * half, dim)
                    to_ref[to_row * shard : (to_row + 1) * shard, to_col : to_col + half] = up_ref[
                        :, at : at + half
                    ]
                to_ref[2 * shard :, :] = down_ref[core * half : (core + 1) * half, :]

    return pl.pallas_call(
        body,
        in_specs=[SM, VM, VM],
        out_specs=VM,
        out_shape=jax.ShapeDtypeStruct((2 * shard + half, dim), w_up.dtype),
        compiler_params=pltpu.CompilerParams(vmem_limit_bytes=8 << 20),
        cost_estimate=SMALL,
        name="mlp_half",
    )(c[None], w_up, w_down)


def attention_end(q, att, from_core, from_x, attn_w, hidden, gains, blk):
    rows, dim = hidden.shape
    pairs = len(att)
    part = pairs * PAIR
    steps = rows // blk

    def body(q_ref, *refs):
        own_refs = refs[:pairs]
        (
            one_ref, two_ref, three_ref, weight_ref, hidden_ref, gain_ref, att_ref, branch_ref, middle_ref, normed_ref,
        ) = refs[pairs:]
        for p in range(pairs):
            senders = (own_refs[p][...], one_ref[p], two_ref[p], three_ref[p])
            for g, block in enumerate(senders):
                at = lax.bitwise_xor(q_ref[0], g) * part + p * PAIR
                att_ref[:, pl.ds(pl.multiple_of(at, PAIR), PAIR)] = block
        branch = mm(att_ref[...], weight_ref[...])
        branch_ref[...] = branch
        middle = hidden_ref[...].astype(F32) + normalize(branch)[0] * gain_ref[1:2, :].astype(F32)
        middle_ref[...] = middle
        normed_ref[...] = (normalize(middle)[0] * gain_ref[2:3, :].astype(F32)).astype(BF)

    row = pl.BlockSpec((blk, dim), lambda i: (i, 0))
    first = pl.BlockSpec((pairs, blk, PAIR), lambda i: (0, i, 0))
    second = pl.BlockSpec((pairs, blk, PAIR), lambda i: (0, steps + i, 0))
    return pl.pallas_call(
        body,
        grid=(steps,),
        in_specs=[SM]
        + [pl.BlockSpec((blk, PAIR), lambda i: (i, 0))] * pairs
        + [
            first,
            first,
            second,
            pl.BlockSpec(attn_w.shape, lambda i: (0, 0)),
            row,
            pl.BlockSpec(gains.shape, lambda i: (0, 0)),
        ],
        out_specs=[row] * 4,
        out_shape=[
            jax.ShapeDtypeStruct((rows, dim), BF),
            jax.ShapeDtypeStruct((rows, dim), F32),
            jax.ShapeDtypeStruct((rows, dim), F32),
            jax.ShapeDtypeStruct((rows, dim), BF),
        ],
        compiler_params=pltpu.CompilerParams(vmem_limit_bytes=24 << 20),
        cost_estimate=SMALL,
        name="attention_end",
    )(q[None], *att, from_core, from_x, from_core, attn_w, hidden, gains)


def lifted_back(grad_lowered, down_w, slope):
    rows, dim = grad_lowered.shape
    wide = down_w.shape[0]
    step = 512

    def body(grad_ref, weight_ref, slope_ref, out_ref):
        out_ref[...] = (
            mm_nt(grad_ref[...], weight_ref[...]) * slope_ref[...].astype(F32)
        ).astype(BF)

    return pl.pallas_call(
        body,
        grid=(wide // step,),
        in_specs=[
            pl.BlockSpec((rows, dim), lambda i: (0, 0)),
            pl.BlockSpec((step, dim), lambda i: (i, 0)),
            pl.BlockSpec((rows, step), lambda i: (0, i)),
        ],
        out_specs=pl.BlockSpec((rows, step), lambda i: (0, i)),
        out_shape=jax.ShapeDtypeStruct((rows, wide), BF),
        compiler_params=pltpu.CompilerParams(vmem_limit_bytes=32 << 20),
        cost_estimate=SMALL,
        name="lifted_back",
    )(grad_lowered, down_w, slope)


def upstream_of(base_ref, length_ref, cotangent_ref, blk):
    pos = base_ref[pl.program_id(0)] * blk + lax.broadcasted_iota(jnp.int32, (blk, 1), 0)
    return cotangent_ref[...].astype(F32) * jnp.where(pos < length_ref[0], 1.0, 0.0)


def column_sums(value):
    return jnp.sum(value, axis=0, keepdims=True)


def top(bases, length, own, came, middle, cotangent, gains, blk):
    rows, dim = middle.shape

    def body(base_ref, length_ref, own_ref, came_ref, middle_ref, cot_ref, gain_ref, result_ref, grad_ref, sum_ref):
        gain = gain_ref[3:4, :].astype(F32)
        unit, scale = normalize(own_ref[...] + came_ref[...])
        result_ref[...] = (middle_ref[...] + unit * gain).astype(BF)
        upstream = upstream_of(base_ref, length_ref, cot_ref, blk)
        grad_ref[...] = norm_back(unit, scale, gain, upstream).astype(BF)

        @pl.when(pl.program_id(0) == 0)
        def _():
            sum_ref[...] = jnp.zeros_like(sum_ref)

        sum_ref[0:1, :] += column_sums(upstream * unit)

    row = pl.BlockSpec((blk, dim), lambda i: (i, 0))
    return pl.pallas_call(
        body,
        grid=(rows // blk,),
        in_specs=[SM, SM, row, row, row, row, pl.BlockSpec(gains.shape, lambda i: (0, 0))],
        out_specs=[row, row, pl.BlockSpec((8, dim), lambda i: (0, 0))],
        out_shape=[
            jax.ShapeDtypeStruct((rows, dim), BF),
            jax.ShapeDtypeStruct((rows, dim), BF),
            jax.ShapeDtypeStruct((8, dim), F32),
        ],
        compiler_params=pltpu.CompilerParams(vmem_limit_bytes=24 << 20),
        cost_estimate=pl.CostEstimate(flops=20 << 20, bytes_accessed=9 << 20, transcendentals=0),
        name="top",
    )(bases, length, own, came, middle, cotangent, gains)


def middle_back(q, bases, length, own, came, middle, branch, cotangent, gains, attn_w, last_sum, blk):
    rows, dim = middle.shape
    part = dim // 4
    pairs = part // PAIR
    steps = rows // blk

    def body(
        q_ref, base_ref, length_ref, own_ref, came_ref, middle_ref, branch_ref, cot_ref, gain_ref, weight_ref,
        last_ref, middle_out, branch_out, pieces_out, sums_out, attended, sums,
    ):
        i = pl.program_id(0)
        incoming = own_ref[...] + came_ref[...]
        unit, scale = normalize(middle_ref[...])
        grad_middle = upstream_of(base_ref, length_ref, cot_ref, blk) + norm_back(
            unit, scale, gain_ref[2:3, :].astype(F32), incoming
        )
        middle_out[...] = grad_middle
        sum2 = column_sums(incoming * unit)
        unit, scale = normalize(branch_ref[...])
        sum1 = column_sums(grad_middle * unit)
        grad_branch = norm_back(unit, scale, gain_ref[1:2, :].astype(F32), grad_middle).astype(BF)
        branch_out[...] = grad_branch
        attended[...] = mm_nt(grad_branch, weight_ref[...]).astype(BF)
        for g in range(4):
            at = lax.bitwise_xor(q_ref[0], g) * part
            for p in range(pairs):
                pieces_out[p, g] = attended[:, pl.ds(pl.multiple_of(at + p * PAIR, PAIR), PAIR)]

        @pl.when(i == 0)
        def _():
            sums[...] = jnp.zeros_like(sums)

        sums[0:1, :] += sum1
        sums[1:2, :] += sum2

        @pl.when(i == steps - 1)
        def _():
            sums[2:3, :] = last_ref[0:1, :]
            sums_out[...] = sums[...].astype(BF)

    row = pl.BlockSpec((blk, dim), lambda i: (i, 0))

    def whole(array):
        return pl.BlockSpec(array.shape, lambda i: (0, 0))

    return pl.pallas_call(
        body,
        grid=(steps,),
        in_specs=[SM, SM, SM, row, row, row, row, row, whole(gains), whole(attn_w), whole(last_sum)],
        out_specs=[
            row,
            row,
            pl.BlockSpec((pairs, 4, blk, PAIR), lambda i: (0, 0, i, 0)),
            pl.BlockSpec((EXTRA, dim), lambda i: (0, 0)),
        ],
        out_shape=[
            jax.ShapeDtypeStruct((rows, dim), F32),
            jax.ShapeDtypeStruct((rows, dim), BF),
            jax.ShapeDtypeStruct((pairs, 4, rows, PAIR), BF),
            jax.ShapeDtypeStruct((EXTRA, dim), BF),
        ],
        scratch_shapes=[pltpu.VMEM((blk, dim), BF), pltpu.VMEM((EXTRA, dim), F32)],
        compiler_params=pltpu.CompilerParams(vmem_limit_bytes=32 << 20),
        cost_estimate=pl.CostEstimate(
            flops=2 * rows * dim * dim, bytes_accessed=16 << 20, transcendentals=0
        ),
        name="middle_back",
    )(q[None], bases, length, own, came, middle, branch, cotangent, gains, attn_w, last_sum)


def bottom(own, from_core, from_x, hidden, grad_middle, gains, blk):
    rows, dim = hidden.shape

    def body(own_ref, core_ref, x_ref, hidden_ref, middle_ref, gain_ref, out_ref):
        incoming = own_ref[...] + core_ref[...].astype(F32) + x_ref[...].astype(F32)
        unit, scale = normalize(hidden_ref[...].astype(F32))
        out_ref[...] = middle_ref[...] + norm_back(
            unit, scale, gain_ref[0:1, :].astype(F32), incoming
        )

    row = pl.BlockSpec((blk, dim), lambda i: (i, 0))
    return pl.pallas_call(
        body,
        grid=(rows // blk,),
        in_specs=[row] * 5 + [pl.BlockSpec(gains.shape, lambda i: (0, 0))],
        out_specs=row,
        out_shape=jax.ShapeDtypeStruct((rows, dim), F32),
        compiler_params=pltpu.CompilerParams(vmem_limit_bytes=24 << 20),
        cost_estimate=pl.CostEstimate(flops=20 << 20, bytes_accessed=9 << 20, transcendentals=0),
        name="bottom",
    )(own, from_core, from_x, hidden, grad_middle, gains)


def up_end(c, mine, peer, shard, n, ff_half):
    wide = n * ff_half
    dim = wide // 2
    if ff_half % 128:
        mine, peer = [jnp.concatenate([v[:shard], v[shard:]], axis=1) for v in (mine, peer)]
        first, second = jnp.where(c == 0, mine, peer), jnp.where(c == 0, peer, mine)
        blocks = [v.reshape(shard, n, ff_half) for v in (first, second)]
        return jnp.stack(blocks, axis=2).reshape(shard, 2 * wide)

    def body(c_ref, mine_ref, peer_ref, up_ref):
        def put(first, second):
            for s in range(n):
                row, col = divmod(s * ff_half, dim)
                at = (slice(row * shard, (row + 1) * shard), slice(col, col + ff_half))
                up_ref[:, 2 * s * ff_half : (2 * s + 1) * ff_half] = first[at]
                up_ref[:, (2 * s + 1) * ff_half : (2 * s + 2) * ff_half] = second[at]

        @pl.when(c_ref[0] == 0)
        def _():
            put(mine_ref, peer_ref)

        @pl.when(c_ref[0] == 1)
        def _():
            put(peer_ref, mine_ref)

    return pl.pallas_call(
        body,
        in_specs=[SM, VM, VM],
        out_specs=VM,
        out_shape=jax.ShapeDtypeStruct((shard, 2 * wide), F32),
        compiler_params=pltpu.CompilerParams(vmem_limit_bytes=16 << 20),
        cost_estimate=SMALL,
        name="up_end",
    )(c[None], mine, peer)


def last_end(q, quarters, w_qkv, own_gains, late, part):
    shard, wide = w_qkv.shape
    pairs = part // PAIR
    dim = wide // 3

    def body(q_ref, quarters_ref, weight_ref, gain_ref, late_ref, out_ref, attn_ref, gains_ref):
        total = jnp.zeros((shard, PAIR), F32)
        for b in range(4):
            block = quarters_ref[lax.bitwise_xor(q_ref[0], b)][:shard].astype(F32)
            for p in range(pairs):
                for t in range(3):
                    at = t * dim + b * part + p * PAIR
                    value = block[:, (3 * p + t) * PAIR : (3 * p + t + 1) * PAIR]
                    out_ref[:, at : at + PAIR] = value
                    total = total + value * weight_ref[:, at : at + PAIR].astype(F32)
            attn_ref[:, b * part : (b + 1) * part] = block[:, 3 * part :]
        first = jnp.sum(total, axis=1, keepdims=True) / gain_ref[:, 0:1].astype(F32)
        lane = lax.broadcasted_iota(jnp.int32, (shard, 4), 1)
        gains_ref[...] = jnp.where(lane == 0, first, late_ref[...])

    return pl.pallas_call(
        body,
        in_specs=[SM] + [VM] * 4,
        out_specs=[VM] * 3,
        out_shape=[
            jax.ShapeDtypeStruct((shard, wide), F32),
            jax.ShapeDtypeStruct((shard, dim), F32),
            jax.ShapeDtypeStruct((shard, 4), F32),
        ],
        compiler_params=pltpu.CompilerParams(vmem_limit_bytes=16 << 20),
        cost_estimate=SMALL,
        name="last_end",
    )(q[None], quarters, w_qkv, own_gains, late)


def per_device(n, hidden_in, cotangent, lengths, block_of, w_qkv, w_attn, w_up, w_down, norm_gains):
    own_rows, dim = hidden_in.shape[1:]
    rows = 4 * own_rows
    blk = own_rows // 2
    ff = w_up.shape[1]
    shard = dim // n
    ff_half = ff // n // 2
    part = dim // 4
    pairs = part // PAIR
    q = lax.axis_index("ctx")
    c = lax.rem(q, 2)

    gain_rows = jnp.pad(norm_gains.T, ((0, EXTRA - 4), (0, 0)))
    bundle = bundle_up(q, w_qkv, w_attn, gain_rows, part)

    def store_bundle(target, owner, block):
        to_qkv, to_attn, to_gains = target
        return (
            lax.dynamic_update_slice(to_qkv, block[:shard, : 3 * part], (owner * shard, 0)),
            lax.dynamic_update_slice(to_attn, block[:shard, 3 * part :], (owner * shard, 0)),
            lax.dynamic_update_slice(to_gains, block[shard:, :shard], (0, owner * shard)),
        )

    def store_rows(target, owner, block):
        return lax.dynamic_update_slice(target, block, (owner * block.shape[0], 0))

    lead = Gather(
        bundle,
        n,
        False,
        store_bundle,
        (blank((dim, 3 * part), BF), blank((dim, part), BF), blank((EXTRA, dim), BF)),
    )
    mlp_own = mlp_half(c, w_up, w_down, n)
    bases = lax.dynamic_slice_in_dim(block_of, q, 1, 0)[0]
    tables = rotary_tables(blk, 8)
    hidden_b = hidden_in[0]

    hidden_all = lax.dynamic_update_slice(blank((rows, dim), BF), hidden_b, (0, 0))
    hidden_x = swap(hidden_b, 2)
    came, hidden_c = tie(lead.send(), swap(hidden_b, 1))
    lead.land(came)
    hidden_all = lax.dynamic_update_slice(hidden_all, hidden_c, (own_rows, 0))
    came, mlp_own = tie(lead.send(), mlp_own)
    lead.land(came)
    came, hidden_x = tie(lead.send(), hidden_x)
    lead.land(came)
    hidden_all = lax.dynamic_update_slice(hidden_all, hidden_x, (2 * own_rows, 0))
    mlp = MergedGather(
        mlp_own, n, blank((dim, n * ff_half), BF), blank((n * ff_half, dim), BF)
    )
    came, hidden_d, mlp.blocks, mlp.targets = tie(
        lead.send(), swap(hidden_x, 1), mlp.blocks, mlp.targets
    )
    hidden_all = lax.dynamic_update_slice(hidden_all, hidden_d, (3 * own_rows, 0))
    lead.land(came)
    qkv_w, attn_q, gains = lead.rest()

    normed, *qkv = project(q, block_of, hidden_all, qkv_w, gains, tables, blk)
    att, lse = attention(q, block_of, lengths, qkv, blk)
    came_mlp, attn_x, att, attn_q, mlp.targets = tie(
        mlp.send(), swap(attn_q, 2), att, attn_q, mlp.targets
    )
    mlp.land(came_mlp)

    half_rows = rows // 2
    from_x = swap(jnp.stack([a[half_rows:] for a in att]), 2)
    from_core = swap(
        jnp.stack(
            [
                jnp.concatenate([a[own_rows:half_rows], from_x[p, own_rows:]], axis=0)
                for p, a in enumerate(att)
            ]
        ),
        1,
    )
    attn_c = swap(jnp.stack([attn_q, attn_x]), 1)
    came_mlp, from_x, from_core, att, attn_x, attn_q, attn_c, mlp.targets = tie(
        mlp.send(), from_x, from_core, att, attn_x, attn_q, attn_c, mlp.targets
    )
    mlp.land(came_mlp)
    attn_parts = jnp.stack([attn_q, attn_c[0], attn_x, attn_c[1]])
    attn_w = jnp.concatenate(
        [
            lax.dynamic_index_in_dim(attn_parts, lax.bitwise_xor(q, b), 0, keepdims=False)
            for b in range(4)
        ],
        axis=1,
    )

    attended, branch, middle, normed_mid = attention_end(
        q, [a[:own_rows] for a in att], from_core, from_x, attn_w, hidden_b, gains, blk
    )
    came_mlp, normed_mid, normed_mid_c, mlp.targets = tie(
        mlp.send(), normed_mid, swap(normed_mid, 1), mlp.targets
    )
    mlp.land(came_mlp)

    came_mlp, normed_mid, normed_mid_c, mlp.targets = tie(
        mlp.send(), normed_mid, normed_mid_c, mlp.targets
    )
    mlp.land(came_mlp)
    normed_mid2 = jnp.concatenate([normed_mid, normed_mid_c], axis=0)
    up_w, down_w = mlp.rest()
    lifted = mm(normed_mid2, up_w)
    activated, slope = [v.astype(BF) for v in gelu_both(lifted)]
    lowered_c = swap(mm(activated[own_rows:], down_w), 1)
    lowered = mm(activated[:own_rows], down_w)
    result, grad_lowered, last_sum = top(
        bases, lengths, lowered, lowered_c, middle, cotangent[0], gains, blk
    )

    grad_lowered2 = jnp.concatenate([grad_lowered, swap(grad_lowered, 1)], axis=0)
    x = lax.div(q, 2)
    down_g = mm_tn(activated, grad_lowered2).astype(BF)
    grad_lifted = lifted_back(grad_lowered2, down_w, slope)
    up_g = mm_tn(normed_mid2, grad_lifted).astype(BF)
    mlp_ring = MergedScatter(up_g, down_g, n)
    mlp_ring.blocks, grad_lifted = tie(mlp_ring.blocks, grad_lifted)

    grad_normed_mid_c = swap(mm_nt(grad_lifted[own_rows:], up_w), 1)
    grad_normed_mid = mm_nt(grad_lifted[:own_rows], up_w)
    grad_middle, grad_branch, pieces, sums = middle_back(
        q, bases, lengths, grad_normed_mid, grad_normed_mid_c, middle, branch, cotangent[0], gains,
        attn_w, last_sum, blk,
    )
    came_mlp, grad_branch, pieces = tie(mlp_ring.send(), grad_branch, pieces)
    mlp_ring.land(came_mlp)

    pieces = pieces.reshape(pairs, rows, PAIR)
    went_x = swap(pieces[:, half_rows:], 2)
    went_core = swap(
        jnp.concatenate([pieces[:, own_rows:half_rows], went_x[:, own_rows:]], axis=1), 1
    )
    attn_g = mm_tn(attended, grad_branch).astype(BF)
    half_cols = dim // 2
    attn_cols = jnp.concatenate(
        [attn_g[:, b * part : (b + 1) * part] for b in (0, 2, 1, 3)], axis=1
    )
    attn_own = lax.dynamic_slice_in_dim(attn_cols, c * half_cols, half_cols, 1)
    attn_came = swap(lax.dynamic_slice_in_dim(attn_cols, (1 - c) * half_cols, half_cols, 1), 1)
    came_mlp, went_x, went_core, pieces, attn_own, attn_came = tie(
        mlp_ring.send(), went_x, went_core, pieces, attn_own, attn_came
    )
    mlp_ring.land(came_mlp)
    grad_out = jnp.concatenate(
        [pieces[:, :own_rows], went_core[:, :own_rows], went_x[:, :own_rows], went_core[:, own_rows:]],
        axis=1,
    )
    attn_half = (attn_own.astype(F32) + attn_came.astype(F32)).astype(BF)

    def back(p):
        return attention_back(
            q, block_of, lengths, qkv[p], grad_out[p], att[p], lse[p], tables, blk
        )

    attn_x_own = lax.dynamic_slice_in_dim(attn_half, x * part, part, 1)
    attn_x_other = lax.dynamic_slice_in_dim(attn_half, (1 - x) * part, part, 1)
    mixed = [back(0)]
    attn_came, came_mlp, mixed, grad_out, attn_x_own = tie(
        swap(attn_x_other, 2), mlp_ring.send(), mixed, grad_out, attn_x_own
    )
    mlp_ring.land(came_mlp)
    attn_g = (attn_x_own.astype(F32) + attn_came.astype(F32)).astype(BF)

    mixed.append(back(1))
    came_mlp, mixed, attn_g = tie(mlp_ring.send(), mixed, attn_g)
    mlp_ring.land(came_mlp)
    mlp_sum = mlp_ring.rest()
    up_sum, down_sum = mlp_sum[: 2 * shard], mlp_sum[2 * shard :]

    def normed_back(g):
        at = slice(g * own_rows, (g + 1) * own_rows)
        wide = 3 * PAIR
        return sum(mm_nt(mixed[p][at], qkv_w[:, p * wide : (p + 1) * wide]) for p in range(pairs))

    qkv_g = jnp.concatenate([mm_tn(normed, m).astype(BF) for m in mixed], axis=1)
    to_core = jnp.concatenate([normed_back(1).astype(BF), normed_back(3).astype(BF)], axis=0)
    up_x, mixed, qkv_g, to_core, attn_g, up_sum, down_sum = tie(
        swap(up_sum, 2), mixed, qkv_g, to_core, attn_g, up_sum, down_sum
    )
    up_sum = up_sum.astype(F32) + up_x.astype(F32)

    last_ring = Scatter(last_pick(qkv_g, attn_g, sums, shard), n, False)
    came_last, came_core, down_x, own_part, for_x, up_sum, down_sum = tie(
        last_ring.send(),
        swap(to_core, 1),
        swap(down_sum, 2),
        normed_back(0),
        normed_back(2),
        up_sum,
        down_sum,
    )
    last_ring.land(came_last)
    for_x = (for_x + came_core[own_rows:].astype(F32)).astype(BF)
    down_sum = down_sum.astype(F32) + down_x.astype(F32)

    quarter = own_rows // 2
    came_last, from_x0, mlp_c, up_sum, down_sum, for_x = tie(
        last_ring.send(),
        swap(for_x[:quarter], 2),
        swap(jnp.concatenate([up_sum, down_sum], axis=0), 1),
        up_sum,
        down_sum,
        for_x,
    )
    last_ring.land(came_last)
    up_out = up_end(c, up_sum, mlp_c[: 2 * shard], shard, n, ff_half)
    down_c = mlp_c[2 * shard :]
    down_out = jnp.concatenate(
        [jnp.where(c == 0, down_sum, down_c), jnp.where(c == 0, down_c, down_sum)], axis=0
    )
    came_last, from_x1, up_out, down_out = tie(
        last_ring.send(), swap(for_x[quarter:], 2), up_out, down_out
    )
    last_ring.land(came_last)
    input_grad = bottom(
        own_part, came_core[:own_rows], jnp.concatenate([from_x0, from_x1], axis=0), hidden_b, grad_middle, gains, blk
    )

    came_last, input_grad = tie(last_ring.send(), input_grad)
    last_ring.land(came_last)
    last = last_ring.rest()

    last_x, last = tie(swap(last, 2), last)
    last_pair = jnp.stack([last, last_x])
    last_c, last_pair = tie(swap(last_pair, 1), last_pair)
    last_all = jnp.stack([last_pair[0], last_c[0], last_pair[1], last_c[1]])
    me = lax.axis_index("fsdp")
    late = lax.dynamic_slice(last_all, (0, shard, me * shard), (4, 4, shard)).astype(F32)
    late = (
        lax.dynamic_index_in_dim(late, q, 0, keepdims=False)
        + lax.dynamic_index_in_dim(late, lax.bitwise_xor(q, 1), 0, keepdims=False)
    ) + (
        lax.dynamic_index_in_dim(late, lax.bitwise_xor(q, 2), 0, keepdims=False)
        + lax.dynamic_index_in_dim(late, lax.bitwise_xor(q, 3), 0, keepdims=False)
    )
    late = jnp.roll(late, 1, axis=0).T
    qkv_out, attn_out, gains_out = last_end(q, last_all, w_qkv, norm_gains, late, part)
    return (
        result[None],
        input_grad[None],
        qkv_out,
        attn_out,
        up_out,
        down_out,
        gains_out,
    )


def solution(mesh):
    n = mesh.shape["fsdp"]

    def step(*args):
        return per_device(n, *args)

    rows = P("fsdp", "ctx", None)
    weight = P("fsdp", None)
    return jax.shard_map(
        step,
        mesh=mesh,
        in_specs=(rows, rows, P("fsdp"), P()) + (weight,) * 5,
        out_specs=(rows, rows) + (weight,) * 5,
        check_vma=False,
    )
```

```python
import math

import jax
import jax.numpy as jnp
import numpy as np
from jax import lax
from jax.experimental import pallas as pl
from jax.experimental.pallas import tpu as pltpu
from jax.sharding import PartitionSpec as P

HEAD_DIM = 64
PAIR = 2 * HEAD_DIM
EXTRA = 16
BF = jnp.bfloat16
F32 = jnp.float32
NEG = -1e30
EPS = 1e-05
VM = pl.BlockSpec(memory_space=pltpu.VMEM)
SM = pl.BlockSpec(memory_space=pltpu.SMEM)
SMALL = pl.CostEstimate(flops=1 << 10, bytes_accessed=1 << 10, transcendentals=0)


def mm(left, right):
    return jnp.dot(left, right, preferred_element_type=F32)


def mm_tn(left, right):
    return lax.dot_general(left, right, (((0,), (0,)), ((), ())), preferred_element_type=F32)


def mm_nt(left, right):
    return lax.dot_general(left, right, (((1,), (1,)), ((), ())), preferred_element_type=F32)


def swap(value, bit):
    return lax.ppermute(value, "ctx", [(i, i ^ bit) for i in range(4)])


def blank(shape, dtype):
    return pl.pallas_call(
        lambda out_ref: None,
        out_specs=pl.BlockSpec(memory_space=pl.ANY),
        out_shape=jax.ShapeDtypeStruct(shape, dtype),
        name="blank",
    )()


def ring_pairs(n):
    order = list(range(0, n, 2)) + list(range(n - 1, 0, -2))
    ahead = [(order[i], order[(i + 1) % n]) for i in range(n)]
    return ahead, [(b, a) for a, b in ahead]


def ring_owner(place, n):
    place = lax.rem(place + 2 * n, n)
    return jnp.where(place < n // 2, 2 * place, 2 * (n - place) - 1)


def ring_place(me, n):
    return jnp.where(lax.rem(me, 2) == 0, lax.div(me, 2), n - 1 - lax.div(me, 2))


HBM = pl.BlockSpec(memory_space=pltpu.HBM)


def in_hbm(array):
    return pltpu.with_memory_space_constraint(array, pltpu.HBM)


def tie(*trees):
    return lax.optimization_barrier(trees)


class Gather:
    def __init__(self, block, n, flip, store, target):
        self.ahead, self.back = ring_pairs(n)
        self.sign = -1
        if flip:
            self.ahead, self.back, self.sign = self.back, self.ahead, 1
        me = lax.axis_index("fsdp")
        self.n, self.place, self.count = n, ring_place(me, n), 0
        self.store, self.blocks = store, [block, block]
        self.target = store(target, me, block)

    def more(self):
        return self.count < self.n // 2

    def send(self):
        self.count += 1
        sent = [lax.ppermute(self.blocks[0], "fsdp", self.ahead)]
        if self.count <= (self.n - 1) // 2:
            sent.append(lax.ppermute(self.blocks[1], "fsdp", self.back))
        return sent

    def land(self, came):
        self.blocks = came
        for block, sign in zip(came, (self.sign, -self.sign)):
            owner = ring_owner(self.place + sign * self.count, self.n)
            self.target = self.store(self.target, owner, block)

    def rest(self):
        while self.more():
            self.land(tie(self.send())[0])
        return self.target


class Scatter:
    def __init__(self, pick, n, flip):
        self.ahead, self.back = ring_pairs(n)
        self.sign = 1
        if flip:
            self.ahead, self.back, self.sign = self.back, self.ahead, -1
        self.place = ring_place(lax.axis_index("fsdp"), n)
        self.n, self.pick, self.count = n, pick, 0
        self.blocks = [self.at(self.sign * (n // 2)), self.at(-self.sign * ((n - 1) // 2))]

    def at(self, offset, *blocks):
        return self.pick(offset, ring_owner(self.place + offset, self.n), *blocks)

    def more(self):
        return self.count < self.n // 2

    def send(self):
        self.count += 1
        sent = [lax.ppermute(self.blocks[0], "fsdp", self.ahead)]
        if self.count <= (self.n - 1) // 2:
            sent.append(lax.ppermute(self.blocks[1], "fsdp", self.back))
        return sent

    def land(self, came):
        one, two = self.n // 2 - self.count, (self.n - 1) // 2 - self.count
        if one > 0:
            self.blocks[0] = self.at(self.sign * one, came[0])
            if two > 0:
                self.blocks[1] = self.at(-self.sign * two, came[1])
            elif len(came) > 1:
                self.blocks[1] = came[1]
        else:
            self.total = self.at(0, came[0], came[1] if len(came) > 1 else self.blocks[1])

    def rest(self):
        while self.more():
            self.land(tie(self.send())[0])
        return self.total


def rows_of(array, size):
    def pick(offset, owner, *blocks):
        value = lax.dynamic_slice_in_dim(array, owner * size, size, 0)
        if not blocks:
            return value
        value = value.astype(F32)
        for block in blocks:
            value = value + block.astype(F32)
        return value.astype(BF)

    return pick


class MergedGather:
    def __init__(self, block, n, up_w, down_w):
        self.ahead, self.back = ring_pairs(n)
        me = lax.axis_index("fsdp")
        self.n, self.place, self.count = n, ring_place(me, n), 0
        self.half = block.shape[0] // 2
        self.blocks = [block, block]
        self.targets = [up_w, down_w]
        self.store([me, me], [block, block], [0])

    def store(self, owners, blocks, which):
        shard = self.half // 2
        dim = blocks[0].shape[1]

        def body(owners_ref, *refs):
            block_refs, (up_ref, down_ref) = refs[: len(blocks)], refs[len(blocks) + 2 :]

            def put(up_from, down_from):
                up_ref[:, :dim] = up_from[:shard, :]
                up_ref[:, dim:] = up_from[shard : 2 * shard, :]
                down_ref[...] = down_from[down_from.shape[0] - 2 * shard :, :]

            if len(which) == 1:
                put(*block_refs)
            else:
                for k in which:

                    @pl.when(pl.program_id(0) == k)
                    def _(k=k):
                        put(block_refs[k], block_refs[k])

        def whole(array):
            return pl.BlockSpec(array.shape, lambda i, o: (0, 0))

        self.targets = pl.pallas_call(
            body,
            grid_spec=pltpu.PrefetchScalarGridSpec(
                num_scalar_prefetch=1,
                grid=(len(which),),
                in_specs=[whole(b) for b in blocks] + [HBM, HBM],
                out_specs=[
                    pl.BlockSpec((shard, 2 * dim), lambda i, o: (o[i], 0)),
                    pl.BlockSpec((2 * shard, dim), lambda i, o: (o[i], 0)),
                ],
            ),
            out_shape=[pltpu.HBM(t.shape, t.dtype) for t in self.targets],
            input_output_aliases={1 + len(blocks): 0, 2 + len(blocks): 1},
            compiler_params=pltpu.CompilerParams(vmem_limit_bytes=16 << 20),
            cost_estimate=SMALL,
            name="store",
        )(jnp.stack(owners), *blocks, *self.targets)

    def more(self):
        return self.count < self.n // 2

    def send(self):
        self.count += 1
        one, two = self.blocks
        if not self.more():
            one, two = one[: self.half], two[self.half :]
        return [lax.ppermute(one, "fsdp", self.ahead), lax.ppermute(two, "fsdp", self.back)]

    def land(self, came):
        self.blocks = came
        owners = [ring_owner(self.place + sign * self.count, self.n) for sign in (-1, 1)]
        self.store(owners, came, [0, 1] if self.more() else [0])

    def rest(self):
        while self.more():
            self.land(tie(self.send())[0])
        return self.targets


class MergedScatter:
    def __init__(self, up_g, down_g, n):
        self.ahead, self.back = ring_pairs(n)
        self.place = ring_place(lax.axis_index("fsdp"), n)
        self.n, self.count, self.addends = n, 0, (up_g, down_g)
        self.half = 2 * up_g.shape[0] // n
        far = self.pick(n // 2, [])
        self.blocks = [far[: self.half], far[self.half :]]

    def pick(self, offset, adds):
        up_g, down_g = self.addends
        shard, dim = up_g.shape[0] // self.n, down_g.shape[1]
        half = self.half

        def body(owner_ref, up_ref, down_ref, *refs):
            out_ref = refs[-1]

            def put(start, size, value):
                value = value.astype(F32)
                for (first, block), ref in zip(adds, refs[:-1]):
                    if first <= start < first + block.shape[0]:
                        value = value + ref[start - first : start - first + size, :].astype(F32)
                out_ref[start : start + size, :] = value.astype(BF)

            put(0, shard, up_ref[:, :dim])
            put(shard, shard, up_ref[:, dim:])
            put(half, half, down_ref[...])

        return pl.pallas_call(
            body,
            grid_spec=pltpu.PrefetchScalarGridSpec(
                num_scalar_prefetch=1,
                grid=(1,),
                in_specs=[
                    pl.BlockSpec((shard, 2 * dim), lambda i, o: (o[0], 0)),
                    pl.BlockSpec((half, dim), lambda i, o: (o[0], 0)),
                ]
                + [pl.BlockSpec(b.shape, lambda i, o: (0, 0)) for _, b in adds],
                out_specs=pl.BlockSpec((2 * half, dim), lambda i, o: (0, 0)),
            ),
            out_shape=jax.ShapeDtypeStruct((2 * half, dim), BF),
            compiler_params=pltpu.CompilerParams(vmem_limit_bytes=16 << 20),
            cost_estimate=SMALL,
            name="merged_pick",
        )(ring_owner(self.place + offset, self.n)[None], up_g, down_g, *[b for _, b in adds])

    def more(self):
        return self.count < self.n // 2

    def send(self):
        self.count += 1
        return [
            lax.ppermute(self.blocks[0], "fsdp", self.ahead),
            lax.ppermute(self.blocks[1], "fsdp", self.back),
        ]

    def land(self, came):
        starts = (0, self.half) if self.count == 1 else (0, 0)
        if self.more():
            left = self.n // 2 - self.count
            self.blocks = [
                self.pick(sign * left, [(start, block)])
                for sign, start, block in zip((1, -1), starts, came)
            ]
        else:
            self.total = self.pick(0, list(zip(starts, came)))

    def rest(self):
        while self.more():
            self.land(tie(self.send())[0])
        return self.total


def last_pick(wide_g, narrow_g, sums, rows):
    wide, narrow = wide_g.shape[1], narrow_g.shape[1]

    def pick(offset, owner, *blocks):
        def body(owner_ref, wide_ref, narrow_ref, sums_ref, *refs):
            out_ref = refs[-1]

            def put(at_rows, at_cols, value):
                value = value.astype(F32)
                for ref in refs[:-1]:
                    value = value + ref[at_rows, at_cols].astype(F32)
                out_ref[at_rows, at_cols] = value.astype(BF)

            upper, lower = slice(0, rows), slice(rows, rows + EXTRA)
            put(upper, slice(0, wide), wide_ref[...])
            put(upper, slice(wide, wide + narrow), narrow_ref[...])
            put(lower, slice(0, wide + narrow), sums_ref[...])

        whole = pl.BlockSpec((rows + EXTRA, wide + narrow), lambda i, o: (0, 0))
        return pl.pallas_call(
            body,
            grid_spec=pltpu.PrefetchScalarGridSpec(
                num_scalar_prefetch=1,
                grid=(1,),
                in_specs=[
                    pl.BlockSpec((rows, wide), lambda i, o: (o[0], 0)),
                    pl.BlockSpec((rows, narrow), lambda i, o: (o[0], 0)),
                    pl.BlockSpec(sums.shape, lambda i, o: (0, 0)),
                ]
                + [whole] * len(blocks),
                out_specs=whole,
            ),
            out_shape=jax.ShapeDtypeStruct((rows + EXTRA, wide + narrow), BF),
            compiler_params=pltpu.CompilerParams(vmem_limit_bytes=8 << 20),
            cost_estimate=SMALL,
            name="last_pick",
        )(owner[None], wide_g, narrow_g, sums, *blocks)

    return pick


def normalize(values):
    average = jnp.mean(values, axis=-1, keepdims=True)
    centered = values - average
    variance = jnp.mean(centered * centered, axis=-1, keepdims=True)
    scale = lax.rsqrt(variance + EPS)
    return centered * scale, scale


def norm_back(unit, scale, gain, incoming):
    weighted = incoming * gain
    return (
        weighted
        - jnp.mean(weighted, axis=-1, keepdims=True)
        - unit * jnp.mean(weighted * unit, axis=-1, keepdims=True)
    ) * scale


def turned(value, cosine, sine_signed, inverse):
    width = value.shape[1]
    lane = lax.broadcasted_iota(jnp.int32, value.shape, 1)
    half = HEAD_DIM // 2
    other = jnp.where(
        lax.rem(lane, HEAD_DIM) < half,
        pltpu.roll(value, width - half, 1),
        pltpu.roll(value, half, 1),
    )
    repeat = width // cosine.shape[1]
    cosine = jnp.concatenate([cosine] * repeat, axis=1)
    sine_signed = jnp.concatenate([sine_signed] * repeat, axis=1)
    if inverse:
        return value * cosine - other * sine_signed
    return value * cosine + other * sine_signed


def block_at(q_ref, block_ref, k):
    return block_ref[lax.bitwise_xor(q_ref[0], lax.div(k, 2)), lax.rem(k, 2)]


def fill_order(order, q_ref, block_ref, count):
    def put(k, carry):
        order[block_at(q_ref, block_ref, k)] = k
        return carry

    lax.fori_loop(0, count, put, 0)


def rotary_tables(blk, count):
    lane = np.arange(PAIR)
    half = HEAD_DIM // 2
    inverse = np.exp(-2.0 * math.log(10000.0) / HEAD_DIM * (lane % half))
    sign = np.where(lane % HEAD_DIM < half, -1.0, 1.0)
    inside = np.arange(blk)[:, None] * inverse[None, :]
    starts = np.arange(count)[:, None] * blk * inverse[None, :]
    return [
        jnp.asarray(v, F32)
        for v in (np.cos(inside), np.sin(inside) * sign, np.cos(starts), np.sin(starts) * sign)
    ]


def tables_at(table_refs, block):
    cos_in, sin_in, cos_at, sin_at = table_refs
    cos_b, sin_b = cos_at[pl.ds(block, 1), :], sin_at[pl.ds(block, 1), :]
    cos_r, sin_r = cos_in[...], sin_in[...]
    return cos_r * cos_b - sin_r * sin_b, sin_r * cos_b + cos_r * sin_b


def project(q, block_of, hidden, weight, gains, tables, blk):
    rows, dim = hidden.shape
    width = weight.shape[1]
    pairs = width // (3 * PAIR)
    step = 2 * blk

    def body(q_ref, block_ref, hidden_ref, weight_ref, gain_ref, *refs):
        table_refs, normed_ref, out_refs = refs[:4], refs[4], refs[5:]
        unit, _ = normalize(hidden_ref[...].astype(F32))
        normed = (unit * gain_ref[0:1, :].astype(F32)).astype(BF)
        normed_ref[...] = normed
        mixed = mm(normed, weight_ref[...])
        halves = [
            tables_at(table_refs, block_at(q_ref, block_ref, 2 * pl.program_id(0) + k))
            for k in range(2)
        ]
        cos_part, sin_part = [jnp.concatenate(v, axis=0) for v in zip(*halves)]
        for p, out_ref in enumerate(out_refs):
            at = 3 * PAIR * p
            queries = turned(mixed[:, at : at + PAIR], cos_part, sin_part, False)
            out_ref[:, :PAIR] = (queries * (0.125 * math.log2(math.e))).astype(BF)
            out_ref[:, PAIR : 2 * PAIR] = turned(
                mixed[:, at + PAIR : at + 2 * PAIR], cos_part, sin_part, False
            ).astype(BF)
            out_ref[:, 2 * PAIR :] = mixed[:, at + 2 * PAIR : at + 3 * PAIR].astype(BF)

    def whole(array):
        return pl.BlockSpec(array.shape, lambda i: (0, 0))

    return pl.pallas_call(
        body,
        grid=(rows // step,),
        in_specs=[SM, SM, pl.BlockSpec((step, dim), lambda i: (i, 0)), whole(weight), whole(gains)]
        + [whole(t) for t in tables],
        out_specs=[pl.BlockSpec((step, dim), lambda i: (i, 0))]
        + [pl.BlockSpec((step, 3 * PAIR), lambda i: (i, 0))] * pairs,
        out_shape=[jax.ShapeDtypeStruct((rows, dim), BF)]
        + [jax.ShapeDtypeStruct((rows, 3 * PAIR), BF)] * pairs,
        compiler_params=pltpu.CompilerParams(vmem_limit_bytes=32 << 20),
        cost_estimate=pl.CostEstimate(
            flops=2 * rows * dim * width, bytes_accessed=12 << 20, transcendentals=rows
        ),
        name="project",
    )(q[None], block_of, in_hbm(hidden), weight, gains, *tables)


def folded(value, op):
    rows, cols = value.shape
    return op(value.reshape(rows // 8, 8, cols), axis=0)


def head_columns(target, p, value_t, heads):
    for h in range(heads):
        at = slice(h * HEAD_DIM, (h + 1) * HEAD_DIM)
        if h:
            target[p, h, : h * HEAD_DIM, :] = jnp.zeros((h * HEAD_DIM, value_t.shape[1]), BF)
        target[p, h, at, :] = value_t[at, :]
        rest = (heads - 1 - h) * HEAD_DIM
        if rest:
            target[p, h, (h + 1) * HEAD_DIM :, :] = jnp.zeros((rest, value_t.shape[1]), BF)


def tile_mask(i, j, live, blk):
    key = j * blk + lax.broadcasted_iota(jnp.int32, (blk, blk), 0)
    query = i * blk + lax.broadcasted_iota(jnp.int32, (blk, blk), 1)
    return (key <= query) & (key < live)


def open_tiles(edge, nb):
    return sum(jnp.minimum(i, edge) for i in range(nb))


def next_open(i, j, edge, nb):
    end = j + 1 >= jnp.minimum(i, edge)
    return jnp.minimum(jnp.where(end, i + 1, i), nb - 1), jnp.where(end, 0, j + 1)


def attention(q, block_of, length, qkv, blk):
    rows = qkv[0].shape[0]
    pairs = len(qkv)
    width = pairs * PAIR
    heads = width // HEAD_DIM
    nb = rows // blk

    def body(
        q_ref, block_ref, length_ref, *refs,
    ):
        qkv_refs, out_refs, lse_refs = refs[:pairs], refs[pairs : 2 * pairs], refs[2 * pairs : 3 * pairs]
        (keys, values_t, q_cols, even, odd, even_top, odd_top, total, tops, sums, order_ref) = refs[3 * pairs :]
        fill_order(order_ref, q_ref, block_ref, nb)
        live = length_ref[0]
        edge = lax.div(live, blk)

        def fill(p, carry):
            rows_at = pl.ds(pl.multiple_of(order_ref[p] * blk, blk), blk)
            keys[p] = jnp.concatenate([r[rows_at, PAIR : 2 * PAIR] for r in qkv_refs], axis=1)
            values_t[p] = jnp.transpose(
                jnp.concatenate([r[rows_at, 2 * PAIR :] for r in qkv_refs], axis=1)
            )
            queries = jnp.concatenate([r[rows_at, :PAIR] for r in qkv_refs], axis=1)
            head_columns(q_cols, p, jnp.transpose(queries), heads)
            return carry

        lax.fori_loop(0, nb, fill, 0)

        def ahead(i, j, into, top, masks):
            key_block = keys[j]
            for h in range(heads):
                s = mm(key_block, q_cols[i, h])
                if masks:
                    s = jnp.where(tile_mask(i, j, live, blk), s, NEG)
                into[h] = s
                top[h] = folded(s, jnp.max)

        def work(i, j, scores, top, first):
            for h in range(heads):
                new = jnp.broadcast_to(jnp.max(top[h], axis=0, keepdims=True), (8, blk))
                if not first:
                    old = tops[i, h]
                    new = jnp.maximum(old, new)
                    shrink = jnp.exp2(old - new)
                tops[i, h] = new
                p = jnp.exp2(scores[h] - new[0:1])
                added = folded(p, jnp.sum)
                sums[i, h] = added if first else sums[i, h] * shrink + added
                at = slice(h * HEAD_DIM, (h + 1) * HEAD_DIM)
                product = mm(values_t[j, at, :], p.astype(BF))
                total[i, at, :] = product if first else total[i, at, :] * shrink[0:1] + product

        ahead(0, 0, even, even_top, True)

        def masked_pair(t, carry):
            i0 = 2 * t
            i1 = i0 + 1
            i2 = jnp.minimum(i0 + 2, nb - 1)
            ahead(i1, jnp.minimum(i1, edge), odd, odd_top, True)
            work(i0, jnp.minimum(i0, edge), even, even_top, True)
            ahead(i2, jnp.minimum(i2, edge), even, even_top, True)
            work(i1, jnp.minimum(i1, edge), odd, odd_top, True)
            return carry

        lax.fori_loop(0, nb // 2, masked_pair, 0)

        ahead(1, 0, even, even_top, False)

        def pair(t, place):
            i0, j0 = place
            i1, j1 = next_open(i0, j0, edge, nb)
            ahead(i1, j1, odd, odd_top, False)
            work(i0, j0, even, even_top, False)
            i2, j2 = next_open(i1, j1, edge, nb)
            ahead(i2, j2, even, even_top, False)
            work(i1, j1, odd, odd_top, False)
            return (i2, j2)

        count = open_tiles(edge, nb)
        i_last, j_last = lax.fori_loop(0, lax.div(count, 2), pair, (jnp.int32(1), jnp.int32(0)))

        @pl.when(lax.rem(count, 2) == 1)
        def _():
            work(i_last, j_last, even, even_top, False)

        def drain(p, carry):
            rows_at = pl.ds(pl.multiple_of(order_ref[p] * blk, blk), blk)
            scaled = []
            for h in range(heads):
                sum_h = jnp.sum(sums[p, h], axis=0, keepdims=True)
                lse_refs[h // 2][p, h % 2 : h % 2 + 1, :] = tops[p, h][0:1] + jnp.log2(sum_h)
                scaled.append((total[p, h * HEAD_DIM : (h + 1) * HEAD_DIM, :] * (1.0 / sum_h)).astype(BF))
            both = jnp.transpose(jnp.concatenate(scaled, axis=0))
            for k, ref in enumerate(out_refs):
                ref[rows_at, :] = both[:, k * PAIR : (k + 1) * PAIR]
            return carry

        lax.fori_loop(0, nb, drain, 0)

    vm = pl.BlockSpec(memory_space=pltpu.VMEM)
    sm = pl.BlockSpec(memory_space=pltpu.SMEM)
    result = pl.pallas_call(
        body,
        in_specs=[sm, sm, sm] + [vm] * pairs,
        out_specs=[vm] * (2 * pairs),
        out_shape=[jax.ShapeDtypeStruct((rows, PAIR), BF)] * pairs
        + [jax.ShapeDtypeStruct((nb, 8, blk), F32)] * pairs,
        scratch_shapes=[
            pltpu.VMEM((nb, blk, width), BF),
            pltpu.VMEM((nb, width, blk), BF),
            pltpu.VMEM((nb, heads, width, blk), BF),
            pltpu.VMEM((heads, blk, blk), F32),
            pltpu.VMEM((heads, blk, blk), F32),
            pltpu.VMEM((heads, 8, blk), F32),
            pltpu.VMEM((heads, 8, blk), F32),
            pltpu.VMEM((nb, width, blk), F32),
            pltpu.VMEM((nb, heads, 8, blk), F32),
            pltpu.VMEM((nb, heads, 8, blk), F32),
            pltpu.SMEM((nb,), jnp.int32),
        ],
        compiler_params=pltpu.CompilerParams(vmem_limit_bytes=24 << 20),
        cost_estimate=pl.CostEstimate(
            flops=heads * 4500000000, bytes_accessed=3 << 20, transcendentals=heads << 21
        ),
        name="attention",
    )(q[None], block_of, length, *qkv)
    return result[:pairs], result[pairs:]


def attention_back(q, block_of, length, qkv, grad_out, out, lse, tables, blk):
    rows = qkv.shape[0]
    width = qkv.shape[1] // 3
    heads = width // HEAD_DIM
    nb = rows // blk

    def body(
        q_ref, block_ref, length_ref, qkv_ref, gout_ref, att_ref, lse_ref, cos_in, sin_in, cos_at, sin_at, result_ref,
        keys, keys_t, values, q_cols, q_rows, g_cols, g_rows, grad_q, grad_k, grad_v, inner,
        even_p, even_d, odd_p, odd_d, order_ref,
    ):
        fill_order(order_ref, q_ref, block_ref, nb)
        live = length_ref[0]
        edge = lax.div(live, blk)
        lane_head = lax.div(lax.broadcasted_iota(jnp.int32, (1, width), 1), HEAD_DIM)
        picks = [jnp.where(lane_head == h, 1.0, 0.0).astype(BF) for h in range(heads)]

        def fill(p, carry):
            rows_at = pl.ds(pl.multiple_of(order_ref[p] * blk, blk), blk)
            key_block = qkv_ref[rows_at, width : 2 * width]
            keys[p] = key_block
            keys_t[p] = jnp.transpose(key_block)
            values[p] = qkv_ref[rows_at, 2 * width :]
            grad_k[p] = jnp.zeros((blk, width), F32)
            grad_v[p] = jnp.zeros((blk, width), F32)
            query = qkv_ref[rows_at, :width]
            gout = gout_ref[rows_at, :]
            inner_t = jnp.transpose(gout.astype(F32) * att_ref[rows_at, :].astype(F32))
            head_columns(q_cols, p, jnp.transpose(query), heads)
            head_columns(g_cols, p, jnp.transpose(gout), heads)
            for h in range(heads):
                at = slice(h * blk, (h + 1) * blk)
                q_rows[p, at, :] = query * picks[h]
                g_rows[p, at, :] = gout * picks[h]
                inner[p, h : h + 1, :] = jnp.sum(
                    inner_t[h * HEAD_DIM : (h + 1) * HEAD_DIM, :], axis=0, keepdims=True
                )
            return carry

        lax.fori_loop(0, nb, fill, 0)

        def make(i, j, to_p, to_d, masks):
            key_block, value_block = keys[j], values[j]
            for h in range(heads):
                s = mm(key_block, q_cols[i, h])
                if masks:
                    s = jnp.where(tile_mask(i, j, live, blk), s, NEG)
                p = jnp.exp2(s - lse_ref[i, h : h + 1, :])
                d = p * (mm(value_block, g_cols[i, h]) - inner[i, h : h + 1, :])
                to_p[:, h * blk : (h + 1) * blk] = p.astype(BF)
                to_d[:, h * blk : (h + 1) * blk] = d.astype(BF)

        def use(i, j, from_p, from_d, first):
            grad_v[j] += mm(from_p[...], g_rows[i])
            grad_k[j] += mm(from_d[...], q_rows[i])
            for h in range(heads):
                at = slice(h * HEAD_DIM, (h + 1) * HEAD_DIM)
                product = mm(keys_t[j, at, :], from_d[:, h * blk : (h + 1) * blk])
                if first:
                    grad_q[i, at, :] = product
                else:
                    grad_q[i, at, :] += product

        make(0, 0, even_p, even_d, True)

        def masked_pair(t, carry):
            i0 = 2 * t
            i1 = i0 + 1
            i2 = jnp.minimum(i0 + 2, nb - 1)
            make(i1, jnp.minimum(i1, edge), odd_p, odd_d, True)
            use(i0, jnp.minimum(i0, edge), even_p, even_d, True)
            make(i2, jnp.minimum(i2, edge), even_p, even_d, True)
            use(i1, jnp.minimum(i1, edge), odd_p, odd_d, True)
            return carry

        lax.fori_loop(0, nb // 2, masked_pair, 0)

        make(1, 0, even_p, even_d, False)

        def pair(t, place):
            i0, j0 = place
            i1, j1 = next_open(i0, j0, edge, nb)
            make(i1, j1, odd_p, odd_d, False)
            use(i0, j0, even_p, even_d, False)
            i2, j2 = next_open(i1, j1, edge, nb)
            make(i2, j2, even_p, even_d, False)
            use(i1, j1, odd_p, odd_d, False)
            return (i2, j2)

        count = open_tiles(edge, nb)
        i_last, j_last = lax.fori_loop(0, lax.div(count, 2), pair, (jnp.int32(1), jnp.int32(0)))

        @pl.when(lax.rem(count, 2) == 1)
        def _():
            use(i_last, j_last, even_p, even_d, False)

        def drain(p, carry):
            rows_at = pl.ds(pl.multiple_of(order_ref[p] * blk, blk), blk)
            cos_part, sin_part = tables_at((cos_in, sin_in, cos_at, sin_at), p)
            result_ref[rows_at, :width] = turned(jnp.transpose(grad_q[p]) * 0.125, cos_part, sin_part, True).astype(BF)
            result_ref[rows_at, width : 2 * width] = turned(grad_k[p] * math.log(2.0), cos_part, sin_part, True).astype(BF)
            result_ref[rows_at, 2 * width :] = grad_v[p].astype(BF)
            return carry

        lax.fori_loop(0, nb, drain, 0)

    vm = pl.BlockSpec(memory_space=pltpu.VMEM)
    sm = pl.BlockSpec(memory_space=pltpu.SMEM)
    return pl.pallas_call(
        body,
        in_specs=[sm] * 3 + [vm] * 8,
        out_specs=vm,
        out_shape=jax.ShapeDtypeStruct((rows, 3 * width), BF),
        scratch_shapes=[
            pltpu.VMEM((nb, blk, width), BF),
            pltpu.VMEM((nb, width, blk), BF),
            pltpu.VMEM((nb, blk, width), BF),
            pltpu.VMEM((nb, heads, width, blk), BF),
            pltpu.VMEM((nb, heads * blk, width), BF),
            pltpu.VMEM((nb, heads, width, blk), BF),
            pltpu.VMEM((nb, heads * blk, width), BF),
            pltpu.VMEM((nb, width, blk), F32),
            pltpu.VMEM((nb, blk, width), F32),
            pltpu.VMEM((nb, blk, width), F32),
            pltpu.VMEM((nb, 8, blk), F32),
            pltpu.VMEM((blk, heads * blk), BF),
            pltpu.VMEM((blk, heads * blk), BF),
            pltpu.VMEM((blk, heads * blk), BF),
            pltpu.VMEM((blk, heads * blk), BF),
            pltpu.SMEM((nb,), jnp.int32),
        ],
        compiler_params=pltpu.CompilerParams(vmem_limit_bytes=36 << 20),
        cost_estimate=pl.CostEstimate(
            flops=heads * 9000000000, bytes_accessed=6 << 20, transcendentals=heads << 21
        ),
        name="attention_back",
    )(q[None], block_of, length, qkv, grad_out, out, lse, *tables)


def gelu_both(u):
    scale = math.sqrt(2.0 / math.pi)
    cubic = (0.044715 * scale) * (u * u)
    inside = jnp.tanh(u * (scale + cubic))
    half = 0.5 + 0.5 * inside
    value = u * half
    return value, half + value * (1.0 - inside) * (scale + 3.0 * cubic)


def bundle_up(q, w_qkv, w_attn, gain_rows, part):
    shard, dim = w_attn.shape
    pairs = part // PAIR

    def body(q_ref, qkv_ref, attn_ref, gain_ref, out_ref):
        at = q_ref[0] * part
        for p in range(pairs):
            for t in range(3):
                to = (3 * p + t) * PAIR
                out_ref[:shard, to : to + PAIR] = qkv_ref[
                    :, pl.ds(pl.multiple_of(t * dim + at + p * PAIR, PAIR), PAIR)
                ]
        out_ref[:shard, 3 * part :] = attn_ref[:, pl.ds(pl.multiple_of(at, part), part)]
        out_ref[shard:, :] = jnp.zeros((EXTRA, dim), BF)
        out_ref[shard:, : gain_ref.shape[1]] = gain_ref[...]

    return pl.pallas_call(
        body,
        in_specs=[SM, VM, VM, VM],
        out_specs=VM,
        out_shape=jax.ShapeDtypeStruct((shard + EXTRA, dim), BF),
        compiler_params=pltpu.CompilerParams(vmem_limit_bytes=8 << 20),
        name="bundle_up",
    )(q[None], in_hbm(w_qkv), in_hbm(w_attn), gain_rows)


def mlp_half(c, w_up, w_down, n):
    shard, ff = w_up.shape
    dim = w_down.shape[1]
    half = ff // n // 2
    if half % 128:
        up = lax.dynamic_index_in_dim(
            w_up.reshape(shard, n, 2, half), c, 2, keepdims=False
        ).reshape(shard, n * half)
        down = lax.dynamic_slice_in_dim(w_down, c * half, half, 0)
        return jnp.concatenate([up[:, :dim], up[:, dim:], down], axis=0)

    def body(c_ref, up_ref, down_ref, to_ref):
        for core in range(2):

            @pl.when(c_ref[0] == core)
            def _(core=core):
                for s in range(n):
                    at = (2 * s + core) * half
                    to_row, to_col = divmod(s * half, dim)
                    to_ref[to_row * shard : (to_row + 1) * shard, to_col : to_col + half] = up_ref[
                        :, at : at + half
                    ]
                to_ref[2 * shard :, :] = down_ref[core * half : (core + 1) * half, :]

    return pl.pallas_call(
        body,
        in_specs=[SM, VM, VM],
        out_specs=VM,
        out_shape=jax.ShapeDtypeStruct((2 * shard + half, dim), w_up.dtype),
        compiler_params=pltpu.CompilerParams(vmem_limit_bytes=8 << 20),
        cost_estimate=SMALL,
        name="mlp_half",
    )(c[None], w_up, w_down)


def attention_end(q, att, from_core, from_x, attn_w, hidden, gains, blk):
    rows, dim = hidden.shape
    pairs = len(att)
    part = pairs * PAIR
    steps = rows // blk

    def body(q_ref, *refs):
        own_refs = refs[:pairs]
        (
            one_ref, two_ref, three_ref, weight_ref, hidden_ref, gain_ref, att_ref, branch_ref, middle_ref, normed_ref,
        ) = refs[pairs:]
        for p in range(pairs):
            senders = (own_refs[p][...], one_ref[p], two_ref[p], three_ref[p])
            for g, block in enumerate(senders):
                at = lax.bitwise_xor(q_ref[0], g) * part + p * PAIR
                att_ref[:, pl.ds(pl.multiple_of(at, PAIR), PAIR)] = block
        branch = mm(att_ref[...], weight_ref[...])
        branch_ref[...] = branch
        middle = hidden_ref[...].astype(F32) + normalize(branch)[0] * gain_ref[1:2, :].astype(F32)
        middle_ref[...] = middle
        normed_ref[...] = (normalize(middle)[0] * gain_ref[2:3, :].astype(F32)).astype(BF)

    row = pl.BlockSpec((blk, dim), lambda i: (i, 0))
    first = pl.BlockSpec((pairs, blk, PAIR), lambda i: (0, i, 0))
    second = pl.BlockSpec((pairs, blk, PAIR), lambda i: (0, steps + i, 0))
    return pl.pallas_call(
        body,
        grid=(steps,),
        in_specs=[SM]
        + [pl.BlockSpec((blk, PAIR), lambda i: (i, 0))] * pairs
        + [
            first,
            first,
            second,
            pl.BlockSpec(attn_w.shape, lambda i: (0, 0)),
            row,
            pl.BlockSpec(gains.shape, lambda i: (0, 0)),
        ],
        out_specs=[row] * 4,
        out_shape=[
            jax.ShapeDtypeStruct((rows, dim), BF),
            jax.ShapeDtypeStruct((rows, dim), F32),
            jax.ShapeDtypeStruct((rows, dim), F32),
            jax.ShapeDtypeStruct((rows, dim), BF),
        ],
        compiler_params=pltpu.CompilerParams(vmem_limit_bytes=24 << 20),
        cost_estimate=SMALL,
        name="attention_end",
    )(q[None], *att, from_core, from_x, from_core, attn_w, hidden, gains)


def lifted_back(grad_lowered, down_w, slope):
    rows, dim = grad_lowered.shape
    wide = down_w.shape[0]
    step = 512

    def body(grad_ref, weight_ref, slope_ref, out_ref):
        out_ref[...] = (
            mm_nt(grad_ref[...], weight_ref[...]) * slope_ref[...].astype(F32)
        ).astype(BF)

    return pl.pallas_call(
        body,
        grid=(wide // step,),
        in_specs=[
            pl.BlockSpec((rows, dim), lambda i: (0, 0)),
            pl.BlockSpec((step, dim), lambda i: (i, 0)),
            pl.BlockSpec((rows, step), lambda i: (0, i)),
        ],
        out_specs=pl.BlockSpec((rows, step), lambda i: (0, i)),
        out_shape=jax.ShapeDtypeStruct((rows, wide), BF),
        compiler_params=pltpu.CompilerParams(vmem_limit_bytes=32 << 20),
        cost_estimate=SMALL,
        name="lifted_back",
    )(grad_lowered, down_w, slope)


def upstream_of(base_ref, length_ref, cotangent_ref, blk):
    pos = base_ref[pl.program_id(0)] * blk + lax.broadcasted_iota(jnp.int32, (blk, 1), 0)
    return cotangent_ref[...].astype(F32) * jnp.where(pos < length_ref[0], 1.0, 0.0)


def column_sums(value):
    return jnp.sum(value, axis=0, keepdims=True)


def top(bases, length, own, came, middle, cotangent, gains, blk):
    rows, dim = middle.shape

    def body(base_ref, length_ref, own_ref, came_ref, middle_ref, cot_ref, gain_ref, result_ref, grad_ref, sum_ref):
        gain = gain_ref[3:4, :].astype(F32)
        unit, scale = normalize(own_ref[...] + came_ref[...])
        result_ref[...] = (middle_ref[...] + unit * gain).astype(BF)
        upstream = upstream_of(base_ref, length_ref, cot_ref, blk)
        grad_ref[...] = norm_back(unit, scale, gain, upstream).astype(BF)

        @pl.when(pl.program_id(0) == 0)
        def _():
            sum_ref[...] = jnp.zeros_like(sum_ref)

        sum_ref[0:1, :] += column_sums(upstream * unit)

    row = pl.BlockSpec((blk, dim), lambda i: (i, 0))
    return pl.pallas_call(
        body,
        grid=(rows // blk,),
        in_specs=[SM, SM, row, row, row, row, pl.BlockSpec(gains.shape, lambda i: (0, 0))],
        out_specs=[row, row, pl.BlockSpec((8, dim), lambda i: (0, 0))],
        out_shape=[
            jax.ShapeDtypeStruct((rows, dim), BF),
            jax.ShapeDtypeStruct((rows, dim), BF),
            jax.ShapeDtypeStruct((8, dim), F32),
        ],
        compiler_params=pltpu.CompilerParams(vmem_limit_bytes=24 << 20),
        cost_estimate=pl.CostEstimate(flops=20 << 20, bytes_accessed=9 << 20, transcendentals=0),
        name="top",
    )(bases, length, own, came, middle, cotangent, gains)


def middle_back(q, bases, length, own, came, middle, branch, cotangent, gains, attn_w, last_sum, blk):
    rows, dim = middle.shape
    part = dim // 4
    pairs = part // PAIR
    steps = rows // blk

    def body(
        q_ref, base_ref, length_ref, own_ref, came_ref, middle_ref, branch_ref, cot_ref, gain_ref, weight_ref,
        last_ref, middle_out, branch_out, pieces_out, sums_out, attended, sums,
    ):
        i = pl.program_id(0)
        incoming = own_ref[...] + came_ref[...]
        unit, scale = normalize(middle_ref[...])
        grad_middle = upstream_of(base_ref, length_ref, cot_ref, blk) + norm_back(
            unit, scale, gain_ref[2:3, :].astype(F32), incoming
        )
        middle_out[...] = grad_middle
        sum2 = column_sums(incoming * unit)
        unit, scale = normalize(branch_ref[...])
        sum1 = column_sums(grad_middle * unit)
        grad_branch = norm_back(unit, scale, gain_ref[1:2, :].astype(F32), grad_middle).astype(BF)
        branch_out[...] = grad_branch
        attended[...] = mm_nt(grad_branch, weight_ref[...]).astype(BF)
        for g in range(4):
            at = lax.bitwise_xor(q_ref[0], g) * part
            for p in range(pairs):
                pieces_out[p, g] = attended[:, pl.ds(pl.multiple_of(at + p * PAIR, PAIR), PAIR)]

        @pl.when(i == 0)
        def _():
            sums[...] = jnp.zeros_like(sums)

        sums[0:1, :] += sum1
        sums[1:2, :] += sum2

        @pl.when(i == steps - 1)
        def _():
            sums[2:3, :] = last_ref[0:1, :]
            sums_out[...] = sums[...].astype(BF)

    row = pl.BlockSpec((blk, dim), lambda i: (i, 0))

    def whole(array):
        return pl.BlockSpec(array.shape, lambda i: (0, 0))

    return pl.pallas_call(
        body,
        grid=(steps,),
        in_specs=[SM, SM, SM, row, row, row, row, row, whole(gains), whole(attn_w), whole(last_sum)],
        out_specs=[
            row,
            row,
            pl.BlockSpec((pairs, 4, blk, PAIR), lambda i: (0, 0, i, 0)),
            pl.BlockSpec((EXTRA, dim), lambda i: (0, 0)),
        ],
        out_shape=[
            jax.ShapeDtypeStruct((rows, dim), F32),
            jax.ShapeDtypeStruct((rows, dim), BF),
            jax.ShapeDtypeStruct((pairs, 4, rows, PAIR), BF),
            jax.ShapeDtypeStruct((EXTRA, dim), BF),
        ],
        scratch_shapes=[pltpu.VMEM((blk, dim), BF), pltpu.VMEM((EXTRA, dim), F32)],
        compiler_params=pltpu.CompilerParams(vmem_limit_bytes=32 << 20),
        cost_estimate=pl.CostEstimate(
            flops=2 * rows * dim * dim, bytes_accessed=16 << 20, transcendentals=0
        ),
        name="middle_back",
    )(q[None], bases, length, own, came, middle, branch, cotangent, gains, attn_w, last_sum)


def bottom(own, from_core, from_x, hidden, grad_middle, gains, blk):
    rows, dim = hidden.shape

    def body(own_ref, core_ref, x_ref, hidden_ref, middle_ref, gain_ref, out_ref):
        incoming = own_ref[...] + core_ref[...].astype(F32) + x_ref[...].astype(F32)
        unit, scale = normalize(hidden_ref[...].astype(F32))
        out_ref[...] = middle_ref[...] + norm_back(
            unit, scale, gain_ref[0:1, :].astype(F32), incoming
        )

    row = pl.BlockSpec((blk, dim), lambda i: (i, 0))
    return pl.pallas_call(
        body,
        grid=(rows // blk,),
        in_specs=[row] * 5 + [pl.BlockSpec(gains.shape, lambda i: (0, 0))],
        out_specs=row,
        out_shape=jax.ShapeDtypeStruct((rows, dim), F32),
        compiler_params=pltpu.CompilerParams(vmem_limit_bytes=24 << 20),
        cost_estimate=pl.CostEstimate(flops=20 << 20, bytes_accessed=9 << 20, transcendentals=0),
        name="bottom",
    )(own, from_core, from_x, hidden, grad_middle, gains)


def up_end(c, mine, peer, shard, n, ff_half):
    wide = n * ff_half
    dim = wide // 2
    if ff_half % 128:
        mine, peer = [jnp.concatenate([v[:shard], v[shard:]], axis=1) for v in (mine, peer)]
        first, second = jnp.where(c == 0, mine, peer), jnp.where(c == 0, peer, mine)
        blocks = [v.reshape(shard, n, ff_half) for v in (first, second)]
        return jnp.stack(blocks, axis=2).reshape(shard, 2 * wide)

    def body(c_ref, mine_ref, peer_ref, up_ref):
        def put(first, second):
            for s in range(n):
                row, col = divmod(s * ff_half, dim)
                at = (slice(row * shard, (row + 1) * shard), slice(col, col + ff_half))
                up_ref[:, 2 * s * ff_half : (2 * s + 1) * ff_half] = first[at]
                up_ref[:, (2 * s + 1) * ff_half : (2 * s + 2) * ff_half] = second[at]

        @pl.when(c_ref[0] == 0)
        def _():
            put(mine_ref, peer_ref)

        @pl.when(c_ref[0] == 1)
        def _():
            put(peer_ref, mine_ref)

    return pl.pallas_call(
        body,
        in_specs=[SM, VM, VM],
        out_specs=VM,
        out_shape=jax.ShapeDtypeStruct((shard, 2 * wide), F32),
        compiler_params=pltpu.CompilerParams(vmem_limit_bytes=16 << 20),
        cost_estimate=SMALL,
        name="up_end",
    )(c[None], mine, peer)


def last_end(q, quarters, w_qkv, own_gains, late, part):
    shard, wide = w_qkv.shape
    pairs = part // PAIR
    dim = wide // 3

    def body(q_ref, quarters_ref, weight_ref, gain_ref, late_ref, out_ref, attn_ref, gains_ref):
        total = jnp.zeros((shard, PAIR), F32)
        for b in range(4):
            block = quarters_ref[lax.bitwise_xor(q_ref[0], b)][:shard].astype(F32)
            for p in range(pairs):
                for t in range(3):
                    at = t * dim + b * part + p * PAIR
                    value = block[:, (3 * p + t) * PAIR : (3 * p + t + 1) * PAIR]
                    out_ref[:, at : at + PAIR] = value
                    total = total + value * weight_ref[:, at : at + PAIR].astype(F32)
            attn_ref[:, b * part : (b + 1) * part] = block[:, 3 * part :]
        first = jnp.sum(total, axis=1, keepdims=True) / gain_ref[:, 0:1].astype(F32)
        lane = lax.broadcasted_iota(jnp.int32, (shard, 4), 1)
        gains_ref[...] = jnp.where(lane == 0, first, late_ref[...])

    return pl.pallas_call(
        body,
        in_specs=[SM] + [VM] * 4,
        out_specs=[VM] * 3,
        out_shape=[
            jax.ShapeDtypeStruct((shard, wide), F32),
            jax.ShapeDtypeStruct((shard, dim), F32),
            jax.ShapeDtypeStruct((shard, 4), F32),
        ],
        compiler_params=pltpu.CompilerParams(vmem_limit_bytes=16 << 20),
        cost_estimate=SMALL,
        name="last_end",
    )(q[None], quarters, w_qkv, own_gains, late)


def per_device(n, hidden_in, cotangent, lengths, block_of, w_qkv, w_attn, w_up, w_down, norm_gains):
    own_rows, dim = hidden_in.shape[1:]
    rows = 4 * own_rows
    blk = own_rows // 2
    ff = w_up.shape[1]
    shard = dim // n
    ff_half = ff // n // 2
    part = dim // 4
    pairs = part // PAIR
    q = lax.axis_index("ctx")
    c = lax.rem(q, 2)

    gain_rows = jnp.pad(norm_gains.T, ((0, EXTRA - 4), (0, 0)))
    bundle = bundle_up(q, w_qkv, w_attn, gain_rows, part)

    def store_bundle(target, owner, block):
        to_qkv, to_attn, to_gains = target
        return (
            lax.dynamic_update_slice(to_qkv, block[:shard, : 3 * part], (owner * shard, 0)),
            lax.dynamic_update_slice(to_attn, block[:shard, 3 * part :], (owner * shard, 0)),
            lax.dynamic_update_slice(to_gains, block[shard:, :shard], (0, owner * shard)),
        )

    def store_rows(target, owner, block):
        return lax.dynamic_update_slice(target, block, (owner * block.shape[0], 0))

    lead = Gather(
        bundle,
        n,
        False,
        store_bundle,
        (blank((dim, 3 * part), BF), blank((dim, part), BF), blank((EXTRA, dim), BF)),
    )
    mlp_own = mlp_half(c, w_up, w_down, n)
    bases = lax.dynamic_slice_in_dim(block_of, q, 1, 0)[0]
    tables = rotary_tables(blk, 8)
    hidden_b = hidden_in[0]

    hidden_all = lax.dynamic_update_slice(blank((rows, dim), BF), hidden_b, (0, 0))
    hidden_x = swap(hidden_b, 2)
    came, hidden_c = tie(lead.send(), swap(hidden_b, 1))
    lead.land(came)
    hidden_all = lax.dynamic_update_slice(hidden_all, hidden_c, (own_rows, 0))
    came, mlp_own = tie(lead.send(), mlp_own)
    lead.land(came)
    came, hidden_x = tie(lead.send(), hidden_x)
    lead.land(came)
    hidden_all = lax.dynamic_update_slice(hidden_all, hidden_x, (2 * own_rows, 0))
    mlp = MergedGather(
        mlp_own, n, blank((dim, n * ff_half), BF), blank((n * ff_half, dim), BF)
    )
    came, hidden_d, mlp.blocks, mlp.targets = tie(
        lead.send(), swap(hidden_x, 1), mlp.blocks, mlp.targets
    )
    hidden_all = lax.dynamic_update_slice(hidden_all, hidden_d, (3 * own_rows, 0))
    lead.land(came)
    qkv_w, attn_q, gains = lead.rest()

    normed, *qkv = project(q, block_of, hidden_all, qkv_w, gains, tables, blk)
    att, lse = attention(q, block_of, lengths, qkv, blk)
    came_mlp, attn_x, att, attn_q, mlp.targets = tie(
        mlp.send(), swap(attn_q, 2), att, attn_q, mlp.targets
    )
    mlp.land(came_mlp)

    half_rows = rows // 2
    from_x = swap(jnp.stack([a[half_rows:] for a in att]), 2)
    from_core = swap(
        jnp.stack(
            [
                jnp.concatenate([a[own_rows:half_rows], from_x[p, own_rows:]], axis=0)
                for p, a in enumerate(att)
            ]
        ),
        1,
    )
    attn_c = swap(jnp.stack([attn_q, attn_x]), 1)
    came_mlp, from_x, from_core, att, attn_x, attn_q, attn_c, mlp.targets = tie(
        mlp.send(), from_x, from_core, att, attn_x, attn_q, attn_c, mlp.targets
    )
    mlp.land(came_mlp)
    attn_parts = jnp.stack([attn_q, attn_c[0], attn_x, attn_c[1]])
    attn_w = jnp.concatenate(
        [
            lax.dynamic_index_in_dim(attn_parts, lax.bitwise_xor(q, b), 0, keepdims=False)
            for b in range(4)
        ],
        axis=1,
    )

    attended, branch, middle, normed_mid = attention_end(
        q, [a[:own_rows] for a in att], from_core, from_x, attn_w, hidden_b, gains, blk
    )
    came_mlp, normed_mid, normed_mid_c, mlp.targets = tie(
        mlp.send(), normed_mid, swap(normed_mid, 1), mlp.targets
    )
    mlp.land(came_mlp)

    came_mlp, normed_mid, normed_mid_c, mlp.targets = tie(
        mlp.send(), normed_mid, normed_mid_c, mlp.targets
    )
    mlp.land(came_mlp)
    normed_mid2 = jnp.concatenate([normed_mid, normed_mid_c], axis=0)
    up_w, down_w = mlp.rest()
    lifted = mm(normed_mid2, up_w)
    activated, slope = [v.astype(BF) for v in gelu_both(lifted)]
    lowered_c = swap(mm(activated[own_rows:], down_w), 1)
    lowered = mm(activated[:own_rows], down_w)
    result, grad_lowered, last_sum = top(
        bases, lengths, lowered, lowered_c, middle, cotangent[0], gains, blk
    )

    grad_lowered2 = jnp.concatenate([grad_lowered, swap(grad_lowered, 1)], axis=0)
    x = lax.div(q, 2)
    down_g = mm_tn(activated, grad_lowered2).astype(BF)
    grad_lifted = lifted_back(grad_lowered2, down_w, slope)
    up_g = mm_tn(normed_mid2, grad_lifted).astype(BF)
    mlp_ring = MergedScatter(up_g, down_g, n)
    mlp_ring.blocks, grad_lifted = tie(mlp_ring.blocks, grad_lifted)

    grad_normed_mid_c = swap(mm_nt(grad_lifted[own_rows:], up_w), 1)
    grad_normed_mid = mm_nt(grad_lifted[:own_rows], up_w)
    grad_middle, grad_branch, pieces, sums = middle_back(
        q, bases, lengths, grad_normed_mid, grad_normed_mid_c, middle, branch, cotangent[0], gains,
        attn_w, last_sum, blk,
    )
    came_mlp, grad_branch, pieces = tie(mlp_ring.send(), grad_branch, pieces)
    mlp_ring.land(came_mlp)

    pieces = pieces.reshape(pairs, rows, PAIR)
    went_x = swap(pieces[:, half_rows:], 2)
    went_core = swap(
        jnp.concatenate([pieces[:, own_rows:half_rows], went_x[:, own_rows:]], axis=1), 1
    )
    attn_g = mm_tn(attended, grad_branch).astype(BF)
    half_cols = dim // 2
    attn_cols = jnp.concatenate(
        [attn_g[:, b * part : (b + 1) * part] for b in (0, 2, 1, 3)], axis=1
    )
    attn_own = lax.dynamic_slice_in_dim(attn_cols, c * half_cols, half_cols, 1)
    attn_came = swap(lax.dynamic_slice_in_dim(attn_cols, (1 - c) * half_cols, half_cols, 1), 1)
    grad_out = [
        jnp.concatenate(
            [pieces[p, :own_rows], went_core[p, :own_rows], went_x[p, :own_rows], went_core[p, own_rows:]],
            axis=0,
        )
        for p in range(pairs)
    ]
    came_mlp, grad_out, attn_own, attn_came = tie(mlp_ring.send(), grad_out, attn_own, attn_came)
    mlp_ring.land(came_mlp)
    attn_half = (attn_own.astype(F32) + attn_came.astype(F32)).astype(BF)

    def back(p):
        return attention_back(
            q, block_of, lengths, qkv[p], grad_out[p], att[p], lse[p], tables, blk
        )

    attn_x_own = lax.dynamic_slice_in_dim(attn_half, x * part, part, 1)
    attn_x_other = lax.dynamic_slice_in_dim(attn_half, (1 - x) * part, part, 1)
    mixed = [back(0)]
    attn_came, came_mlp, mixed, grad_out, attn_x_own = tie(
        swap(attn_x_other, 2), mlp_ring.send(), mixed, grad_out, attn_x_own
    )
    mlp_ring.land(came_mlp)
    attn_g = (attn_x_own.astype(F32) + attn_came.astype(F32)).astype(BF)

    mixed.append(back(1))
    came_mlp, mixed, attn_g = tie(mlp_ring.send(), mixed, attn_g)
    mlp_ring.land(came_mlp)
    mlp_sum = mlp_ring.rest()
    up_sum, down_sum = mlp_sum[: 2 * shard], mlp_sum[2 * shard :]

    def normed_back(g):
        at = slice(g * own_rows, (g + 1) * own_rows)
        wide = 3 * PAIR
        return sum(mm_nt(mixed[p][at], qkv_w[:, p * wide : (p + 1) * wide]) for p in range(pairs))

    qkv_g = jnp.concatenate([mm_tn(normed, m).astype(BF) for m in mixed], axis=1)
    to_core = jnp.concatenate([normed_back(1).astype(BF), normed_back(3).astype(BF)], axis=0)
    up_x, mixed, qkv_g, to_core, attn_g, up_sum, down_sum = tie(
        swap(up_sum, 2), mixed, qkv_g, to_core, attn_g, up_sum, down_sum
    )
    up_sum = up_sum.astype(F32) + up_x.astype(F32)

    last_ring = Scatter(last_pick(qkv_g, attn_g, sums, shard), n, False)
    came_last, came_core, down_x, own_part, for_x, up_sum, down_sum = tie(
        last_ring.send(),
        swap(to_core, 1),
        swap(down_sum, 2),
        normed_back(0),
        normed_back(2),
        up_sum,
        down_sum,
    )
    last_ring.land(came_last)
    for_x = (for_x + came_core[own_rows:].astype(F32)).astype(BF)
    down_sum = down_sum.astype(F32) + down_x.astype(F32)

    quarter = own_rows // 2
    came_last, from_x0, mlp_c, up_sum, down_sum, for_x = tie(
        last_ring.send(),
        swap(for_x[:quarter], 2),
        swap(jnp.concatenate([up_sum, down_sum], axis=0), 1),
        up_sum,
        down_sum,
        for_x,
    )
    last_ring.land(came_last)
    up_out = up_end(c, up_sum, mlp_c[: 2 * shard], shard, n, ff_half)
    down_c = mlp_c[2 * shard :]
    down_out = jnp.concatenate(
        [jnp.where(c == 0, down_sum, down_c), jnp.where(c == 0, down_c, down_sum)], axis=0
    )
    came_last, from_x1, up_out, down_out = tie(
        last_ring.send(), swap(for_x[quarter:], 2), up_out, down_out
    )
    last_ring.land(came_last)
    input_grad = bottom(
        own_part, came_core[:own_rows], jnp.concatenate([from_x0, from_x1], axis=0), hidden_b, grad_middle, gains, blk
    )

    came_last, input_grad = tie(last_ring.send(), input_grad)
    last_ring.land(came_last)
    last = last_ring.rest()

    last_x, last = tie(swap(last, 2), last)
    last_pair = jnp.stack([last, last_x])
    last_c, last_pair = tie(swap(last_pair, 1), last_pair)
    last_all = jnp.stack([last_pair[0], last_c[0], last_pair[1], last_c[1]])
    me = lax.axis_index("fsdp")
    late = lax.dynamic_slice(last_all, (0, shard, me * shard), (4, 4, shard)).astype(F32)
    late = (
        lax.dynamic_index_in_dim(late, q, 0, keepdims=False)
        + lax.dynamic_index_in_dim(late, lax.bitwise_xor(q, 1), 0, keepdims=False)
    ) + (
        lax.dynamic_index_in_dim(late, lax.bitwise_xor(q, 2), 0, keepdims=False)
        + lax.dynamic_index_in_dim(late, lax.bitwise_xor(q, 3), 0, keepdims=False)
    )
    late = jnp.roll(late, 1, axis=0).T
    qkv_out, attn_out, gains_out = last_end(q, last_all, w_qkv, norm_gains, late, part)
    return (
        result[None],
        input_grad[None],
        qkv_out,
        attn_out,
        up_out,
        down_out,
        gains_out,
    )


def solution(mesh):
    n = mesh.shape["fsdp"]

    def step(*args):
        return per_device(n, *args)

    rows = P("fsdp", "ctx", None)
    weight = P("fsdp", None)
    return jax.shard_map(
        step,
        mesh=mesh,
        in_specs=(rows, rows, P("fsdp"), P()) + (weight,) * 5,
        out_specs=(rows, rows) + (weight,) * 5,
        check_vma=False,
    )
```
